32 devices in a mesh: groups: 2 (over x), blk: 16 (over z, y, core).
Axes of the slice: x: 2, y: 2, z: 4, core: 2. Of those that a mesh axis runs over, the one named last changes fastest.
Arguments:
- points: bfloat16 [8192, 128], P(('groups', 'blk')), parts along dimension 0, may hold values from -4 to 4
- lengthscale: float32 [8], P('groups'), parts along dimension 0, may hold values from 0.6 to 2.5
- noise: float32 [8], P('groups'), parts along dimension 0, may hold values from 0.1 to 1
- solution: float32 [4, 8192], P(None, ('groups', 'blk')), parts along dimension 1, may hold values from -6 to 6
- residual: float32 [4, 8192], P(None, ('groups', 'blk')), parts along dimension 1, may hold values from -16 to 16
- direction: float32 [4, 8192], P(None, ('groups', 'blk')), parts along dimension 1, may hold values from -16 to 16
Outputs:
- next_solution: float32 [4, 8192], P(None, ('groups', 'blk')), parts along dimension 1
- next_residual: float32 [4, 8192], P(None, ('groups', 'blk')), parts along dimension 1
- next_direction: float32 [4, 8192], P(None, ('groups', 'blk')), parts along dimension 1
The draws below stay inside these ranges and needn't reach their ends.
There are 2 independent parts, one for each index of `groups`. The reference program is written for one: setup_inputs(seed, part) draws one part's arguments, and reference() takes and returns one part's arrays. A program takes and returns all parts, laid end to end along the dimension named above; each array names one. Nothing has to cross between parts.
All inputs are finite; a program needn't handle non-finite values.
Results may differ from the reference program's by a relative error of at most 0.0075.
Values may be sent and summed in bfloat16 or wider, within the bound.
No kernel may reach another device: no remote copies, remote signals or barrier semaphores. Data moves between devices by JAX's collectives and lax.ppermute only.
A program may use at most 128 MiB of HBM per device.

```python
import math
import jax
import jax.numpy as jnp
from jax import lax

D = 128
CANDS = 4
NPTS = 4096


def draw_points(key, part):
    key = jax.random.fold_in(key, 11)
    key_base, key_scale, key_column, key_jitter = jax.random.split(key, 4)
    latent_dims = 8
    scales = jnp.exp(jax.random.uniform(key_scale, (NPTS, 1), jnp.float32, math.log(0.5), math.log(2.0)))
    column = jax.random.uniform(key_column, (1, D), jnp.float32, 0.8, 1.2)
    position = jnp.clip(jax.random.normal(key_base, (NPTS, latent_dims), jnp.float32), -4.0, 4.0)
    spread = jnp.tile(0.7 * position * scales, (1, D // latent_dims)) * column * math.sqrt(latent_dims / D)
    jitter = 0.15 * jnp.clip(jax.random.normal(key_jitter, (NPTS, D), jnp.float32), -4.0, 4.0)
    return jnp.clip(spread + jitter, -4.0, 4.0).astype(jnp.bfloat16)


def rising_vector(key):
    key_base = jax.random.fold_in(key, 0)
    ramp = 1.0 + 2.0 * jnp.arange(NPTS, dtype=jnp.float32) / (NPTS - 1)
    base = jnp.clip(jax.random.normal(key_base, (CANDS, NPTS), jnp.float32), -5.0, 5.0)
    return base * ramp[None, :]


def draw_residual(key, part):
    key = jax.random.fold_in(key, 23)
    return rising_vector(key)


def draw_direction(key, part):
    key = jax.random.fold_in(key, 37)
    return rising_vector(key)


def block_scale(stream_key, dims, shards, smallest, high):
    def one(dim, blocks):
        steps = jax.random.uniform(jax.random.fold_in(jax.random.fold_in(stream_key, 6), dim), (blocks,), jnp.float32, smallest / len(shards), high / len(shards))
        return jnp.repeat(jnp.exp(steps), dims[dim] // blocks).reshape((-1,) + (1,) * (len(dims) - dim - 1))

    gain = one(*shards[0])
    for cut in shards[1:]:
        gain = gain * one(*cut)
    return gain


def normal_values(own_key, extent, width, most, cuts=(), kind=jnp.bfloat16):
    gain = block_scale(own_key, extent, cuts, -0.22, 0.18) if cuts else 1.0
    drawn = jax.random.normal(own_key, extent, jnp.float32) * width * gain
    return jnp.minimum(jnp.maximum(drawn, -most), most).astype(kind)


def setup_inputs(seed: int = 0, part: int = 0) -> dict:
    arg_keys = jax.random.split(jax.random.key(seed), 7)
    part_splits = jax.random.split(jax.random.fold_in(arg_keys[6], part), 7)
    return {
        "points": draw_points(jax.random.fold_in(jax.random.fold_in(arg_keys[6], part), 71), part),
        "lengthscale": jnp.clip(jnp.exp(jax.random.uniform(part_splits[1], (CANDS,), jnp.float32, math.log(0.6), math.log(2.5))), 0.6, 2.5),
        "noise": jnp.clip(jnp.exp(jax.random.uniform(part_splits[2], (CANDS,), jnp.float32, math.log(0.1), math.log(1.0))), 0.1, 1.0),
        "solution": normal_values(part_splits[3], (CANDS, NPTS), 1.0, 6.0, ((1, 16),), jnp.float32),
        "residual": draw_residual(jax.random.fold_in(jax.random.fold_in(arg_keys[6], part), 71), part),
        "direction": draw_direction(jax.random.fold_in(jax.random.fold_in(arg_keys[6], part), 71), part),
    }


def reference(points, lengthscale, noise, solution, residual, direction):
    rows = math.gcd(NPTS, 512)
    sq = jnp.sum(jnp.square(points.astype(jnp.float32)), axis=1)
    inv = 0.5 / (lengthscale * lengthscale)
    dir_low = direction.astype(jnp.bfloat16).astype(jnp.float32)

    def block(index):
        start = (index * rows).astype(jnp.int32)
        target = lax.dynamic_slice_in_dim(points, start, rows, 0)
        target_sq = lax.dynamic_slice_in_dim(sq, start, rows, 0)
        cross = jnp.dot(target, points.T, preferred_element_type=jnp.float32)
        dist = target_sq[:, None] + sq[None, :] - 2.0 * cross
        kern = jnp.exp(-inv[:, None, None] * dist[None]).astype(jnp.bfloat16)
        return jnp.einsum('cij,cj->ci', kern.astype(jnp.float32), dir_low)

    blocks = lax.map(block, jnp.arange(NPTS // rows, dtype=jnp.int32))
    product = jnp.transpose(blocks, (1, 0, 2)).reshape(CANDS, NPTS)
    image = product + noise[:, None] * direction
    norm_now = jnp.sum(residual * residual, axis=1)
    curve = jnp.sum(direction * image, axis=1)
    alpha = norm_now / curve
    next_solution = solution + alpha[:, None] * direction
    next_residual = residual - alpha[:, None] * image
    norm_next = jnp.sum(next_residual * next_residual, axis=1)
    beta = norm_next / norm_now
    next_direction = next_residual + beta[:, None] * direction
    return next_solution, next_residual, next_direction
```

```python
import functools
import math

import jax
import jax.numpy as jnp
from jax import lax
from jax.experimental import pallas as pl
from jax.experimental.pallas import tpu as pltpu
from jax.sharding import PartitionSpec as P

LOG2E = 1.4426950408889634


def split_sizes(devices):
    lo = max(d for d in range(1, math.isqrt(devices) + 1) if devices % d == 0)
    return devices // lo, lo


def squares(block):
    wide = block.astype(jnp.float32)
    return jnp.sum(wide * wide, axis=1, keepdims=True)


def widen(block, scale, first):
    sq = squares(block)
    high = sq.astype(jnp.bfloat16).astype(jnp.float32)
    middle = (sq - high).astype(jnp.bfloat16).astype(jnp.float32)
    low = sq - high - middle
    lane = lax.broadcasted_iota(jnp.int32, block.shape, 1)
    base = 0 if first else 3
    one = 3 - base
    extra = jnp.where(lane == base, high, 0.0)
    extra = jnp.where(lane == base + 1, middle, extra)
    extra = jnp.where(lane == base + 2, low, extra)
    extra = jnp.where((lane >= one) & (lane < one + 3), 1.0, extra)
    scaled = block.astype(jnp.float32) * scale
    return jnp.concatenate(
        [scaled.astype(jnp.bfloat16), extra.astype(jnp.bfloat16)], axis=1
    )


def product_kernel(lo, hi, *refs):
    rows, refs = refs[:lo], refs[lo:]
    cols, refs = refs[:hi], refs[hi:]
    dirs, refs = refs[:hi], refs[hi:]
    length, out, row_wide = refs
    size = rows[0].shape[0]
    cands = length.shape[0]
    for k in range(lo):
        row_wide[pl.ds(k * size, size), :] = widen(rows[k][...], 1.0, True)
    rates = [
        (-0.5 * LOG2E) / (length[c] * length[c]) for c in range(cands)
    ]
    total = [None] * lo
    for h in range(hi):
        col_wide = widen(cols[h][...], -2.0, False)
        low = dirs[h][...].astype(jnp.bfloat16)
        which = lax.broadcasted_iota(jnp.int32, low.shape, 0)
        only = [jnp.where(which == c, low, jnp.zeros_like(low)) for c in range(cands)]
        for k in range(lo):
            dist = lax.dot_general(
                col_wide,
                row_wide[pl.ds(k * size, size), :],
                (((1,), (1,)), ((), ())),
                preferred_element_type=jnp.float32,
            )
            for c in range(cands):
                kern = jnp.exp2(dist * rates[c]).astype(jnp.bfloat16)
                part = jnp.dot(only[c], kern, preferred_element_type=jnp.float32)
                total[k] = part if total[k] is None else total[k] + part
    for k in range(lo):
        out[:, pl.ds(k * size, size)] = total[k]


def sums_kernel(lo, *refs):
    parts, refs = refs[:lo], refs[lo:]
    dirs, refs = refs[:lo], refs[lo:]
    ress, refs = refs[:lo], refs[lo:]
    noise, image_out, sums_out = refs
    cands, size = dirs[0].shape
    row = lax.broadcasted_iota(jnp.int32, (cands, 1), 0)
    sigma = jnp.zeros((cands, 1), jnp.float32)
    for c in range(cands):
        sigma = jnp.where(row == c, noise[c], sigma)
    sums = [jnp.zeros((cands, 1), jnp.float32)] * 4
    for k in range(lo):
        image = sigma * dirs[k][...]
        for m in range(lo):
            image += parts[m][:, pl.ds(((k - m) % lo) * size, size)]
        if k == 0:
            image_out[...] = image
        direction, residual = dirs[k][...], ress[k][...]
        terms = (
            residual * residual,
            direction * image,
            residual * image,
            image * image,
        )
        sums = [
            s + jnp.sum(t, axis=1, keepdims=True) for s, t in zip(sums, terms)
        ]
    lane = lax.broadcasted_iota(jnp.int32, (cands, 128), 1)
    packed = jnp.zeros((cands, 128), jnp.float32)
    for t in range(4):
        packed = jnp.where(lane == t, sums[t], packed)
    sums_out[...] = packed


def update_kernel(hi, *refs):
    sums, refs = refs[:hi], refs[hi:]
    image, solution, residual, direction, out_s, out_r, out_d = refs
    total = sums[0][...]
    for h in range(1, hi):
        total = total + sums[h][...]
    norm, curve, cross, square = (total[:, t : t + 1] for t in range(4))
    alpha = norm / curve
    norm_next = norm - 2.0 * alpha * cross + alpha * (alpha * square)
    beta = norm_next / norm
    step = direction[...]
    fresh = residual[...] - alpha * image[...]
    out_s[...] = solution[...] + alpha * step
    out_r[...] = fresh
    out_d[...] = fresh + beta * step


def per_device(devices, points, lengthscale, noise, solution, residual, direction):
    hi, lo = split_sizes(devices)
    size = points.shape[0]
    cands = direction.shape[0]

    def near(x):
        return [x] + [
            lax.ppermute(
                x,
                "blk",
                [
                    (h * lo + (l + k) % lo, h * lo + l)
                    for h in range(hi)
                    for l in range(lo)
                ],
            )
            for k in range(1, lo)
        ]

    def far(x):
        return [x] + [
            lax.ppermute(
                x,
                "blk",
                [
                    (((h + k) % hi) * lo + l, h * lo + l)
                    for h in range(hi)
                    for l in range(lo)
                ],
            )
            for k in range(1, hi)
        ]

    vmem = pl.BlockSpec(memory_space=pltpu.VMEM)
    smem = pl.BlockSpec(memory_space=pltpu.SMEM)
    params = pltpu.CompilerParams(vmem_limit_bytes=48 * 1024 * 1024)

    cols = far(points)
    col_dirs = far(direction)
    rows = near(points)
    row_dirs = near(direction)
    row_ress = near(residual)

    partial = pl.pallas_call(
        functools.partial(product_kernel, lo, hi),
        out_shape=jax.ShapeDtypeStruct((cands, lo * size), jnp.float32),
        in_specs=[vmem] * (lo + 2 * hi) + [smem],
        out_specs=vmem,
        scratch_shapes=[pltpu.VMEM((lo * size, 2 * points.shape[1]), jnp.bfloat16)],
        compiler_params=params,
        name="product",
    )(*rows, *cols, *col_dirs, lengthscale)

    image, sums = pl.pallas_call(
        functools.partial(sums_kernel, lo),
        out_shape=(
            jax.ShapeDtypeStruct((cands, size), jnp.float32),
            jax.ShapeDtypeStruct((cands, 128), jnp.float32),
        ),
        in_specs=[vmem] * (3 * lo) + [smem],
        out_specs=(vmem, vmem),
        compiler_params=params,
        name="sums",
    )(*near(partial), *row_dirs, *row_ress, noise)

    return pl.pallas_call(
        functools.partial(update_kernel, hi),
        out_shape=(jax.ShapeDtypeStruct((cands, size), jnp.float32),) * 3,
        in_specs=[vmem] * (hi + 4),
        out_specs=(vmem,) * 3,
        compiler_params=params,
        name="update",
    )(*far(sums), image, solution, residual, direction)


def solution(mesh):
    split = P(None, ("groups", "blk"))
    return jax.shard_map(
        functools.partial(per_device, mesh.shape["blk"]),
        mesh=mesh,
        in_specs=(P(("groups", "blk"), None), P("groups"), P("groups"), split, split, split),
        out_specs=(split, split, split),
        check_vma=False,
    )
```

```python
import functools
import math

import jax
import jax.numpy as jnp
from jax import lax
from jax.experimental import pallas as pl
from jax.experimental.pallas import tpu as pltpu
from jax.sharding import PartitionSpec as P

LOG2E = 1.4426950408889634


def split_sizes(devices):
    lo = max(d for d in range(1, math.isqrt(devices) + 1) if devices % d == 0)
    return devices // lo, lo


def squares(block):
    wide = block.astype(jnp.float32)
    return jnp.sum(wide * wide, axis=1, keepdims=True)


def widen(block, scale, first):
    sq = squares(block)
    high = sq.astype(jnp.bfloat16).astype(jnp.float32)
    middle = (sq - high).astype(jnp.bfloat16).astype(jnp.float32)
    low = sq - high - middle
    lane = lax.broadcasted_iota(jnp.int32, block.shape, 1)
    base = 0 if first else 3
    one = 3 - base
    extra = jnp.where(lane == base, high, 0.0)
    extra = jnp.where(lane == base + 1, middle, extra)
    extra = jnp.where(lane == base + 2, low, extra)
    extra = jnp.where((lane >= one) & (lane < one + 3), 1.0, extra)
    scaled = block.astype(jnp.float32) * scale
    return jnp.concatenate(
        [scaled.astype(jnp.bfloat16), extra.astype(jnp.bfloat16)], axis=1
    )


def pack_kernel(points, direction, to_cols, to_rows):
    size, dims = points.shape
    extra = to_cols.shape[1] - size
    pieces = [direction[:, pl.ds(p * dims, dims)] for p in range(size // dims)]
    spare = extra - sum(p.shape[0] for p in pieces)
    if spare:
        pieces.append(jnp.zeros((spare, dims), jnp.float32))
    tail = jnp.concatenate(pieces, axis=0).astype(jnp.bfloat16)
    for h in range(to_cols.shape[0]):
        to_cols[h, :size, :] = points[...]
        to_cols[h, size:, :] = tail
    for l in range(to_rows.shape[0]):
        to_rows[l] = points[...]


def product_kernel(rows, cols, length, out, row_wide):
    lo, size, dims = rows.shape
    hi = cols.shape[0]
    cands = length.shape[0]
    for k in range(lo):
        row_wide[pl.ds(k * size, size), :] = widen(rows[k], 1.0, True)
    rates = [
        (-0.5 * LOG2E) / (length[c] * length[c]) for c in range(cands)
    ]
    total = [None] * lo
    for h in range(hi):
        col_wide = widen(cols[h, :size, :], -2.0, False)
        tail = cols[h, size:, :].astype(jnp.float32)
        low = jnp.concatenate(
            [tail[p * cands : (p + 1) * cands] for p in range(size // dims)], axis=1
        )
        which = lax.broadcasted_iota(jnp.int32, low.shape, 0)
        only = [
            jnp.where(which == c, low, 0.0).astype(jnp.bfloat16) for c in range(cands)
        ]
        for k in range(lo):
            dist = lax.dot_general(
                col_wide,
                row_wide[pl.ds(k * size, size), :],
                (((1,), (1,)), ((), ())),
                preferred_element_type=jnp.float32,
            )
            for c in range(cands):
                kern = jnp.exp2(dist * rates[c]).astype(jnp.bfloat16)
                part = jnp.dot(only[c], kern, preferred_element_type=jnp.float32)
                total[k] = part if total[k] is None else total[k] + part
    for k in range(lo):
        out[k] = total[k]


def sums_kernel(parts, direction, residual, noise, image_out, sums_out):
    cands, size = direction.shape
    row = lax.broadcasted_iota(jnp.int32, (cands, 1), 0)
    sigma = jnp.zeros((cands, 1), jnp.float32)
    for c in range(cands):
        sigma = jnp.where(row == c, noise[c], sigma)
    step, rest = direction[...], residual[...]
    image = sigma * step
    for m in range(parts.shape[0]):
        image += parts[m]
    image_out[...] = image
    terms = (rest * rest, step * image, rest * image, image * image)
    lane = lax.broadcasted_iota(jnp.int32, (cands, 128), 1)
    packed = jnp.zeros((cands, 128), jnp.float32)
    for t in range(4):
        packed = jnp.where(lane == t, jnp.sum(terms[t], axis=1, keepdims=True), packed)
    for n in range(sums_out.shape[0]):
        sums_out[n] = packed


def update_kernel(sums, image, solution, residual, direction, out_s, out_r, out_d):
    total = sums[0]
    for n in range(1, sums.shape[0]):
        total = total + sums[n]
    norm, curve, cross, square = (total[:, t : t + 1] for t in range(4))
    alpha = norm / curve
    norm_next = norm - 2.0 * alpha * cross + alpha * (alpha * square)
    beta = norm_next / norm
    step = direction[...]
    fresh = residual[...] - alpha * image[...]
    out_s[...] = solution[...] + alpha * step
    out_r[...] = fresh
    out_d[...] = fresh + beta * step


def per_device(devices, points, lengthscale, noise, solution, residual, direction):
    hi, lo = split_sizes(devices)
    size, dims = points.shape
    cands = direction.shape[0]
    row_groups = [[h * lo + l for l in range(lo)] for h in range(hi)]
    col_groups = [[h * lo + l for h in range(hi)] for l in range(lo)]

    def exchange(x, groups):
        return lax.all_to_all(
            x, "blk", split_axis=0, concat_axis=0, axis_index_groups=groups
        )

    vmem = pl.BlockSpec(memory_space=pltpu.VMEM)
    smem = pl.BlockSpec(memory_space=pltpu.SMEM)
    params = pltpu.CompilerParams(vmem_limit_bytes=48 * 1024 * 1024)

    extra = -(-cands * (size // dims) // 16) * 16
    to_cols, to_rows = pl.pallas_call(
        pack_kernel,
        out_shape=(
            jax.ShapeDtypeStruct((hi, size + extra, dims), jnp.bfloat16),
            jax.ShapeDtypeStruct((lo, size, dims), jnp.bfloat16),
        ),
        in_specs=[vmem, vmem],
        out_specs=(vmem, vmem),
        compiler_params=params,
        name="pack",
    )(points, direction)
    cols = exchange(to_cols, col_groups)
    rows = exchange(to_rows, row_groups)

    partial = pl.pallas_call(
        product_kernel,
        out_shape=jax.ShapeDtypeStruct((lo, cands, size), jnp.float32),
        in_specs=[vmem, vmem, smem],
        out_specs=vmem,
        scratch_shapes=[pltpu.VMEM((lo * size, 2 * dims), jnp.bfloat16)],
        compiler_params=params,
        name="product",
    )(rows, cols, lengthscale)

    image, sums = pl.pallas_call(
        sums_kernel,
        out_shape=(
            jax.ShapeDtypeStruct((cands, size), jnp.float32),
            jax.ShapeDtypeStruct((devices, cands, 128), jnp.float32),
        ),
        in_specs=[vmem, vmem, vmem, smem],
        out_specs=(vmem, vmem),
        compiler_params=params,
        name="sums",
    )(exchange(partial, row_groups), direction, residual, noise)

    return pl.pallas_call(
        update_kernel,
        out_shape=(jax.ShapeDtypeStruct((cands, size), jnp.float32),) * 3,
        in_specs=[vmem] * 5,
        out_specs=(vmem,) * 3,
        compiler_params=params,
        name="update",
    )(exchange(sums, None), image, solution, residual, direction)


def solution(mesh):
    split = P(None, ("groups", "blk"))
    return jax.shard_map(
        functools.partial(per_device, mesh.shape["blk"]),
        mesh=mesh,
        in_specs=(P(("groups", "blk"), None), P("groups"), P("groups"), split, split, split),
        out_specs=(split, split, split),
        check_vma=False,
    )
```

```python
import functools
import math

import jax
import jax.numpy as jnp
from jax import lax
from jax.experimental import pallas as pl
from jax.experimental.pallas import tpu as pltpu
from jax.sharding import PartitionSpec as P

LOG2E = 1.4426950408889634


def split_sizes(devices):
    lo = max(d for d in range(1, math.isqrt(devices) + 1) if devices % d == 0)
    return devices // lo, lo


def peer(index, step, count):
    return index ^ step if count & (count - 1) == 0 else (step - index) % count


def pieces_of(wide):
    high = wide.astype(jnp.bfloat16).astype(jnp.float32)
    middle = (wide - high).astype(jnp.bfloat16).astype(jnp.float32)
    return high, middle, wide - high - middle


def fold(wide, dims):
    return jnp.concatenate(
        [wide[:, p : p + dims] for p in range(0, wide.shape[1], dims)], axis=0
    )


def unfold(tall, cands):
    return jnp.concatenate(
        [tall[p : p + cands] for p in range(0, tall.shape[0], cands)], axis=1
    )


def squares(block):
    wide = block.astype(jnp.float32)
    return jnp.sum(wide * wide, axis=1, keepdims=True)


def widen(block, scale, first):
    sq = squares(block)
    high, middle, low = pieces_of(sq)
    lane = lax.broadcasted_iota(jnp.int32, block.shape, 1)
    base = 0 if first else 3
    one = 3 - base
    extra = jnp.where(lane == base, high, 0.0)
    extra = jnp.where(lane == base + 1, middle, extra)
    extra = jnp.where(lane == base + 2, low, extra)
    extra = jnp.where((lane >= one) & (lane < one + 3), 1.0, extra)
    scaled = block.astype(jnp.float32) * scale
    return jnp.concatenate(
        [scaled.astype(jnp.bfloat16), extra.astype(jnp.bfloat16)], axis=1
    )


def pack_kernel(points, direction, residual, to_col, to_row):
    size, dims = points.shape
    step = fold(direction[...], dims)
    rest = fold(residual[...], dims)
    zero = jnp.zeros_like(step)
    to_col[:size, :] = points[...]
    to_row[:size, :] = points[...]
    to_col[size:, :] = jnp.concatenate([step, zero], axis=0).astype(jnp.bfloat16)
    to_row[size:, :] = jnp.concatenate(
        [*pieces_of(step), *pieces_of(rest)], axis=0
    ).astype(jnp.bfloat16)


def product_kernel(lo, hi, *refs):
    rows, refs = refs[:lo], refs[lo:]
    cols, refs = refs[:hi], refs[hi:]
    length, out, row_wide = refs
    cands = length.shape[0]
    size = out.shape[1] // lo
    dims = rows[0].shape[1]
    tall = cands * size // dims
    for k in range(lo):
        row_wide[pl.ds(k * size, size), :] = widen(rows[k][:size, :], 1.0, True)
    rates = [
        (-0.5 * LOG2E) / (length[c] * length[c]) for c in range(cands)
    ]
    total = [None] * lo
    for h in range(hi):
        col_wide = widen(cols[h][:size, :], -2.0, False)
        tail = cols[h][size:, :].astype(jnp.float32)
        low = unfold(tail[:tall], cands)
        which = lax.broadcasted_iota(jnp.int32, low.shape, 0)
        only = [
            jnp.where(which == c, low, 0.0).astype(jnp.bfloat16) for c in range(cands)
        ]
        for k in range(lo):
            dist = lax.dot_general(
                col_wide,
                row_wide[pl.ds(k * size, size), :],
                (((1,), (1,)), ((), ())),
                preferred_element_type=jnp.float32,
            )
            for c in range(cands):
                kern = jnp.exp2(dist * rates[c]).astype(jnp.bfloat16)
                part = jnp.dot(only[c], kern, preferred_element_type=jnp.float32)
                total[k] = part if total[k] is None else total[k] + part
    for k in range(lo):
        out[:, pl.ds(k * size, size)] = total[k]


def sums_kernel(lo, *refs):
    parts, refs = refs[:lo], refs[lo:]
    rows, refs = refs[:lo], refs[lo:]
    noise, image_out, sums_out = refs
    cands, size = image_out.shape
    dims = rows[0].shape[1]
    tall = cands * size // dims
    row = lax.broadcasted_iota(jnp.int32, (cands, 1), 0)
    sigma = jnp.zeros((cands, 1), jnp.float32)
    for c in range(cands):
        sigma = jnp.where(row == c, noise[c], sigma)
    sums = [jnp.zeros((cands, 1), jnp.float32)] * 4
    for k in range(lo):
        tail = rows[k][size:, :].astype(jnp.float32)
        step, rest = (
            unfold(sum(tail[p * tall : (p + 1) * tall] for p in three), cands)
            for three in ((0, 1, 2), (3, 4, 5))
        )
        image = sigma * step
        for m in range(lo):
            image += parts[m][:, pl.ds(peer(m, k, lo) * size, size)]
        if k == 0:
            image_out[...] = image
        terms = (rest * rest, step * image, rest * image, image * image)
        sums = [
            s + jnp.sum(t, axis=1, keepdims=True) for s, t in zip(sums, terms)
        ]
    lane = lax.broadcasted_iota(jnp.int32, (cands, 128), 1)
    packed = jnp.zeros((cands, 128), jnp.float32)
    for t in range(4):
        packed = jnp.where(lane == t, sums[t], packed)
    sums_out[...] = packed


def update_kernel(sums, image, solution, residual, direction, out_s, out_r, out_d):
    total = sums[0]
    for n in range(1, sums.shape[0]):
        total = total + sums[n]
    norm, curve, cross, square = (total[:, t : t + 1] for t in range(4))
    alpha = norm / curve
    norm_next = norm - 2.0 * alpha * cross + alpha * (alpha * square)
    beta = norm_next / norm
    step = direction[...]
    fresh = residual[...] - alpha * image[...]
    out_s[...] = solution[...] + alpha * step
    out_r[...] = fresh
    out_d[...] = fresh + beta * step


def per_device(devices, points, lengthscale, noise, solution, residual, direction):
    hi, lo = split_sizes(devices)
    size, dims = points.shape
    cands = direction.shape[0]
    tall = cands * size // dims

    def row_peers(x):
        return [x] + [
            lax.ppermute(
                x,
                "blk",
                [
                    (h * lo + l, h * lo + peer(l, k, lo))
                    for h in range(hi)
                    for l in range(lo)
                ],
            )
            for k in range(1, lo)
        ]

    def col_peers(x):
        return [x] + [
            lax.ppermute(
                x,
                "blk",
                [
                    (h * lo + l, peer(h, k, hi) * lo + l)
                    for h in range(hi)
                    for l in range(lo)
                ],
            )
            for k in range(1, hi)
        ]

    vmem = pl.BlockSpec(memory_space=pltpu.VMEM)
    smem = pl.BlockSpec(memory_space=pltpu.SMEM)
    params = pltpu.CompilerParams(vmem_limit_bytes=48 * 1024 * 1024)

    to_col, to_row = pl.pallas_call(
        pack_kernel,
        out_shape=(
            jax.ShapeDtypeStruct((size + 2 * tall, dims), jnp.bfloat16),
            jax.ShapeDtypeStruct((size + 6 * tall, dims), jnp.bfloat16),
        ),
        in_specs=[vmem] * 3,
        out_specs=(vmem, vmem),
        compiler_params=params,
        name="pack",
    )(points, direction, residual)
    cols = col_peers(to_col)
    rows = row_peers(to_row)

    partial = pl.pallas_call(
        functools.partial(product_kernel, lo, hi),
        out_shape=jax.ShapeDtypeStruct((cands, lo * size), jnp.float32),
        in_specs=[vmem] * (lo + hi) + [smem],
        out_specs=vmem,
        scratch_shapes=[pltpu.VMEM((lo * size, 2 * dims), jnp.bfloat16)],
        compiler_params=params,
        name="product",
    )(*rows, *cols, lengthscale)

    image, sums = pl.pallas_call(
        functools.partial(sums_kernel, lo),
        out_shape=(
            jax.ShapeDtypeStruct((cands, size), jnp.float32),
            jax.ShapeDtypeStruct((cands, 128), jnp.float32),
        ),
        in_specs=[vmem] * (2 * lo) + [smem],
        out_specs=(vmem, vmem),
        compiler_params=params,
        name="sums",
    )(*row_peers(partial), *rows, noise)

    all_sums = lax.all_gather(
        sums,
        "blk",
        axis_index_groups=[[h * lo + l for h in range(hi)] for l in range(lo)],
    )
    return pl.pallas_call(
        update_kernel,
        out_shape=(jax.ShapeDtypeStruct((cands, size), jnp.float32),) * 3,
        in_specs=[vmem] * 5,
        out_specs=(vmem,) * 3,
        compiler_params=params,
        name="update",
    )(all_sums, image, solution, residual, direction)


def solution(mesh):
    split = P(None, ("groups", "blk"))
    return jax.shard_map(
        functools.partial(per_device, mesh.shape["blk"]),
        mesh=mesh,
        in_specs=(P(("groups", "blk"), None), P("groups"), P("groups"), split, split, split),
        out_specs=(split, split, split),
        check_vma=False,
    )
```

```python
import functools
import math

import jax
import jax.numpy as jnp
from jax import lax
from jax.experimental import pallas as pl
from jax.experimental.pallas import tpu as pltpu
from jax.sharding import PartitionSpec as P

LOG2E = 1.4426950408889634


def split_sizes(devices):
    lo = max(d for d in range(1, math.isqrt(devices) + 1) if devices % d == 0)
    return devices // lo, lo


def peer(index, step, count):
    return index ^ step if count & (count - 1) == 0 else (step - index) % count


def pieces_of(wide):
    high = wide.astype(jnp.bfloat16).astype(jnp.float32)
    middle = (wide - high).astype(jnp.bfloat16).astype(jnp.float32)
    return high, middle, wide - high - middle


def fold(wide, dims):
    return jnp.concatenate(
        [wide[:, p : p + dims] for p in range(0, wide.shape[1], dims)], axis=0
    )


def unfold(tall, cands):
    return jnp.concatenate(
        [tall[p : p + cands] for p in range(0, tall.shape[0], cands)], axis=1
    )


def squares(block):
    wide = block.astype(jnp.float32)
    return jnp.sum(wide * wide, axis=1, keepdims=True)


def widen(block, scale, first):
    sq = squares(block)
    high, middle, low = pieces_of(sq)
    lane = lax.broadcasted_iota(jnp.int32, block.shape, 1)
    base = 0 if first else 3
    one = 3 - base
    extra = jnp.where(lane == base, high, 0.0)
    extra = jnp.where(lane == base + 1, middle, extra)
    extra = jnp.where(lane == base + 2, low, extra)
    extra = jnp.where((lane >= one) & (lane < one + 3), 1.0, extra)
    scaled = block.astype(jnp.float32) * scale
    return jnp.concatenate(
        [scaled.astype(jnp.bfloat16), extra.astype(jnp.bfloat16)], axis=1
    )


def pack_kernel(points, direction, residual, to_col, to_row, step_in, rest_in, sems):
    size, dims = points.shape
    copies = [
        pltpu.make_async_copy(source, target, sems.at[i])
        for i, (source, target) in enumerate(
            (
                (direction, step_in),
                (residual, rest_in),
                (points, to_col.at[pl.ds(0, size), :]),
                (points, to_row.at[pl.ds(0, size), :]),
            )
        )
    ]
    for copy in copies:
        copy.start()
    for copy in copies[:2]:
        copy.wait()
    step = fold(step_in[...], dims)
    rest = fold(rest_in[...], dims)
    zero = jnp.zeros_like(step)
    to_col[size:, :] = jnp.concatenate([step, zero], axis=0).astype(jnp.bfloat16)
    to_row[size:, :] = jnp.concatenate(
        [*pieces_of(step), *pieces_of(rest)], axis=0
    ).astype(jnp.bfloat16)
    for copy in copies[2:]:
        copy.wait()


def product_kernel(lo, hi, *refs):
    rows, refs = refs[:lo], refs[lo:]
    cols, refs = refs[:hi], refs[hi:]
    length, out, row_wide = refs
    cands = length.shape[0]
    dims = rows[0].shape[1]
    tall = out.shape[0] // lo
    size = tall * dims // cands
    for k in range(lo):
        row_wide[pl.ds(k * size, size), :] = widen(rows[k][:size, :], 1.0, True)
    rates = [
        (-0.5 * LOG2E) / (length[c] * length[c]) for c in range(cands)
    ]
    total = [None] * lo
    for h in range(hi):
        col_wide = widen(cols[h][:size, :], -2.0, False)
        tail = cols[h][size:, :].astype(jnp.float32)
        low = unfold(tail[:tall], cands)
        which = lax.broadcasted_iota(jnp.int32, low.shape, 0)
        only = [
            jnp.where(which == c, low, 0.0).astype(jnp.bfloat16) for c in range(cands)
        ]
        for k in range(lo):
            dist = lax.dot_general(
                col_wide,
                row_wide[pl.ds(k * size, size), :],
                (((1,), (1,)), ((), ())),
                preferred_element_type=jnp.float32,
            )
            for c in range(cands):
                kern = jnp.exp2(dist * rates[c]).astype(jnp.bfloat16)
                part = jnp.dot(only[c], kern, preferred_element_type=jnp.float32)
                total[k] = part if total[k] is None else total[k] + part
    for k in range(lo):
        out[pl.ds(k * tall, tall), :] = fold(total[k], dims)


def sums_kernel(lo, *refs):
    parts, refs = refs[:lo], refs[lo:]
    rows, refs = refs[:lo], refs[lo:]
    noise, image_out, sums_out = refs
    cands = noise.shape[0]
    tall, dims = image_out.shape
    size = rows[0].shape[0] - 6 * tall
    which = lax.broadcasted_iota(jnp.int32, (tall, 1), 0) % cands
    sigma = jnp.zeros((tall, 1), jnp.float32)
    for c in range(cands):
        sigma = jnp.where(which == c, noise[c], sigma)
    sums = [jnp.zeros((tall, dims), jnp.float32)] * 4
    for k in range(lo):
        tail = rows[k][size:, :].astype(jnp.float32)
        tail = [tail[p * tall : (p + 1) * tall] for p in range(6)]
        step = tail[0] + tail[1] + tail[2]
        rest = tail[3] + tail[4] + tail[5]
        image = sigma * step
        for m in range(lo):
            image += parts[m][pl.ds(peer(m, k, lo) * tall, tall), :]
        if k == 0:
            image_out[...] = image
        terms = (rest * rest, step * image, rest * image, image * image)
        sums = [s + t for s, t in zip(sums, terms)]
    for i, s in enumerate(sums):
        sums_out[pl.ds(i * cands, cands), :] = sum(
            s[p : p + cands] for p in range(0, tall, cands)
        )


def update_kernel(hi, *refs):
    sums, refs = refs[:hi], refs[hi:]
    image, solution, residual, direction, out_s, out_r, out_d = refs
    cands = solution.shape[0]
    total = sums[0][...]
    for h in range(1, hi):
        total = total + sums[h][...]
    total = jnp.sum(total, axis=1, keepdims=True)
    norm, curve, cross, square = (
        total[i * cands : (i + 1) * cands] for i in range(4)
    )
    alpha = norm / curve
    norm_next = norm - 2.0 * alpha * cross + alpha * (alpha * square)
    beta = norm_next / norm
    step = direction[...]
    fresh = residual[...] - alpha * unfold(image[...], cands)
    out_s[...] = solution[...] + alpha * step
    out_r[...] = fresh
    out_d[...] = fresh + beta * step


def per_device(devices, points, lengthscale, noise, solution, residual, direction):
    hi, lo = split_sizes(devices)
    size, dims = points.shape
    cands = direction.shape[0]
    tall = cands * size // dims

    def row_peers(x):
        return [x] + [
            lax.ppermute(
                x,
                "blk",
                [
                    (h * lo + l, h * lo + peer(l, k, lo))
                    for h in range(hi)
                    for l in range(lo)
                ],
            )
            for k in range(1, lo)
        ]

    def col_peers(x):
        return [x] + [
            lax.ppermute(
                x,
                "blk",
                [
                    (h * lo + l, peer(h, k, hi) * lo + l)
                    for h in range(hi)
                    for l in range(lo)
                ],
            )
            for k in range(1, hi)
        ]

    vmem = pl.BlockSpec(memory_space=pltpu.VMEM)
    smem = pl.BlockSpec(memory_space=pltpu.SMEM)
    params = pltpu.CompilerParams(vmem_limit_bytes=48 * 1024 * 1024)

    to_col, to_row = pl.pallas_call(
        pack_kernel,
        out_shape=(
            jax.ShapeDtypeStruct((size + 2 * tall, dims), jnp.bfloat16),
            jax.ShapeDtypeStruct((size + 6 * tall, dims), jnp.bfloat16),
        ),
        in_specs=[pl.BlockSpec(memory_space=pl.ANY)] * 3,
        out_specs=(vmem, vmem),
        scratch_shapes=[
            pltpu.VMEM((cands, size), jnp.float32),
            pltpu.VMEM((cands, size), jnp.float32),
            pltpu.SemaphoreType.DMA((4,)),
        ],
        compiler_params=params,
        name="pack",
    )(points, direction, residual)
    cols = col_peers(to_col)
    rows = row_peers(to_row)

    partial = pl.pallas_call(
        functools.partial(product_kernel, lo, hi),
        out_shape=jax.ShapeDtypeStruct((lo * tall, dims), jnp.float32),
        in_specs=[vmem] * (lo + hi) + [smem],
        out_specs=vmem,
        scratch_shapes=[pltpu.VMEM((lo * size, 2 * dims), jnp.bfloat16)],
        compiler_params=params,
        name="product",
    )(*rows, *cols, lengthscale)

    image, sums = pl.pallas_call(
        functools.partial(sums_kernel, lo),
        out_shape=(
            jax.ShapeDtypeStruct((tall, dims), jnp.float32),
            jax.ShapeDtypeStruct((4 * cands, dims), jnp.float32),
        ),
        in_specs=[vmem] * (2 * lo) + [smem],
        out_specs=(vmem, vmem),
        compiler_params=params,
        name="sums",
    )(*row_peers(partial), *rows, noise)

    return pl.pallas_call(
        functools.partial(update_kernel, hi),
        out_shape=(jax.ShapeDtypeStruct((cands, size), jnp.float32),) * 3,
        in_specs=[vmem] * (hi + 4),
        out_specs=(vmem,) * 3,
        compiler_params=params,
        name="update",
    )(*col_peers(sums), image, solution, residual, direction)


def solution(mesh):
    split = P(None, ("groups", "blk"))
    return jax.shard_map(
        functools.partial(per_device, mesh.shape["blk"]),
        mesh=mesh,
        in_specs=(P(("groups", "blk"), None), P("groups"), P("groups"), split, split, split),
        out_specs=(split, split, split),
        check_vma=False,
    )
```

```python
import functools
import math

import jax
import jax.numpy as jnp
from jax import lax
from jax.experimental import pallas as pl
from jax.experimental.pallas import tpu as pltpu
from jax.sharding import PartitionSpec as P

LOG2E = 1.4426950408889634


def split_sizes(devices):
    lo = max(d for d in range(1, math.isqrt(devices) + 1) if devices % d == 0)
    return devices // lo, lo


def pieces_of(wide):
    high = wide.astype(jnp.bfloat16).astype(jnp.float32)
    middle = (wide - high).astype(jnp.bfloat16).astype(jnp.float32)
    return high, middle, wide - high - middle


def fold(wide, dims):
    return jnp.concatenate(
        [wide[:, p : p + dims] for p in range(0, wide.shape[1], dims)], axis=0
    )


def unfold(tall, cands):
    return jnp.concatenate(
        [tall[p : p + cands] for p in range(0, tall.shape[0], cands)], axis=1
    )


def squares(block):
    wide = block.astype(jnp.float32)
    return jnp.sum(wide * wide, axis=1, keepdims=True)


def widen(block, scale, first):
    sq = squares(block)
    high, middle, low = pieces_of(sq)
    lane = lax.broadcasted_iota(jnp.int32, block.shape, 1)
    base = 0 if first else 3
    one = 3 - base
    extra = jnp.where(lane == base, high, 0.0)
    extra = jnp.where(lane == base + 1, middle, extra)
    extra = jnp.where(lane == base + 2, low, extra)
    extra = jnp.where((lane >= one) & (lane < one + 3), 1.0, extra)
    scaled = block.astype(jnp.float32) * scale
    return jnp.concatenate(
        [scaled.astype(jnp.bfloat16), extra.astype(jnp.bfloat16)], axis=1
    )


def pack_kernel(points, direction, residual, to_col, to_row, step_in, rest_in, sems):
    size, dims = points.shape
    copies = [
        pltpu.make_async_copy(source, target, sems.at[i])
        for i, (source, target) in enumerate(
            (
                (direction, step_in),
                (residual, rest_in),
                (points, to_col.at[pl.ds(0, size), :]),
                (points, to_row.at[pl.ds(0, size), :]),
            )
        )
    ]
    for copy in copies:
        copy.start()
    for copy in copies[:2]:
        copy.wait()
    step = fold(step_in[...], dims)
    rest = fold(rest_in[...], dims)
    zero = jnp.zeros_like(step)
    to_col[size:, :] = jnp.concatenate([step, zero], axis=0).astype(jnp.bfloat16)
    to_row[size:, :] = jnp.concatenate(
        [*pieces_of(step), *pieces_of(rest)], axis=0
    ).astype(jnp.bfloat16)
    for copy in copies[2:]:
        copy.wait()


def product_kernel(lo, hi, *refs):
    rows, refs = refs[:lo], refs[lo:]
    cols, refs = refs[:hi], refs[hi:]
    length, out, row_wide, weights, dist = refs
    cands = length.shape[0]
    dims = rows[0].shape[1]
    tall = out.shape[0] // lo
    size = tall * dims // cands
    chunk = 32
    rates = [
        (-0.5 * LOG2E) / (length[c] * length[c]) for c in range(cands)
    ]
    for k in range(lo):
        row_wide[pl.ds(k * size, size), :] = widen(rows[k][:size, :], 1.0, True)
    total = [[jnp.zeros((8, size), jnp.float32)] * cands for _ in range(lo)]
    for h in range(hi):
        tail = cols[h][size:, :].astype(jnp.float32)
        step = unfold(tail[:tall], cands)
        step = jnp.concatenate([step, jnp.zeros((8 - cands, size), jnp.float32)]).T
        for c in range(cands):
            weights[c] = jnp.broadcast_to(step[:, c : c + 1], (size, dims))
        dist[...] = lax.dot_general(
            widen(cols[h][:size, :], -2.0, False),
            row_wide[...],
            (((1,), (1,)), ((), ())),
            preferred_element_type=jnp.float32,
        )
        for k in range(lo):
            for j in range(0, size, chunk):
                here = dist[pl.ds(j, chunk), pl.ds(k * size, size)]
                for c in range(cands):
                    weight = weights[c, pl.ds(j, chunk), :]
                    weight = jnp.concatenate([weight] * (size // dims), axis=1)
                    kern = jnp.exp2(here * rates[c]) * weight
                    total[k][c] = total[k][c] + jnp.sum(
                        kern.reshape(chunk // 8, 8, size), axis=0
                    )
    for k in range(lo):
        part = [jnp.sum(total[k][c], axis=0, keepdims=True) for c in range(cands)]
        out[pl.ds(k * tall, tall), :] = fold(jnp.concatenate(part, axis=0), dims)


def add_kernel(step, tall, mine, other, out):
    for k in range(mine.shape[0] // tall):
        at = pl.ds(k * tall, tall)
        out[at, :] = mine[at, :] + other[pl.ds((k ^ step) * tall, tall), :]


def sums_kernel(lo, *refs):
    parts, refs = refs[:2], refs[2:]
    rows, refs = refs[:lo], refs[lo:]
    noise, image_out, sums_out = refs
    cands = noise.shape[0]
    tall, dims = image_out.shape
    size = rows[0].shape[0] - 6 * tall
    which = lax.broadcasted_iota(jnp.int32, (tall, 1), 0) % cands
    sigma = jnp.zeros((tall, 1), jnp.float32)
    for c in range(cands):
        sigma = jnp.where(which == c, noise[c], sigma)
    sums = [jnp.zeros((tall, dims), jnp.float32)] * 4
    for k in range(lo):
        tail = rows[k][size:, :].astype(jnp.float32)
        tail = [tail[p * tall : (p + 1) * tall] for p in range(6)]
        step = tail[0] + tail[1] + tail[2]
        rest = tail[3] + tail[4] + tail[5]
        image = sigma * step
        image += parts[0][pl.ds(k * tall, tall), :]
        image += parts[1][pl.ds((k ^ (lo // 2)) * tall, tall), :]
        if k == 0:
            image_out[...] = image
        terms = (rest * rest, step * image, rest * image, image * image)
        sums = [s + t for s, t in zip(sums, terms)]
    for i, s in enumerate(sums):
        sums_out[pl.ds(i * cands, cands), :] = sum(
            s[p : p + cands] for p in range(0, tall, cands)
        )


def update_kernel(*refs):
    sums, refs = refs[:2], refs[2:]
    image, solution, residual, direction, out_s, out_r, out_d = refs
    cands = solution.shape[0]
    total = sums[0][...] + sums[1][...]
    total = jnp.sum(total, axis=1, keepdims=True)
    norm, curve, cross, square = (
        total[i * cands : (i + 1) * cands] for i in range(4)
    )
    alpha = norm / curve
    norm_next = norm - 2.0 * alpha * cross + alpha * (alpha * square)
    beta = norm_next / norm
    step = direction[...]
    fresh = residual[...] - alpha * unfold(image[...], cands)
    out_s[...] = solution[...] + alpha * step
    out_r[...] = fresh
    out_d[...] = fresh + beta * step


def per_device(devices, points, lengthscale, noise, solution, residual, direction):
    hi, lo = split_sizes(devices)
    assert hi & (hi - 1) == lo & (lo - 1) == 0
    size, dims = points.shape
    cands = direction.shape[0]
    tall = cands * size // dims

    def from_row(x, k):
        pairs = [
            (h * lo + l, h * lo + (l ^ k)) for h in range(hi) for l in range(lo)
        ]
        return lax.ppermute(x, "blk", pairs)

    def from_col(x, k):
        pairs = [
            (h * lo + l, (h ^ k) * lo + l) for h in range(hi) for l in range(lo)
        ]
        return lax.ppermute(x, "blk", pairs)

    def butterfly(x, fetch, count, tall, swaps):
        k = 1
        while 2 * k < count:
            x = pl.pallas_call(
                functools.partial(add_kernel, k if swaps else 0, tall),
                out_shape=jax.ShapeDtypeStruct(x.shape, x.dtype),
                in_specs=[vmem, vmem],
                out_specs=vmem,
                compiler_params=params,
                name="add",
            )(x, fetch(x, k))
            k *= 2
        return x, fetch(x, k)

    vmem = pl.BlockSpec(memory_space=pltpu.VMEM)
    smem = pl.BlockSpec(memory_space=pltpu.SMEM)
    params = pltpu.CompilerParams(vmem_limit_bytes=48 * 1024 * 1024)

    to_col, to_row = pl.pallas_call(
        pack_kernel,
        out_shape=(
            jax.ShapeDtypeStruct((size + 2 * tall, dims), jnp.bfloat16),
            jax.ShapeDtypeStruct((size + 6 * tall, dims), jnp.bfloat16),
        ),
        in_specs=[pl.BlockSpec(memory_space=pltpu.HBM)] * 3,
        out_specs=(vmem, vmem),
        scratch_shapes=[
            pltpu.VMEM((cands, size), jnp.float32),
            pltpu.VMEM((cands, size), jnp.float32),
            pltpu.SemaphoreType.DMA((4,)),
        ],
        compiler_params=params,
        name="pack",
    )(*(pltpu.with_memory_space_constraint(x, pltpu.HBM) for x in (points, direction, residual)))
    cols = [to_col] + [from_col(to_col, k) for k in range(1, hi)]
    rows = [to_row] + [from_row(to_row, k) for k in range(1, lo)]

    partial = pl.pallas_call(
        functools.partial(product_kernel, lo, hi),
        out_shape=jax.ShapeDtypeStruct((lo * tall, dims), jnp.float32),
        in_specs=[vmem] * (lo + hi) + [smem],
        out_specs=vmem,
        scratch_shapes=[
            pltpu.VMEM((lo * size, 2 * dims), jnp.bfloat16),
            pltpu.VMEM((cands, size, dims), jnp.float32),
            pltpu.VMEM((size, lo * size), jnp.float32),
        ],
        compiler_params=params,
        name="product",
    )(*rows, *cols, lengthscale)

    image, sums = pl.pallas_call(
        functools.partial(sums_kernel, lo),
        out_shape=(
            jax.ShapeDtypeStruct((tall, dims), jnp.float32),
            jax.ShapeDtypeStruct((4 * cands, dims), jnp.float32),
        ),
        in_specs=[vmem] * (2 + lo) + [smem],
        out_specs=(vmem, vmem),
        compiler_params=params,
        name="sums",
    )(*butterfly(partial, from_row, lo, tall, True), *rows, noise)

    return pl.pallas_call(
        update_kernel,
        out_shape=(jax.ShapeDtypeStruct((cands, size), jnp.float32),) * 3,
        in_specs=[vmem] * 6,
        out_specs=(vmem,) * 3,
        compiler_params=params,
        name="update",
    )(*butterfly(sums, from_col, hi, 4 * cands, False), image, solution, residual, direction)


def solution(mesh):
    split = P(None, ("groups", "blk"))
    return jax.shard_map(
        functools.partial(per_device, mesh.shape["blk"]),
        mesh=mesh,
        in_specs=(P(("groups", "blk"), None), P("groups"), P("groups"), split, split, split),
        out_specs=(split, split, split),
        check_vma=False,
    )
```

```python
import functools
import math

import jax
import jax.numpy as jnp
from jax import lax
from jax.experimental import pallas as pl
from jax.experimental.pallas import tpu as pltpu
from jax.sharding import PartitionSpec as P

LOG2E = 1.4426950408889634
CHUNK = 32


def split_sizes(devices):
    lo = max(d for d in range(1, math.isqrt(devices) + 1) if devices % d == 0)
    hi = devices // lo
    assert hi & (hi - 1) == lo & (lo - 1) == 0
    return hi, lo


def pieces_of(wide):
    high = wide.astype(jnp.bfloat16).astype(jnp.float32)
    middle = (wide - high).astype(jnp.bfloat16).astype(jnp.float32)
    return [high, middle, wide - high - middle]


def fold(wide, dims):
    return jnp.concatenate(
        [wide[:, p : p + dims] for p in range(0, wide.shape[1], dims)], axis=0
    )


def unfold(tall, n):
    return jnp.concatenate(
        [tall[p : p + n] for p in range(0, tall.shape[0], n)], axis=1
    )


def squares(points):
    wide = points.astype(jnp.float32)
    wide = wide * wide
    high = wide.astype(jnp.bfloat16)
    low = (wide - high.astype(jnp.float32)).astype(jnp.bfloat16)
    ones = jnp.ones((8, points.shape[1]), jnp.bfloat16)
    sums = [
        lax.dot_general(
            ones, half, (((1,), (1,)), ((), ())), preferred_element_type=jnp.float32
        )
        for half in (high, low)
    ]
    return (sums[0] + sums[1])[:1]


def pack_kernel(points, direction, residual, length, noise, packed, own, rates, *scratch):
    step_in, rest_in, length_in, noise_in, sems = scratch
    size, dims = points.shape
    cands = direction.shape[0]
    lines = (packed.shape[0] - size) * dims // size
    copies = [
        pltpu.make_async_copy(source, target, sems.at[i])
        for i, (source, target) in enumerate(
            (
                (points, packed.at[pl.ds(0, size), :]),
                (direction, step_in),
                (residual, rest_in),
                (length, length_in),
                (noise, noise_in),
            )
        )
    ]
    for copy in copies:
        copy.start()
    for copy in copies[1:]:
        copy.wait()
    step = step_in[...]
    which = lax.broadcasted_iota(jnp.int32, (cands, 1), 0)
    sigma = jnp.zeros((cands, 1), jnp.float32)
    for c in range(cands):
        sigma = jnp.where(which == c, noise_in[c], sigma)
        rate = (-0.5 * LOG2E) / (length_in[c] * length_in[c])
        rates[pl.ds(8 * c, 8), :] = jnp.full((8, size), rate, jnp.float32)
    tall = own.shape[0] // 3
    for i, wide in enumerate((step, rest_in[...], sigma * step)):
        own[pl.ds(i * tall, tall), :] = fold(wide, dims)
    copies[0].wait()
    sq = squares(packed[:size, :])
    top = [*pieces_of(sq), jnp.ones((3, size), jnp.float32), jnp.zeros((2, size), jnp.float32)]
    top += [step, jnp.zeros((lines - 8 - cands, size), jnp.float32)]
    top = jnp.concatenate([t for t in top if t.shape[0]], axis=0)
    packed[size:, :] = fold(top, dims).astype(jnp.bfloat16)


def product_kernel(lo, hi, cands, *refs):
    cols, refs = refs[:hi], refs[hi:]
    rows, refs = refs[: lo - 1], refs[lo - 1 :]
    own, rates, out, row_wide, weights, dist = refs
    rows = (cols[0], *rows)
    tall = own.shape[0] // 3
    dims = own.shape[1]
    size = rates.shape[1]
    lines = (cols[0].shape[0] - size) * dims // size

    def extra(top):
        top = jnp.concatenate(
            [top, jnp.zeros((dims - top.shape[0], size), jnp.float32)], axis=0
        )
        return top.T

    for k in range(lo):
        top = unfold(rows[k][size:, :].astype(jnp.float32), lines)
        top = jnp.concatenate([top[3:6], top[:3], jnp.zeros((2, size), jnp.float32)])
        row_wide[pl.ds(k * size, size), :] = jnp.concatenate(
            [rows[k][:size, :], extra(top).astype(jnp.bfloat16)], axis=1
        )
    for h in range(hi):
        top = extra(unfold(cols[h][size:, :].astype(jnp.float32), lines))
        for c in range(cands):
            weights[c, pl.ds(h * size, size), :] = jnp.broadcast_to(
                top[:, 8 + c : 9 + c], (size, dims)
            )
        scaled = (cols[h][:size, :].astype(jnp.float32) * -2.0).astype(jnp.bfloat16)
        dist[pl.ds(h * size, size), :] = lax.dot_general(
            jnp.concatenate([scaled, top.astype(jnp.bfloat16)], axis=1),
            row_wide[...],
            (((1,), (1,)), ((), ())),
            preferred_element_type=jnp.float32,
        )

    def body(step, total):
        total = list(total)
        for j in range(0, CHUNK, 8):
            at = pl.ds(pl.multiple_of(step * CHUNK + j, 8), 8)
            for k in range(lo):
                here = dist[at, pl.ds(k * size, size)]
                for c in range(cands):
                    weight = jnp.concatenate(
                        [weights[c, at, :]] * (size // dims), axis=1
                    )
                    kern = jnp.exp2(here * rates[pl.ds(8 * c, 8), :])
                    total[k * cands + c] += kern * weight
        return tuple(total)

    total = lax.fori_loop(
        0,
        hi * size // CHUNK,
        body,
        (jnp.zeros((8, size), jnp.float32),) * (lo * cands),
    )
    for k in range(lo):
        part = [
            jnp.sum(total[k * cands + c], axis=0, keepdims=True) for c in range(cands)
        ]
        part = fold(jnp.concatenate(part, axis=0), dims)
        if k == 0:
            part += own[pl.ds(2 * tall, tall), :]
        out[pl.ds(k * tall, tall), :] = part
    out[pl.ds(lo * tall, 2 * tall), :] = own[pl.ds(0, 2 * tall), :]


def sums_kernel(cands, *refs):
    *parts, image_out, sums_out = refs
    lo = len(parts)
    tall, dims = image_out.shape
    sums = [jnp.zeros((tall, dims), jnp.float32)] * 4
    for k in range(lo):
        step = parts[k][pl.ds(lo * tall, tall), :]
        rest = parts[k][pl.ds((lo + 1) * tall, tall), :]
        image = parts[0][pl.ds(k * tall, tall), :]
        for m in range(1, lo):
            image = image + parts[m][pl.ds((k ^ m) * tall, tall), :]
        if k == 0:
            image_out[...] = image
        terms = (rest * rest, step * image, rest * image, image * image)
        sums = [s + t for s, t in zip(sums, terms)]
    for i, s in enumerate(sums):
        sums_out[pl.ds(i * cands, cands), :] = sum(
            s[p : p + cands] for p in range(0, tall, cands)
        )


def update_kernel(hi, *refs):
    sums, refs = refs[:hi], refs[hi:]
    image, solution, residual, direction, out_s, out_r, out_d = refs
    cands = solution.shape[0]
    total = sums[0][...]
    for h in range(1, hi):
        total = total + sums[h][...]
    total = jnp.sum(total, axis=1, keepdims=True)
    norm, curve, cross, square = (
        total[i * cands : (i + 1) * cands] for i in range(4)
    )
    alpha = norm / curve
    norm_next = norm - 2.0 * alpha * cross + alpha * (alpha * square)
    beta = norm_next / norm
    step = direction[...]
    fresh = residual[...] - alpha * unfold(image[...], cands)
    out_s[...] = solution[...] + alpha * step
    out_r[...] = fresh
    out_d[...] = fresh + beta * step


def per_device(devices, points, lengthscale, noise, solution, residual, direction):
    hi, lo = split_sizes(devices)
    size, dims = points.shape
    cands = direction.shape[0]
    tall = cands * size // dims
    extra = -(-(8 + cands) // 16) * 16 * size // dims

    def meet(x, mask):
        return lax.ppermute(x, "blk", [(d, d ^ mask) for d in range(devices)])

    vmem = pl.BlockSpec(memory_space=pltpu.VMEM)
    hbm = pl.BlockSpec(memory_space=pltpu.HBM)
    params = pltpu.CompilerParams(vmem_limit_bytes=50 * 1024 * 1024)

    packed, own, rates = pl.pallas_call(
        pack_kernel,
        out_shape=(
            jax.ShapeDtypeStruct((size + extra, dims), jnp.bfloat16),
            jax.ShapeDtypeStruct((3 * tall, dims), jnp.float32),
            jax.ShapeDtypeStruct((8 * cands, size), jnp.float32),
        ),
        in_specs=[hbm] * 5,
        out_specs=(vmem,) * 3,
        scratch_shapes=[
            pltpu.VMEM((cands, size), jnp.float32),
            pltpu.VMEM((cands, size), jnp.float32),
            pltpu.SMEM((cands,), jnp.float32),
            pltpu.SMEM((cands,), jnp.float32),
            pltpu.SemaphoreType.DMA((5,)),
        ],
        compiler_params=params,
        name="pack",
    )(
        *(
            pltpu.with_memory_space_constraint(x, pltpu.HBM)
            for x in (points, direction, residual, lengthscale, noise)
        )
    )

    cols = [packed] + [meet(packed, k * lo) for k in range(1, hi)]
    rows = [packed] + [meet(packed, k) for k in range(1, lo) if k == 1 or k % 2 == 0]
    if lo > 2:
        rows = [packed, rows[1]] + [
            block
            for k in range(2, lo, 2)
            for block in (rows[k // 2 + 1], meet(rows[k // 2 + 1], 1))
        ]

    partial = pl.pallas_call(
        functools.partial(product_kernel, lo, hi, cands),
        out_shape=jax.ShapeDtypeStruct(((lo + 2) * tall, dims), jnp.float32),
        in_specs=[vmem] * (hi + lo + 1),
        out_specs=vmem,
        scratch_shapes=[
            pltpu.VMEM((lo * size, 2 * dims), jnp.bfloat16),
            pltpu.VMEM((cands, hi * size, dims), jnp.float32),
            pltpu.VMEM((hi * size, lo * size), jnp.float32),
        ],
        compiler_params=params,
        name="product",
    )(*cols, *rows[1:], own, rates)

    image, sums = pl.pallas_call(
        functools.partial(sums_kernel, cands),
        out_shape=(
            jax.ShapeDtypeStruct((tall, dims), jnp.float32),
            jax.ShapeDtypeStruct((4 * cands, dims), jnp.float32),
        ),
        in_specs=[vmem] * lo,
        out_specs=(vmem, vmem),
        compiler_params=params,
        name="sums",
    )(partial, *(meet(partial, k) for k in range(1, lo)))

    return pl.pallas_call(
        functools.partial(update_kernel, hi),
        out_shape=(jax.ShapeDtypeStruct((cands, size), jnp.float32),) * 3,
        in_specs=[vmem] * (hi + 4),
        out_specs=(vmem,) * 3,
        compiler_params=params,
        name="update",
    )(sums, *(meet(sums, k * lo) for k in range(1, hi)), image, solution, residual, direction)


def solution(mesh):
    split = P(None, ("groups", "blk"))
    return jax.shard_map(
        functools.partial(per_device, mesh.shape["blk"]),
        mesh=mesh,
        in_specs=(P(("groups", "blk"), None), P("groups"), P("groups"), split, split, split),
        out_specs=(split, split, split),
        check_vma=False,
    )
```

```python
import functools
import math

import jax
import jax.numpy as jnp
from jax import lax
from jax.experimental import pallas as pl
from jax.experimental.pallas import tpu as pltpu
from jax.sharding import PartitionSpec as P

CHUNK = 32


def split_sizes(devices):
    lo = max(d for d in range(1, math.isqrt(devices) + 1) if devices % d == 0)
    hi = devices // lo
    assert hi & (hi - 1) == lo & (lo - 1) == 0
    return hi, lo


def pieces_of(wide):
    high = wide.astype(jnp.bfloat16).astype(jnp.float32)
    middle = (wide - high).astype(jnp.bfloat16).astype(jnp.float32)
    return [high, middle, wide - high - middle]


def fold(wide, dims):
    return jnp.concatenate(
        [wide[:, p : p + dims] for p in range(0, wide.shape[1], dims)], axis=0
    )


def unfold(tall, n):
    return jnp.concatenate(
        [tall[p : p + n] for p in range(0, tall.shape[0], n)], axis=1
    )


def squares(points):
    wide = points.astype(jnp.float32)
    wide = wide * wide
    high = wide.astype(jnp.bfloat16)
    low = (wide - high.astype(jnp.float32)).astype(jnp.bfloat16)
    ones = jnp.ones((8, points.shape[1]), jnp.bfloat16)
    sums = [
        lax.dot_general(
            ones, half, (((1,), (1,)), ((), ())), preferred_element_type=jnp.float32
        )
        for half in (high, low)
    ]
    return (sums[0] + sums[1])[:1]


def pack_kernel(points, direction, residual, length, noise, packed, own, rates, *scratch):
    step_in, rest_in, length_in, noise_in, sems = scratch
    size, dims = points.shape
    cands = direction.shape[0]
    lines = (packed.shape[0] - size) * dims // size
    copies = [
        pltpu.make_async_copy(source, target, sems.at[i])
        for i, (source, target) in enumerate(
            (
                (points, packed.at[pl.ds(0, size), :]),
                (direction, step_in),
                (residual, rest_in),
                (length, length_in),
                (noise, noise_in),
            )
        )
    ]
    for copy in copies:
        copy.start()
    for copy in copies[1:]:
        copy.wait()
    step = step_in[...]
    which = lax.broadcasted_iota(jnp.int32, (cands, 1), 0)
    sigma = jnp.zeros((cands, 1), jnp.float32)
    for c in range(cands):
        sigma = jnp.where(which == c, noise_in[c], sigma)
        rate = -0.5 / (length_in[c] * length_in[c])
        rates[pl.ds(8 * c, 8), :] = jnp.full((8, dims), rate, jnp.float32)
    tall = own.shape[0] // 3
    for i, wide in enumerate((step, rest_in[...], sigma * step)):
        own[pl.ds(i * tall, tall), :] = fold(wide, dims)
    copies[0].wait()
    sq = squares(packed[:size, :])
    top = [*pieces_of(sq), jnp.ones((3, size), jnp.float32), jnp.zeros((2, size), jnp.float32)]
    top += [step, jnp.zeros((lines - 8 - cands, size), jnp.float32)]
    top = jnp.concatenate([t for t in top if t.shape[0]], axis=0)
    packed[size:, :] = fold(top, dims).astype(jnp.bfloat16)


def turned(tops, size):
    row = lax.broadcasted_iota(jnp.int32, (size, size), 0)
    lane = lax.broadcasted_iota(jnp.int32, (size, size), 1)
    return lax.dot_general(
        (row == lane).astype(jnp.bfloat16),
        jnp.concatenate(tops, axis=0).astype(jnp.bfloat16),
        (((1,), (1,)), ((), ())),
        preferred_element_type=jnp.float32,
    )


def top_of(block, size):
    lines = (block.shape[0] - size) * block.shape[1] // size
    return unfold(block[size:, :].astype(jnp.float32), lines)


def padded(top, dims):
    return jnp.concatenate(
        [top, jnp.zeros((dims - top.shape[0], top.shape[1]), jnp.float32)], axis=0
    )


def widen_rows(rows, row_wide, size):
    dims = rows[0].shape[1]
    for k, block in enumerate(rows):
        top = top_of(block, size)
        top = jnp.concatenate([top[3:6], top[:3]], axis=0)
        row_wide[pl.ds(k * size, size), :] = jnp.concatenate(
            [block[:size, :], turned([padded(top, dims)], size).astype(jnp.bfloat16)],
            axis=1,
        )


def add_column(col, row_wide, rates, weights, dist, size):
    dims = col.shape[1]
    cands = rates.shape[0] // 8
    lo = row_wide.shape[0] // size
    top = top_of(col, size)
    steps = top[8 : 8 + cands]
    tops = [padded(top, dims)]
    tops += [jnp.broadcast_to(steps[c : c + 1], (dims, size)) for c in range(cands)]
    columns = turned(tops, size)
    for c in range(cands):
        weights[c] = columns[:, (c + 1) * dims : (c + 2) * dims]
    scaled = (col[:size, :].astype(jnp.float32) * -2.0).astype(jnp.bfloat16)
    dist[...] = lax.dot_general(
        jnp.concatenate([scaled, columns[:, :dims].astype(jnp.bfloat16)], axis=1),
        row_wide[...],
        (((1,), (1,)), ((), ())),
        preferred_element_type=jnp.float32,
    )
    wide = size // dims
    rate = [jnp.concatenate([rates[pl.ds(8 * c, 8), :]] * wide, axis=1) for c in range(cands)]

    def body(step, total):
        total = list(total)
        for j in range(0, CHUNK, 8):
            at = pl.ds(pl.multiple_of(step * CHUNK + j, 8), 8)
            weight = [jnp.concatenate([weights[c, at, :]] * wide, axis=1) for c in range(cands)]
            for k in range(lo):
                here = dist[at, pl.ds(k * size, size)]
                for c in range(cands):
                    total[k * cands + c] += jnp.exp(here * rate[c]) * weight[c]
        return tuple(total)

    total = lax.fori_loop(
        0,
        size // CHUNK,
        body,
        (jnp.zeros((8, size), jnp.float32),) * (lo * cands),
    )
    total = [jnp.sum(t, axis=0, keepdims=True) for t in total]
    return [
        fold(jnp.concatenate(total[k * cands : (k + 1) * cands], axis=0), dims)
        for k in range(lo)
    ]


def first_kernel(lo, *refs):
    rows, refs = refs[:lo], refs[lo:]
    own, rates, out, row_wide, weights, dist = refs
    tall, dims = own.shape[0] // 3, own.shape[1]
    size = row_wide.shape[0] // lo
    widen_rows(rows, row_wide, size)
    parts = add_column(rows[0], row_wide, rates, weights, dist, size)
    parts[0] += own[pl.ds(2 * tall, tall), :]
    for k in range(lo):
        out[pl.ds(k * tall, tall), :] = parts[k]
    out[pl.ds(lo * tall, 2 * tall), :] = own[pl.ds(0, 2 * tall), :]


def next_kernel(lo, col, row_wide, rates, before, out, weights, dist):
    size = row_wide.shape[0] // lo
    tall = before.shape[0] // (lo + 2)
    parts = add_column(col, row_wide, rates, weights, dist, size)
    for k in range(lo):
        at = pl.ds(k * tall, tall)
        out[at, :] = before[at, :] + parts[k]
    at = pl.ds(lo * tall, 2 * tall)
    out[at, :] = before[at, :]


def sums_kernel(cands, *refs):
    *parts, image_out, sums_out = refs
    lo = len(parts)
    tall, dims = image_out.shape
    sums = [jnp.zeros((tall, dims), jnp.float32)] * 4
    for k in range(lo):
        step = parts[k][pl.ds(lo * tall, tall), :]
        rest = parts[k][pl.ds((lo + 1) * tall, tall), :]
        image = parts[0][pl.ds(k * tall, tall), :]
        for m in range(1, lo):
            image = image + parts[m][pl.ds((k ^ m) * tall, tall), :]
        if k == 0:
            image_out[...] = image
        terms = (rest * rest, step * image, rest * image, image * image)
        sums = [s + t for s, t in zip(sums, terms)]
    for i, s in enumerate(sums):
        sums_out[pl.ds(i * cands, cands), :] = sum(
            s[p : p + cands] for p in range(0, tall, cands)
        )


def update_kernel(hi, *refs):
    sums, refs = refs[:hi], refs[hi:]
    image, solution, residual, direction, out_s, out_r, out_d = refs
    cands = solution.shape[0]
    total = sums[0][...]
    for h in range(1, hi):
        total = total + sums[h][...]
    total = jnp.sum(total, axis=1, keepdims=True)
    norm, curve, cross, square = (
        total[i * cands : (i + 1) * cands] for i in range(4)
    )
    alpha = norm / curve
    norm_next = norm - 2.0 * alpha * cross + alpha * (alpha * square)
    beta = norm_next / norm
    step = direction[...]
    fresh = residual[...] - alpha * unfold(image[...], cands)
    out_s[...] = solution[...] + alpha * step
    out_r[...] = fresh
    out_d[...] = fresh + beta * step


def per_device(devices, points, lengthscale, noise, solution, residual, direction):
    hi, lo = split_sizes(devices)
    size, dims = points.shape
    cands = direction.shape[0]
    tall = cands * size // dims
    extra = -(-(8 + cands) // 16) * 16 * size // dims

    def meet(x, mask):
        return lax.ppermute(x, "blk", [(d, d ^ mask) for d in range(devices)])

    vmem = pl.BlockSpec(memory_space=pltpu.VMEM)
    hbm = pl.BlockSpec(memory_space=pltpu.HBM)
    params = pltpu.CompilerParams(vmem_limit_bytes=50 * 1024 * 1024)

    packed, own, rates = pl.pallas_call(
        pack_kernel,
        out_shape=(
            jax.ShapeDtypeStruct((size + extra, dims), jnp.bfloat16),
            jax.ShapeDtypeStruct((3 * tall, dims), jnp.float32),
            jax.ShapeDtypeStruct((8 * cands, dims), jnp.float32),
        ),
        in_specs=[hbm] * 5,
        out_specs=(vmem,) * 3,
        scratch_shapes=[
            pltpu.VMEM((cands, size), jnp.float32),
            pltpu.VMEM((cands, size), jnp.float32),
            pltpu.SMEM((cands,), jnp.float32),
            pltpu.SMEM((cands,), jnp.float32),
            pltpu.SemaphoreType.DMA((5,)),
        ],
        compiler_params=params,
        name="pack",
    )(
        *(
            pltpu.with_memory_space_constraint(x, pltpu.HBM)
            for x in (points, direction, residual, lengthscale, noise)
        )
    )

    rows = [packed] + [meet(packed, k) for k in range(1, lo)]

    terms = size * lo * size
    cost = pl.CostEstimate(
        flops=4 * dims * terms + 4 * cands * terms,
        bytes_accessed=4 * terms,
        transcendentals=cands * terms,
    )
    spare = [
        pltpu.VMEM((cands, size, dims), jnp.float32),
        pltpu.VMEM((size, lo * size), jnp.float32),
    ]
    result = jax.ShapeDtypeStruct(((lo + 2) * tall, dims), jnp.float32)
    partial, row_wide = pl.pallas_call(
        functools.partial(first_kernel, lo),
        out_shape=(result, jax.ShapeDtypeStruct((lo * size, 2 * dims), jnp.bfloat16)),
        in_specs=[vmem] * (lo + 2),
        out_specs=(vmem, vmem),
        scratch_shapes=spare,
        compiler_params=params,
        cost_estimate=cost,
        name="product_own",
    )(*rows, own, rates)
    for k in range(hi - 1, 0, -1):
        partial = pl.pallas_call(
            functools.partial(next_kernel, lo),
            out_shape=result,
            in_specs=[vmem] * 4,
            out_specs=vmem,
            scratch_shapes=spare,
            compiler_params=params,
            cost_estimate=cost,
            name="product_%d" % k,
        )(meet(packed, k * lo), row_wide, rates, partial)

    image, sums = pl.pallas_call(
        functools.partial(sums_kernel, cands),
        out_shape=(
            jax.ShapeDtypeStruct((tall, dims), jnp.float32),
            jax.ShapeDtypeStruct((4 * cands, dims), jnp.float32),
        ),
        in_specs=[vmem] * lo,
        out_specs=(vmem, vmem),
        compiler_params=params,
        name="sums",
    )(partial, *(meet(partial, k) for k in range(1, lo)))

    return pl.pallas_call(
        functools.partial(update_kernel, hi),
        out_shape=(jax.ShapeDtypeStruct((cands, size), jnp.float32),) * 3,
        in_specs=[vmem] * (hi + 4),
        out_specs=(vmem,) * 3,
        compiler_params=params,
        name="update",
    )(sums, *(meet(sums, k * lo) for k in range(1, hi)), image, solution, residual, direction)


def solution(mesh):
    split = P(None, ("groups", "blk"))
    return jax.shard_map(
        functools.partial(per_device, mesh.shape["blk"]),
        mesh=mesh,
        in_specs=(P(("groups", "blk"), None), P("groups"), P("groups"), split, split, split),
        out_specs=(split, split, split),
        check_vma=False,
    )
```

```python
import functools
import math

import jax
import jax.numpy as jnp
from jax import lax
from jax.experimental import pallas as pl
from jax.experimental.pallas import tpu as pltpu
from jax.sharding import PartitionSpec as P


def split_sizes(devices):
    lo = max(d for d in range(1, math.isqrt(devices) + 1) if devices % d == 0)
    hi = devices // lo
    assert hi & (hi - 1) == lo & (lo - 1) == 0
    return hi, lo


def pieces_of(wide):
    high = wide.astype(jnp.bfloat16).astype(jnp.float32)
    middle = (wide - high).astype(jnp.bfloat16).astype(jnp.float32)
    return [high, middle, wide - high - middle]


def fold(wide, dims):
    return jnp.concatenate(
        [wide[:, p : p + dims] for p in range(0, wide.shape[1], dims)], axis=0
    )


def unfold(tall, n):
    return jnp.concatenate(
        [tall[p : p + n] for p in range(0, tall.shape[0], n)], axis=1
    )


def squares(points):
    wide = points.astype(jnp.float32)
    wide = wide * wide
    high = wide.astype(jnp.bfloat16)
    low = (wide - high.astype(jnp.float32)).astype(jnp.bfloat16)
    ones = jnp.ones((8, points.shape[1]), jnp.bfloat16)
    sums = [
        lax.dot_general(
            ones, half, (((1,), (1,)), ((), ())), preferred_element_type=jnp.float32
        )
        for half in (high, low)
    ]
    return (sums[0] + sums[1])[:1]


def pack_kernel(points, direction, residual, length, noise, packed, own, rates, *scratch):
    step_in, rest_in, length_in, noise_in, sems = scratch
    size, dims = points.shape
    cands = direction.shape[0]
    lines = (packed.shape[0] - size) * dims // size
    copies = [
        pltpu.make_async_copy(source, target, sems.at[i])
        for i, (source, target) in enumerate(
            (
                (points, packed.at[pl.ds(0, size), :]),
                (direction, step_in),
                (residual, rest_in),
                (length, length_in),
                (noise, noise_in),
            )
        )
    ]
    for copy in copies:
        copy.start()
    for copy in copies[1:]:
        copy.wait()
    step = step_in[...]
    which = lax.broadcasted_iota(jnp.int32, (cands, 1), 0)
    sigma = jnp.zeros((cands, 1), jnp.float32)
    for c in range(cands):
        sigma = jnp.where(which == c, noise_in[c], sigma)
        rate = -0.5 / (length_in[c] * length_in[c])
        rates[pl.ds(8 * c, 8), :] = jnp.full((8, dims), rate, jnp.float32)
    tall = own.shape[0] // 3
    for i, wide in enumerate((step, rest_in[...], sigma * step)):
        own[pl.ds(i * tall, tall), :] = fold(wide, dims)
    copies[0].wait()
    sq = squares(packed[:size, :])
    top = [*pieces_of(sq), jnp.ones((3, size), jnp.float32), jnp.zeros((2, size), jnp.float32)]
    top += [step, jnp.zeros((lines - 8 - cands, size), jnp.float32)]
    top = jnp.concatenate([t for t in top if t.shape[0]], axis=0)
    packed[size:, :] = fold(top, dims).astype(jnp.bfloat16)


def turned(tops, size):
    row = lax.broadcasted_iota(jnp.int32, (size, size), 0)
    lane = lax.broadcasted_iota(jnp.int32, (size, size), 1)
    return lax.dot_general(
        (row == lane).astype(jnp.bfloat16),
        jnp.concatenate(tops, axis=0).astype(jnp.bfloat16),
        (((1,), (1,)), ((), ())),
        preferred_element_type=jnp.float32,
    )


def top_of(block, size):
    lines = (block.shape[0] - size) * block.shape[1] // size
    return unfold(block[size:, :].astype(jnp.float32), lines)


def padded(top, dims):
    return jnp.concatenate(
        [top, jnp.zeros((dims - top.shape[0], top.shape[1]), jnp.float32)], axis=0
    )


def widen_rows(rows, row_wide, size):
    dims = rows[0].shape[1]
    ones = jnp.ones((3, size), jnp.float32)
    for k, block in enumerate(rows):
        top = jnp.concatenate([ones, *pieces_of(squares(block[:size, :]))], axis=0)
        scaled = (block[:size, :].astype(jnp.float32) * -2.0).astype(jnp.bfloat16)
        extra = turned([padded(top, dims)], size).astype(jnp.bfloat16)
        row_wide[pl.ds(k * size, size), :] = jnp.concatenate([scaled, extra], axis=1)


def add_column(col, row_wide, rates, size):
    dims = col.shape[1]
    cands = rates.shape[0] // 8
    top = top_of(col, size)
    steps = top[8 : 8 + cands]
    top = padded(top, dims).astype(jnp.bfloat16)
    which = lax.broadcasted_iota(jnp.int32, (cands, 1), 0)
    only = [jnp.where(which == c, steps, 0.0).astype(jnp.bfloat16) for c in range(cands)]
    rate = [
        jnp.concatenate([rates[pl.ds(8 * c, 8), :]] * (size // dims), axis=1)
        for c in range(cands)
    ]
    parts = []
    for k in range(row_wide.shape[0] // size):
        at = pl.ds(k * size, size)
        dist = lax.dot_general(
            row_wide[at, :dims],
            col[:size, :],
            (((1,), (1,)), ((), ())),
            preferred_element_type=jnp.float32,
        )
        dist += jnp.dot(row_wide[at, dims:], top, preferred_element_type=jnp.float32)
        dist = dist.reshape(size // 8, 8, size)
        part = jnp.zeros((cands, size), jnp.float32)
        for c in range(cands):
            kern = jnp.exp(dist * rate[c][None]).reshape(size, size)
            part += lax.dot_general(
                only[c],
                kern.astype(jnp.bfloat16),
                (((1,), (1,)), ((), ())),
                preferred_element_type=jnp.float32,
            )
        parts.append(fold(part, dims))
    return parts


def first_kernel(lo, *refs):
    rows, refs = refs[:lo], refs[lo:]
    own, rates, out, row_wide = refs
    tall = own.shape[0] // 3
    size = row_wide.shape[0] // lo
    widen_rows(rows, row_wide, size)
    parts = add_column(rows[0], row_wide, rates, size)
    parts[0] += own[pl.ds(2 * tall, tall), :]
    for k in range(lo):
        out[pl.ds(k * tall, tall), :] = parts[k]
    out[pl.ds(lo * tall, 2 * tall), :] = own[pl.ds(0, 2 * tall), :]


def next_kernel(lo, col, row_wide, rates, before, out):
    size = row_wide.shape[0] // lo
    tall = before.shape[0] // (lo + 2)
    parts = add_column(col, row_wide, rates, size)
    for k in range(lo):
        at = pl.ds(k * tall, tall)
        out[at, :] = before[at, :] + parts[k]
    at = pl.ds(lo * tall, 2 * tall)
    out[at, :] = before[at, :]


def sums_kernel(cands, *refs):
    *parts, image_out, sums_out = refs
    lo = len(parts)
    tall, dims = image_out.shape
    sums = [jnp.zeros((tall, dims), jnp.float32)] * 4
    for k in range(lo):
        step = parts[k][pl.ds(lo * tall, tall), :]
        rest = parts[k][pl.ds((lo + 1) * tall, tall), :]
        image = parts[0][pl.ds(k * tall, tall), :]
        for m in range(1, lo):
            image = image + parts[m][pl.ds((k ^ m) * tall, tall), :]
        if k == 0:
            image_out[...] = image
        terms = (rest * rest, step * image, rest * image, image * image)
        sums = [s + t for s, t in zip(sums, terms)]
    for i, s in enumerate(sums):
        sums_out[pl.ds(i * cands, cands), :] = sum(
            s[p : p + cands] for p in range(0, tall, cands)
        )


def update_kernel(hi, *refs):
    sums, refs = refs[:hi], refs[hi:]
    image, solution, residual, direction, out_s, out_r, out_d = refs
    cands = solution.shape[0]
    total = sums[0][...]
    for h in range(1, hi):
        total = total + sums[h][...]
    total = jnp.sum(total, axis=1, keepdims=True)
    norm, curve, cross, square = (
        total[i * cands : (i + 1) * cands] for i in range(4)
    )
    alpha = norm / curve
    norm_next = norm - 2.0 * alpha * cross + alpha * (alpha * square)
    beta = norm_next / norm
    step = direction[...]
    fresh = residual[...] - alpha * unfold(image[...], cands)
    out_s[...] = solution[...] + alpha * step
    out_r[...] = fresh
    out_d[...] = fresh + beta * step


def per_device(devices, points, lengthscale, noise, solution, residual, direction):
    hi, lo = split_sizes(devices)
    size, dims = points.shape
    cands = direction.shape[0]
    tall = cands * size // dims
    extra = -(-(8 + cands) // 16) * 16 * size // dims

    def meet(x, mask):
        return lax.ppermute(x, "blk", [(d, d ^ mask) for d in range(devices)])

    vmem = pl.BlockSpec(memory_space=pltpu.VMEM)
    hbm = pl.BlockSpec(memory_space=pltpu.HBM)
    params = pltpu.CompilerParams(vmem_limit_bytes=50 * 1024 * 1024)

    packed, own, rates = pl.pallas_call(
        pack_kernel,
        out_shape=(
            jax.ShapeDtypeStruct((size + extra, dims), jnp.bfloat16),
            jax.ShapeDtypeStruct((3 * tall, dims), jnp.float32),
            jax.ShapeDtypeStruct((8 * cands, dims), jnp.float32),
        ),
        in_specs=[hbm] * 5,
        out_specs=(vmem,) * 3,
        scratch_shapes=[
            pltpu.VMEM((cands, size), jnp.float32),
            pltpu.VMEM((cands, size), jnp.float32),
            pltpu.SMEM((cands,), jnp.float32),
            pltpu.SMEM((cands,), jnp.float32),
            pltpu.SemaphoreType.DMA((5,)),
        ],
        compiler_params=params,
        name="pack",
    )(
        *(
            pltpu.with_memory_space_constraint(x, pltpu.HBM)
            for x in (points, direction, residual, lengthscale, noise)
        )
    )

    rows = [meet(points, k) for k in range(1, lo)]

    result = jax.ShapeDtypeStruct(((lo + 2) * tall, dims), jnp.float32)
    partial, row_wide = pl.pallas_call(
        functools.partial(first_kernel, lo),
        out_shape=(result, jax.ShapeDtypeStruct((lo * size, 2 * dims), jnp.bfloat16)),
        in_specs=[vmem] * (lo + 2),
        out_specs=(vmem, vmem),
        compiler_params=params,
        name="product_own",
    )(packed, *rows, own, rates)
    for k in range(hi - 1, 0, -1):
        partial = pl.pallas_call(
            functools.partial(next_kernel, lo),
            out_shape=result,
            in_specs=[vmem] * 4,
            out_specs=vmem,
            compiler_params=params,
            name="product_%d" % k,
        )(meet(packed, k * lo), row_wide, rates, partial)

    image, sums = pl.pallas_call(
        functools.partial(sums_kernel, cands),
        out_shape=(
            jax.ShapeDtypeStruct((tall, dims), jnp.float32),
            jax.ShapeDtypeStruct((4 * cands, dims), jnp.float32),
        ),
        in_specs=[vmem] * lo,
        out_specs=(vmem, vmem),
        compiler_params=params,
        name="sums",
    )(partial, *(meet(partial, k) for k in range(1, lo)))

    return pl.pallas_call(
        functools.partial(update_kernel, hi),
        out_shape=(jax.ShapeDtypeStruct((cands, size), jnp.float32),) * 3,
        in_specs=[vmem] * (hi + 4),
        out_specs=(vmem,) * 3,
        compiler_params=params,
        name="update",
    )(sums, *(meet(sums, k * lo) for k in range(1, hi)), image, solution, residual, direction)


def solution(mesh):
    split = P(None, ("groups", "blk"))
    return jax.shard_map(
        functools.partial(per_device, mesh.shape["blk"]),
        mesh=mesh,
        in_specs=(P(("groups", "blk"), None), P("groups"), P("groups"), split, split, split),
        out_specs=(split, split, split),
        check_vma=False,
    )
```

```python
import functools
import math

import jax
import jax.numpy as jnp
from jax import lax
from jax.experimental import pallas as pl
from jax.experimental.pallas import tpu as pltpu
from jax.sharding import PartitionSpec as P


CHUNK = 32


def split_sizes(devices):
    lo = max(d for d in range(1, math.isqrt(devices) + 1) if devices % d == 0)
    hi = devices // lo
    assert lo > 1 and hi & (hi - 1) == lo & (lo - 1) == 0
    return hi, lo


def pieces_of(wide):
    high = wide.astype(jnp.bfloat16).astype(jnp.float32)
    middle = (wide - high).astype(jnp.bfloat16).astype(jnp.float32)
    return [high, middle, wide - high - middle]


def fold(wide, dims):
    return jnp.concatenate(
        [wide[:, p : p + dims] for p in range(0, wide.shape[1], dims)], axis=0
    )


def unfold(tall, n):
    return jnp.concatenate(
        [tall[p : p + n] for p in range(0, tall.shape[0], n)], axis=1
    )


def squares(points):
    wide = points.astype(jnp.float32)
    wide = wide * wide
    high = wide.astype(jnp.bfloat16)
    low = (wide - high.astype(jnp.float32)).astype(jnp.bfloat16)
    ones = jnp.ones((8, points.shape[1]), jnp.bfloat16)
    sums = [
        lax.dot_general(
            ones, half, (((1,), (1,)), ((), ())), preferred_element_type=jnp.float32
        )
        for half in (high, low)
    ]
    return (sums[0] + sums[1])[:1]


def pack_kernel(points, direction, residual, length, noise, packed, own, rates, *scratch):
    step_in, rest_in, length_in, noise_in, sems = scratch
    size, dims = points.shape
    cands = direction.shape[0]
    lines = (packed.shape[0] - size) * dims // size
    copies = [
        pltpu.make_async_copy(source, target, sems.at[i])
        for i, (source, target) in enumerate(
            (
                (points, packed.at[pl.ds(0, size), :]),
                (direction, step_in),
                (residual, rest_in),
                (length, length_in),
                (noise, noise_in),
            )
        )
    ]
    for copy in copies:
        copy.start()
    for copy in copies[1:]:
        copy.wait()
    step = step_in[...]
    which = lax.broadcasted_iota(jnp.int32, (cands, 1), 0)
    sigma = jnp.zeros((cands, 1), jnp.float32)
    for c in range(cands):
        sigma = jnp.where(which == c, noise_in[c], sigma)
        rate = -0.5 / (length_in[c] * length_in[c])
        rates[pl.ds(8 * c, 8), :] = jnp.full((8, dims), rate, jnp.float32)
    tall = own.shape[0] // 3
    for i, wide in enumerate((step, rest_in[...], sigma * step)):
        own[pl.ds(i * tall, tall), :] = fold(wide, dims)
    copies[0].wait()
    sq = squares(packed[:size, :])
    top = [*pieces_of(sq), jnp.ones((3, size), jnp.float32), jnp.zeros((2, size), jnp.float32)]
    top += [step, jnp.zeros((lines - 8 - cands, size), jnp.float32)]
    top = jnp.concatenate([t for t in top if t.shape[0]], axis=0)
    packed[size:, :] = fold(top, dims).astype(jnp.bfloat16)


def turned(tops, size):
    row = lax.broadcasted_iota(jnp.int32, (size, size), 0)
    lane = lax.broadcasted_iota(jnp.int32, (size, size), 1)
    return lax.dot_general(
        (row == lane).astype(jnp.bfloat16),
        jnp.concatenate(tops, axis=0).astype(jnp.bfloat16),
        (((1,), (1,)), ((), ())),
        preferred_element_type=jnp.float32,
    )


def top_of(block, size):
    lines = (block.shape[0] - size) * block.shape[1] // size
    return unfold(block[size:, :].astype(jnp.float32), lines)


def padded(top, dims):
    return jnp.concatenate(
        [top, jnp.zeros((dims - top.shape[0], top.shape[1]), jnp.float32)], axis=0
    )


def widen_rows(rows, row_wide, size):
    dims = rows[0].shape[1]
    ones = jnp.ones((3, size), jnp.float32)
    for k, block in enumerate(rows):
        top = jnp.concatenate([ones, *pieces_of(squares(block[:size, :]))], axis=0)
        scaled = (block[:size, :].astype(jnp.float32) * -2.0).astype(jnp.bfloat16)
        extra = turned([padded(top, dims)], size).astype(jnp.bfloat16)
        row_wide[pl.ds(k * size, size), :] = jnp.concatenate([scaled, extra], axis=1)


def product_kernel(lo, hi, cands, *refs):
    cols, refs = refs[:hi], refs[hi:]
    rows, refs = refs[: lo - 1], refs[lo - 1 :]
    own, rates, out, row_wide, weights, dist = refs
    tall, dims = own.shape[0] // 3, own.shape[1]
    size = row_wide.shape[0] // lo
    wide = size // dims
    widen_rows((cols[0], *rows), row_wide, size)
    for h in range(hi):
        top = top_of(cols[h], size)
        steps = top[8 : 8 + cands]
        tops = [padded(top, dims)]
        tops += [jnp.broadcast_to(steps[c : c + 1], (dims, size)) for c in range(cands)]
        columns = turned(tops, size)
        at = pl.ds(h * size, size)
        for c in range(cands):
            weights[c, at, :] = columns[:, (c + 1) * dims : (c + 2) * dims]
        dist[at, :] = lax.dot_general(
            jnp.concatenate(
                [cols[h][:size, :], columns[:, :dims].astype(jnp.bfloat16)], axis=1
            ),
            row_wide[...],
            (((1,), (1,)), ((), ())),
            preferred_element_type=jnp.float32,
        )
    rate = [
        jnp.concatenate([rates[pl.ds(8 * c, 8), :]] * wide, axis=1) for c in range(cands)
    ]

    def body(step, total):
        total = list(total)
        for j in range(0, CHUNK, 8):
            at = pl.ds(pl.multiple_of(step * CHUNK + j, 8), 8)
            weight = [
                jnp.concatenate([weights[c, at, :]] * wide, axis=1) for c in range(cands)
            ]
            for k in range(lo):
                here = dist[at, pl.ds(k * size, size)]
                for c in range(cands):
                    total[k * cands + c] += jnp.exp(here * rate[c]) * weight[c]
        return tuple(total)

    total = lax.fori_loop(
        0,
        hi * size // CHUNK,
        body,
        (jnp.zeros((8, size), jnp.float32),) * (lo * cands),
    )
    total = [jnp.sum(t, axis=0, keepdims=True) for t in total]
    for k in range(lo):
        part = fold(jnp.concatenate(total[k * cands : (k + 1) * cands], axis=0), dims)
        if k == 0:
            part += own[pl.ds(2 * tall, tall), :]
        out[pl.ds(k * tall, tall), :] = part
    out[pl.ds(lo * tall, 2 * tall), :] = own[pl.ds(0, 2 * tall), :]


def add_kernel(*refs):
    *parts, out = refs
    total = parts[0][...]
    for part in parts[1:]:
        total = total + part[...]
    out[...] = total


def sums_kernel(cands, *refs):
    *parts, image_out, sums_out = refs
    lo = len(parts)
    tall, dims = image_out.shape
    sums = [jnp.zeros((tall, dims), jnp.float32)] * 4
    for k in range(lo):
        step = parts[k][pl.ds(lo * tall, tall), :]
        rest = parts[k][pl.ds((lo + 1) * tall, tall), :]
        image = parts[0][pl.ds(k * tall, tall), :]
        for m in range(1, lo):
            image = image + parts[m][pl.ds((k ^ m) * tall, tall), :]
        if k == 0:
            image_out[...] = image
        terms = (rest * rest, step * image, rest * image, image * image)
        sums = [s + t for s, t in zip(sums, terms)]
    for i, s in enumerate(sums):
        sums_out[pl.ds(i * cands, cands), :] = sum(
            s[p : p + cands] for p in range(0, tall, cands)
        )


def update_kernel(*refs):
    sums, refs = refs[:3], refs[3:]
    image, solution, residual, direction, out_s, out_r, out_d = refs
    cands = solution.shape[0]
    total = sums[0][...] + (sums[1][...] + sums[2][...])
    total = jnp.sum(total, axis=1, keepdims=True)
    norm, curve, cross, square = (
        total[i * cands : (i + 1) * cands] for i in range(4)
    )
    alpha = norm / curve
    norm_next = norm - 2.0 * alpha * cross + alpha * (alpha * square)
    beta = norm_next / norm
    step = direction[...]
    fresh = residual[...] - alpha * unfold(image[...], cands)
    out_s[...] = solution[...] + alpha * step
    out_r[...] = fresh
    out_d[...] = fresh + beta * step


def per_device(devices, points, lengthscale, noise, solution, residual, direction):
    hi, lo = split_sizes(devices)
    size, dims = points.shape
    cands = direction.shape[0]
    tall = cands * size // dims
    extra = -(-(8 + cands) // 16) * 16 * size // dims

    def meet(x, mask, core=None):
        pairs = [(d, d ^ mask) for d in range(devices) if core in (None, d % 2)]
        return lax.ppermute(x, "blk", pairs)

    vmem = pl.BlockSpec(memory_space=pltpu.VMEM)
    hbm = pl.BlockSpec(memory_space=pltpu.HBM)
    params = pltpu.CompilerParams(vmem_limit_bytes=50 * 1024 * 1024)

    packed, own, rates = pl.pallas_call(
        pack_kernel,
        out_shape=(
            jax.ShapeDtypeStruct((size + extra, dims), jnp.bfloat16),
            jax.ShapeDtypeStruct((3 * tall, dims), jnp.float32),
            jax.ShapeDtypeStruct((8 * cands, dims), jnp.float32),
        ),
        in_specs=[hbm] * 5,
        out_specs=(vmem,) * 3,
        scratch_shapes=[
            pltpu.VMEM((cands, size), jnp.float32),
            pltpu.VMEM((cands, size), jnp.float32),
            pltpu.SMEM((cands,), jnp.float32),
            pltpu.SMEM((cands,), jnp.float32),
            pltpu.SemaphoreType.DMA((5,)),
        ],
        compiler_params=params,
        name="pack",
    )(
        *(
            pltpu.with_memory_space_constraint(x, pltpu.HBM)
            for x in (points, direction, residual, lengthscale, noise)
        )
    )

    rows = [meet(points, k) for k in range(1, lo)]

    cols = [packed] + [meet(packed, k * lo) for k in range(1, hi)]
    partial = pl.pallas_call(
        functools.partial(product_kernel, lo, hi, cands),
        out_shape=jax.ShapeDtypeStruct(((lo + 2) * tall, dims), jnp.float32),
        in_specs=[vmem] * (hi + lo + 1),
        out_specs=vmem,
        scratch_shapes=[
            pltpu.VMEM((lo * size, 2 * dims), jnp.bfloat16),
            pltpu.VMEM((cands, hi * size, dims), jnp.float32),
            pltpu.VMEM((hi * size, lo * size), jnp.float32),
        ],
        compiler_params=params,
        name="product",
    )(*cols, *rows, own, rates)

    image, sums = pl.pallas_call(
        functools.partial(sums_kernel, cands),
        out_shape=(
            jax.ShapeDtypeStruct((tall, dims), jnp.float32),
            jax.ShapeDtypeStruct((4 * cands, dims), jnp.float32),
        ),
        in_specs=[vmem] * lo,
        out_specs=(vmem, vmem),
        compiler_params=params,
        name="sums",
    )(partial, *(meet(partial, k) for k in range(1, lo)))

    others = pl.pallas_call(
        add_kernel,
        out_shape=jax.ShapeDtypeStruct(sums.shape, jnp.float32),
        in_specs=[vmem] * (hi - 1),
        out_specs=vmem,
        compiler_params=params,
        name="others",
    )(*(meet(sums, k * lo, int(2 * k >= hi)) for k in range(1, hi)))

    return pl.pallas_call(
        update_kernel,
        out_shape=(jax.ShapeDtypeStruct((cands, size), jnp.float32),) * 3,
        in_specs=[vmem] * 7,
        out_specs=(vmem,) * 3,
        compiler_params=params,
        name="update",
    )(sums, others, meet(others, 1), image, solution, residual, direction)


def solution(mesh):
    split = P(None, ("groups", "blk"))
    return jax.shard_map(
        functools.partial(per_device, mesh.shape["blk"]),
        mesh=mesh,
        in_specs=(P(("groups", "blk"), None), P("groups"), P("groups"), split, split, split),
        out_specs=(split, split, split),
        check_vma=False,
    )
```

```python
import functools

import jax
import jax.numpy as jnp
from jax import lax
from jax.experimental import pallas as pl
from jax.experimental.pallas import tpu as pltpu
from jax.sharding import PartitionSpec as P

CHUNK = 32


def split_masks(devices):
    bits = devices.bit_length() - 1
    assert devices == 1 << bits and bits > 1
    far = bits // 2 - 1
    row = [m << (bits - far) for m in range(1 << far)]
    col = [m << 1 for m in range(1 << (bits - 1 - far))]
    return col, [m + core for m in row for core in (0, 1)]


def pieces_of(wide):
    high = wide.astype(jnp.bfloat16).astype(jnp.float32)
    middle = (wide - high).astype(jnp.bfloat16).astype(jnp.float32)
    return [high, middle, wide - high - middle]


def fold(wide, dims):
    return jnp.concatenate(
        [wide[:, p : p + dims] for p in range(0, wide.shape[1], dims)], axis=0
    )


def unfold(tall, n):
    return jnp.concatenate(
        [tall[p : p + n] for p in range(0, tall.shape[0], n)], axis=1
    )


def squares(points):
    wide = points.astype(jnp.float32)
    wide = wide * wide
    high = wide.astype(jnp.bfloat16)
    low = (wide - high.astype(jnp.float32)).astype(jnp.bfloat16)
    ones = jnp.ones((8, points.shape[1]), jnp.bfloat16)
    sums = [
        lax.dot_general(
            ones, half, (((1,), (1,)), ((), ())), preferred_element_type=jnp.float32
        )
        for half in (high, low)
    ]
    return (sums[0] + sums[1])[:1]


def pack_kernel(points, direction, residual, length, noise, packed, own, rates, *scratch):
    step_in, rest_in, length_in, noise_in, sems = scratch
    size, dims = points.shape
    cands = direction.shape[0]
    lines = (packed.shape[0] - size) * dims // size
    copies = [
        pltpu.make_async_copy(source, target, sems.at[i])
        for i, (source, target) in enumerate(
            (
                (points, packed.at[pl.ds(0, size), :]),
                (direction, step_in),
                (residual, rest_in),
                (length, length_in),
                (noise, noise_in),
            )
        )
    ]
    for copy in copies:
        copy.start()
    for copy in copies[1:]:
        copy.wait()
    step = step_in[...]
    which = lax.broadcasted_iota(jnp.int32, (cands, 1), 0)
    sigma = jnp.zeros((cands, 1), jnp.float32)
    for c in range(cands):
        sigma = jnp.where(which == c, noise_in[c], sigma)
        rate = -0.5 / (length_in[c] * length_in[c])
        rates[pl.ds(8 * c, 8), :] = jnp.full((8, dims), rate, jnp.float32)
    tall = own.shape[0] // 3
    for i, wide in enumerate((step, rest_in[...], sigma * step)):
        own[pl.ds(i * tall, tall), :] = fold(wide, dims)
    copies[0].wait()
    sq = squares(packed[:size, :])
    top = [*pieces_of(sq), jnp.ones((3, size), jnp.float32), jnp.zeros((2, size), jnp.float32)]
    top += [step, jnp.zeros((lines - 8 - cands, size), jnp.float32)]
    top = jnp.concatenate([t for t in top if t.shape[0]], axis=0)
    packed[size:, :] = fold(top, dims).astype(jnp.bfloat16)


def widen_row(points):
    wide = points.astype(jnp.float32)
    sq = pieces_of(jnp.sum(wide * wide, axis=1, keepdims=True))
    lane = lax.broadcasted_iota(jnp.int32, wide.shape, 1)
    extra = jnp.where(lane < 3, 1.0, 0.0)
    for i, piece in enumerate(sq):
        extra = jnp.where(lane == 3 + i, piece, extra)
    return jnp.concatenate(
        [(wide * -2.0).astype(jnp.bfloat16), extra.astype(jnp.bfloat16)], axis=1
    )


def product_kernel(lo, hi, cands, *refs):
    cols, refs = refs[:hi], refs[hi:]
    rows, refs = refs[: lo - 1], refs[lo - 1 :]
    own, rates, out, row_wide, weights, dist = refs
    rows = (cols[0], *rows)
    tall, dims = own.shape[0] // 3, own.shape[1]
    size = row_wide.shape[0] // lo
    wide = size // dims
    lines = (cols[0].shape[0] - size) // wide
    for k in range(lo):
        row_wide[pl.ds(k * size, size), :] = widen_row(rows[k][:size, :])
    for h in range(hi):
        top = unfold(cols[h][size:, :], lines)
        top = jnp.concatenate(
            [top, jnp.zeros((dims - lines, size), top.dtype)], axis=0
        ).T
        steps = top.astype(jnp.float32)
        for c in range(cands):
            weights[c, pl.ds(h * size, size), :] = jnp.broadcast_to(
                steps[:, 8 + c : 9 + c], (size, dims)
            )
        dist[pl.ds(h * size, size), :] = lax.dot_general(
            jnp.concatenate([cols[h][:size, :], top], axis=1),
            row_wide[...],
            (((1,), (1,)), ((), ())),
            preferred_element_type=jnp.float32,
        )
    rate = [
        jnp.concatenate([rates[pl.ds(8 * c, 8), :]] * wide, axis=1) for c in range(cands)
    ]

    def body(step, total):
        total = list(total)
        for j in range(0, CHUNK, 8):
            at = pl.ds(pl.multiple_of(step * CHUNK + j, 8), 8)
            weight = [
                jnp.concatenate([weights[c, at, :]] * wide, axis=1) for c in range(cands)
            ]
            for k in range(lo):
                here = dist[at, pl.ds(k * size, size)]
                for c in range(cands):
                    total[k * cands + c] += jnp.exp(here * rate[c]) * weight[c]
        return tuple(total)

    total = lax.fori_loop(
        0,
        hi * size // CHUNK,
        body,
        (jnp.zeros((8, size), jnp.float32),) * (lo * cands),
    )
    total = [jnp.sum(t, axis=0, keepdims=True) for t in total]
    for k in range(lo):
        part = fold(jnp.concatenate(total[k * cands : (k + 1) * cands], axis=0), dims)
        if k == 0:
            part += own[pl.ds(2 * tall, tall), :]
        out[pl.ds(k * tall, tall), :] = part
    out[pl.ds(lo * tall, 2 * tall), :] = own[pl.ds(0, 2 * tall), :]


def sums_kernel(cands, *refs):
    *parts, image_out, sums_out = refs
    lo = len(parts)
    tall, dims = image_out.shape
    sums = [jnp.zeros((tall, dims), jnp.float32)] * 4
    for k in range(lo):
        step = parts[k][pl.ds(lo * tall, tall), :]
        rest = parts[k][pl.ds((lo + 1) * tall, tall), :]
        image = parts[0][pl.ds(k * tall, tall), :]
        for m in range(1, lo):
            image = image + parts[m][pl.ds((k ^ m) * tall, tall), :]
        if k == 0:
            image_out[...] = image
        terms = (rest * rest, step * image, rest * image, image * image)
        sums = [s + t for s, t in zip(sums, terms)]
    for i, s in enumerate(sums):
        sums_out[pl.ds(i * cands, cands), :] = sum(
            s[p : p + cands] for p in range(0, tall, cands)
        )


def update_kernel(hi, *refs):
    sums, refs = refs[:hi], refs[hi:]
    image, solution, residual, direction, out_s, out_r, out_d = refs
    cands = solution.shape[0]
    total = sums[0][...]
    for h in range(1, hi):
        total = total + sums[h][...]
    total = jnp.sum(total, axis=1, keepdims=True)
    norm, curve, cross, square = (
        total[i * cands : (i + 1) * cands] for i in range(4)
    )
    alpha = norm / curve
    norm_next = norm - 2.0 * alpha * cross + alpha * (alpha * square)
    beta = norm_next / norm
    step = direction[...]
    fresh = residual[...] - alpha * unfold(image[...], cands)
    out_s[...] = solution[...] + alpha * step
    out_r[...] = fresh
    out_d[...] = fresh + beta * step


def per_device(devices, points, lengthscale, noise, solution, residual, direction):
    col_masks, row_masks = split_masks(devices)
    hi, lo = len(col_masks), len(row_masks)
    size, dims = points.shape
    cands = direction.shape[0]
    tall = cands * size // dims
    extra = -(-(8 + cands) // 16) * 16 * size // dims

    def meet(x, mask):
        return lax.ppermute(x, "blk", [(d, d ^ mask) for d in range(devices)])

    vmem = pl.BlockSpec(memory_space=pltpu.VMEM)
    hbm = pl.BlockSpec(memory_space=pltpu.HBM)
    params = pltpu.CompilerParams(vmem_limit_bytes=50 * 1024 * 1024)

    packed, own, rates = pl.pallas_call(
        pack_kernel,
        out_shape=(
            jax.ShapeDtypeStruct((size + extra, dims), jnp.bfloat16),
            jax.ShapeDtypeStruct((3 * tall, dims), jnp.float32),
            jax.ShapeDtypeStruct((8 * cands, dims), jnp.float32),
        ),
        in_specs=[hbm] * 5,
        out_specs=(vmem,) * 3,
        scratch_shapes=[
            pltpu.VMEM((cands, size), jnp.float32),
            pltpu.VMEM((cands, size), jnp.float32),
            pltpu.SMEM((cands,), jnp.float32),
            pltpu.SMEM((cands,), jnp.float32),
            pltpu.SemaphoreType.DMA((5,)),
        ],
        compiler_params=params,
        name="pack",
    )(
        *(
            pltpu.with_memory_space_constraint(x, pltpu.HBM)
            for x in (points, direction, residual, lengthscale, noise)
        )
    )

    rows = [points]
    for mask in row_masks[1:]:
        rows.append(meet(rows[-1], 1) if mask % 2 else meet(points, mask))
    cols = [packed] + [meet(packed, mask) for mask in col_masks[1:]]

    partial = pl.pallas_call(
        functools.partial(product_kernel, lo, hi, cands),
        out_shape=jax.ShapeDtypeStruct(((lo + 2) * tall, dims), jnp.float32),
        in_specs=[vmem] * (hi + lo + 1),
        out_specs=vmem,
        scratch_shapes=[
            pltpu.VMEM((lo * size, 2 * dims), jnp.bfloat16),
            pltpu.VMEM((cands, hi * size, dims), jnp.float32),
            pltpu.VMEM((hi * size, lo * size), jnp.float32),
        ],
        compiler_params=params,
        name="product",
    )(*cols, *rows[1:], own, rates)

    image, sums = pl.pallas_call(
        functools.partial(sums_kernel, cands),
        out_shape=(
            jax.ShapeDtypeStruct((tall, dims), jnp.float32),
            jax.ShapeDtypeStruct((4 * cands, dims), jnp.float32),
        ),
        in_specs=[vmem] * lo,
        out_specs=(vmem, vmem),
        compiler_params=params,
        name="sums",
    )(partial, *(meet(partial, mask) for mask in row_masks[1:]))

    return pl.pallas_call(
        functools.partial(update_kernel, hi),
        out_shape=(jax.ShapeDtypeStruct((cands, size), jnp.float32),) * 3,
        in_specs=[vmem] * (hi + 4),
        out_specs=(vmem,) * 3,
        compiler_params=params,
        name="update",
    )(sums, *(meet(sums, mask) for mask in col_masks[1:]), image, solution, residual, direction)


def solution(mesh):
    split = P(None, ("groups", "blk"))
    return jax.shard_map(
        functools.partial(per_device, mesh.shape["blk"]),
        mesh=mesh,
        in_specs=(P(("groups", "blk"), None), P("groups"), P("groups"), split, split, split),
        out_specs=(split, split, split),
        check_vma=False,
    )
```

```python
import functools

import jax
import jax.numpy as jnp
from jax import lax
from jax.experimental import pallas as pl
from jax.experimental.pallas import tpu as pltpu
from jax.sharding import PartitionSpec as P

CHUNK = 128


def split_masks(devices):
    bits = devices.bit_length() - 1
    assert devices == 1 << bits and bits > 1
    far = bits // 2 - 1
    row = [m << (bits - far) for m in range(1 << far)]
    col = [m << 1 for m in range(1 << (bits - 1 - far))]
    return col, [m + core for m in row for core in (0, 1)]


def pieces_of(wide):
    high = wide.astype(jnp.bfloat16).astype(jnp.float32)
    middle = (wide - high).astype(jnp.bfloat16).astype(jnp.float32)
    return [high, middle, wide - high - middle]


def fold(wide, dims):
    return jnp.concatenate(
        [wide[:, p : p + dims] for p in range(0, wide.shape[1], dims)], axis=0
    )


def unfold(tall, n):
    return jnp.concatenate(
        [tall[p : p + n] for p in range(0, tall.shape[0], n)], axis=1
    )


def squares(points):
    wide = points.astype(jnp.float32)
    wide = wide * wide
    high = wide.astype(jnp.bfloat16)
    low = (wide - high.astype(jnp.float32)).astype(jnp.bfloat16)
    ones = jnp.ones((8, points.shape[1]), jnp.bfloat16)
    sums = [
        lax.dot_general(
            ones, half, (((1,), (1,)), ((), ())), preferred_element_type=jnp.float32
        )
        for half in (high, low)
    ]
    return (sums[0] + sums[1])[:1]


def pack_kernel(points, direction, residual, length, noise, packed, own, rates, *scratch):
    step_in, rest_in, length_in, noise_in, sems = scratch
    size, dims = points.shape
    cands = direction.shape[0]
    lines = (packed.shape[0] - size) * dims // size
    copies = [
        pltpu.make_async_copy(source, target, sems.at[i])
        for i, (source, target) in enumerate(
            (
                (points, packed.at[pl.ds(0, size), :]),
                (direction, step_in),
                (residual, rest_in),
                (length, length_in),
                (noise, noise_in),
            )
        )
    ]
    for copy in copies:
        copy.start()
    for copy in copies[1:]:
        copy.wait()
    step = step_in[...]
    which = lax.broadcasted_iota(jnp.int32, (cands, 1), 0)
    sigma = jnp.zeros((cands, 1), jnp.float32)
    for c in range(cands):
        sigma = jnp.where(which == c, noise_in[c], sigma)
        rate = -0.5 / (length_in[c] * length_in[c])
        rates[pl.ds(8 * c, 8), :] = jnp.full((8, dims), rate, jnp.float32)
    tall = own.shape[0] // 3
    for i, wide in enumerate((step, rest_in[...], sigma * step)):
        own[pl.ds(i * tall, tall), :] = fold(wide, dims)
    copies[0].wait()
    sq = squares(packed[:size, :])
    top = [*pieces_of(sq), jnp.ones((3, size), jnp.float32), jnp.zeros((2, size), jnp.float32)]
    top += [step, jnp.zeros((lines - 8 - cands, size), jnp.float32)]
    top = jnp.concatenate([t for t in top if t.shape[0]], axis=0)
    packed[size:, :] = fold(top, dims).astype(jnp.bfloat16)


def widen_row(points):
    wide = points.astype(jnp.float32)
    sq = pieces_of(jnp.sum(wide * wide, axis=1, keepdims=True))
    lane = lax.broadcasted_iota(jnp.int32, wide.shape, 1)
    extra = jnp.where(lane < 3, 1.0, 0.0)
    for i, piece in enumerate(sq):
        extra = jnp.where(lane == 3 + i, piece, extra)
    return jnp.concatenate(
        [(wide * -2.0).astype(jnp.bfloat16), extra.astype(jnp.bfloat16)], axis=1
    )


def add_column(col, row_wide, rates, weights, dist, lo):
    dims = col.shape[1]
    cands = rates.shape[0] // 8
    size = row_wide.shape[0] // lo
    wide = size // dims
    lines = (col.shape[0] - size) // wide
    top = unfold(col[size:, :], lines)
    top = jnp.concatenate([top, jnp.zeros((dims - lines, size), top.dtype)], axis=0).T
    steps = top.astype(jnp.float32)
    for c in range(cands):
        weights[c] = jnp.broadcast_to(steps[:, 8 + c : 9 + c], (size, dims))
    dist[...] = lax.dot_general(
        jnp.concatenate([col[:size, :], top], axis=1),
        row_wide[...],
        (((1,), (1,)), ((), ())),
        preferred_element_type=jnp.float32,
    )
    rate = [
        jnp.concatenate([rates[pl.ds(8 * c, 8), :]] * wide, axis=1) for c in range(cands)
    ]

    def body(step, total):
        total = list(total)
        for j in range(0, CHUNK, 8):
            at = pl.ds(pl.multiple_of(step * CHUNK + j, 8), 8)
            weight = [
                jnp.concatenate([weights[c, at, :]] * wide, axis=1) for c in range(cands)
            ]
            for k in range(lo):
                here = dist[at, pl.ds(k * size, size)]
                for c in range(cands):
                    total[k * cands + c] += jnp.exp(here * rate[c]) * weight[c]
        return tuple(total)

    total = lax.fori_loop(
        0,
        size // CHUNK,
        body,
        (jnp.zeros((8, size), jnp.float32),) * (lo * cands),
    )
    total = [jnp.sum(t, axis=0, keepdims=True) for t in total]
    return [
        fold(jnp.concatenate(total[k * cands : (k + 1) * cands], axis=0), dims)
        for k in range(lo)
    ]


def first_kernel(lo, col, *refs):
    rows, refs = refs[: lo - 1], refs[lo - 1 :]
    own, rates, out, row_wide, weights, dist = refs
    tall = own.shape[0] // 3
    size = row_wide.shape[0] // lo
    for k, block in enumerate((col, *rows)):
        row_wide[pl.ds(k * size, size), :] = widen_row(block[:size, :])
    parts = add_column(col, row_wide, rates, weights, dist, lo)
    parts[0] += own[pl.ds(2 * tall, tall), :]
    for k in range(lo):
        out[pl.ds(k * tall, tall), :] = parts[k]
    out[pl.ds(lo * tall, 2 * tall), :] = own[pl.ds(0, 2 * tall), :]


def next_kernel(lo, col, row_wide, rates, before, out, weights, dist):
    tall = before.shape[0] // (lo + 2)
    parts = add_column(col, row_wide, rates, weights, dist, lo)
    for k in range(lo):
        at = pl.ds(k * tall, tall)
        out[at, :] = before[at, :] + parts[k]
    at = pl.ds(lo * tall, 2 * tall)
    out[at, :] = before[at, :]


def sums_kernel(cands, *refs):
    *parts, image_out, sums_out = refs
    lo = len(parts)
    tall, dims = image_out.shape
    sums = [jnp.zeros((tall, dims), jnp.float32)] * 4
    for k in range(lo):
        step = parts[k][pl.ds(lo * tall, tall), :]
        rest = parts[k][pl.ds((lo + 1) * tall, tall), :]
        image = parts[0][pl.ds(k * tall, tall), :]
        for m in range(1, lo):
            image = image + parts[m][pl.ds((k ^ m) * tall, tall), :]
        if k == 0:
            image_out[...] = image
        terms = (rest * rest, step * image, rest * image, image * image)
        sums = [s + t for s, t in zip(sums, terms)]
    for i, s in enumerate(sums):
        sums_out[pl.ds(i * cands, cands), :] = sum(
            s[p : p + cands] for p in range(0, tall, cands)
        )


def update_kernel(hi, *refs):
    sums, refs = refs[:hi], refs[hi:]
    image, solution, residual, direction, out_s, out_r, out_d = refs
    cands = solution.shape[0]
    total = sums[0][...]
    for h in range(1, hi):
        total = total + sums[h][...]
    total = jnp.sum(total, axis=1, keepdims=True)
    norm, curve, cross, square = (
        total[i * cands : (i + 1) * cands] for i in range(4)
    )
    alpha = norm / curve
    norm_next = norm - 2.0 * alpha * cross + alpha * (alpha * square)
    beta = norm_next / norm
    step = direction[...]
    fresh = residual[...] - alpha * unfold(image[...], cands)
    out_s[...] = solution[...] + alpha * step
    out_r[...] = fresh
    out_d[...] = fresh + beta * step


def per_device(devices, points, lengthscale, noise, solution, residual, direction):
    col_masks, row_masks = split_masks(devices)
    hi, lo = len(col_masks), len(row_masks)
    size, dims = points.shape
    cands = direction.shape[0]
    tall = cands * size // dims
    extra = -(-(8 + cands) // 16) * 16 * size // dims

    def meet(x, mask):
        return lax.ppermute(x, "blk", [(d, d ^ mask) for d in range(devices)])

    vmem = pl.BlockSpec(memory_space=pltpu.VMEM)
    hbm = pl.BlockSpec(memory_space=pltpu.HBM)
    params = pltpu.CompilerParams(vmem_limit_bytes=50 * 1024 * 1024)

    packed, own, rates = pl.pallas_call(
        pack_kernel,
        out_shape=(
            jax.ShapeDtypeStruct((size + extra, dims), jnp.bfloat16),
            jax.ShapeDtypeStruct((3 * tall, dims), jnp.float32),
            jax.ShapeDtypeStruct((8 * cands, dims), jnp.float32),
        ),
        in_specs=[hbm] * 5,
        out_specs=(vmem,) * 3,
        scratch_shapes=[
            pltpu.VMEM((cands, size), jnp.float32),
            pltpu.VMEM((cands, size), jnp.float32),
            pltpu.SMEM((cands,), jnp.float32),
            pltpu.SMEM((cands,), jnp.float32),
            pltpu.SemaphoreType.DMA((5,)),
        ],
        compiler_params=params,
        name="pack",
    )(
        *(
            pltpu.with_memory_space_constraint(x, pltpu.HBM)
            for x in (points, direction, residual, lengthscale, noise)
        )
    )

    rows = [points]
    for mask in row_masks[1:]:
        rows.append(meet(rows[-1], 1) if mask % 2 else meet(points, mask))
    spare = [
        pltpu.VMEM((cands, size, dims), jnp.float32),
        pltpu.VMEM((size, lo * size), jnp.float32),
    ]
    result = jax.ShapeDtypeStruct(((lo + 2) * tall, dims), jnp.float32)
    partial, row_wide = pl.pallas_call(
        functools.partial(first_kernel, lo),
        out_shape=(result, jax.ShapeDtypeStruct((lo * size, 2 * dims), jnp.bfloat16)),
        in_specs=[vmem] * (lo + 2),
        out_specs=(vmem, vmem),
        scratch_shapes=spare,
        compiler_params=params,
        name="product_0",
    )(packed, *rows[1:], own, rates)
    for mask in reversed(col_masks[1:]):
        partial = pl.pallas_call(
            functools.partial(next_kernel, lo),
            out_shape=result,
            in_specs=[vmem] * 4,
            out_specs=vmem,
            scratch_shapes=spare,
            compiler_params=params,
            name="product_%d" % mask,
        )(meet(packed, mask), row_wide, rates, partial)

    image, sums = pl.pallas_call(
        functools.partial(sums_kernel, cands),
        out_shape=(
            jax.ShapeDtypeStruct((tall, dims), jnp.float32),
            jax.ShapeDtypeStruct((4 * cands, dims), jnp.float32),
        ),
        in_specs=[vmem] * lo,
        out_specs=(vmem, vmem),
        compiler_params=params,
        name="sums",
    )(partial, *(meet(partial, mask) for mask in row_masks[1:]))

    return pl.pallas_call(
        functools.partial(update_kernel, hi),
        out_shape=(jax.ShapeDtypeStruct((cands, size), jnp.float32),) * 3,
        in_specs=[vmem] * (hi + 4),
        out_specs=(vmem,) * 3,
        compiler_params=params,
        name="update",
    )(sums, *(meet(sums, mask) for mask in col_masks[1:]), image, solution, residual, direction)


def solution(mesh):
    split = P(None, ("groups", "blk"))
    return jax.shard_map(
        functools.partial(per_device, mesh.shape["blk"]),
        mesh=mesh,
        in_specs=(P(("groups", "blk"), None), P("groups"), P("groups"), split, split, split),
        out_specs=(split, split, split),
        check_vma=False,
    )
```

```python
import functools

import jax
import jax.numpy as jnp
from jax import lax
from jax.experimental import pallas as pl
from jax.experimental.pallas import tpu as pltpu
from jax.sharding import PartitionSpec as P

CHUNK = 128


def split_masks(devices):
    bits = devices.bit_length() - 1
    assert devices == 1 << bits and bits > 1
    far = bits // 2 - 1
    row = [m << (bits - far) for m in range(1 << far)]
    col = [m << 1 for m in range(1 << (bits - 1 - far))]
    return col, [m + core for m in row for core in (0, 1)]


def pieces_of(wide):
    high = wide.astype(jnp.bfloat16).astype(jnp.float32)
    middle = (wide - high).astype(jnp.bfloat16).astype(jnp.float32)
    return [high, middle, wide - high - middle]


def fold(wide, dims):
    return jnp.concatenate(
        [wide[:, p : p + dims] for p in range(0, wide.shape[1], dims)], axis=0
    )


def unfold(tall, n):
    return jnp.concatenate(
        [tall[p : p + n] for p in range(0, tall.shape[0], n)], axis=1
    )


def squares(points):
    wide = points.astype(jnp.float32)
    wide = wide * wide
    high = wide.astype(jnp.bfloat16)
    low = (wide - high.astype(jnp.float32)).astype(jnp.bfloat16)
    ones = jnp.ones((8, points.shape[1]), jnp.bfloat16)
    sums = [
        lax.dot_general(
            ones, half, (((1,), (1,)), ((), ())), preferred_element_type=jnp.float32
        )
        for half in (high, low)
    ]
    return (sums[0] + sums[1])[:1]


def pack_kernel(points, direction, residual, length, noise, packed, own, rates, *scratch):
    step_in, rest_in, length_in, noise_in, sems = scratch
    size, dims = points.shape
    cands = direction.shape[0]
    lines = (packed.shape[0] - size) * dims // size
    copies = [
        pltpu.make_async_copy(source, target, sems.at[i])
        for i, (source, target) in enumerate(
            (
                (points, packed.at[pl.ds(0, size), :]),
                (direction, step_in),
                (residual, rest_in),
                (length, length_in),
                (noise, noise_in),
            )
        )
    ]
    for copy in copies:
        copy.start()
    for copy in copies[1:]:
        copy.wait()
    step = step_in[...]
    which = lax.broadcasted_iota(jnp.int32, (cands, 1), 0)
    sigma = jnp.zeros((cands, 1), jnp.float32)
    for c in range(cands):
        sigma = jnp.where(which == c, noise_in[c], sigma)
        rate = -0.5 / (length_in[c] * length_in[c])
        rates[pl.ds(8 * c, 8), :] = jnp.full((8, dims), rate, jnp.float32)
    tall = own.shape[0] // 3
    for i, wide in enumerate((step, rest_in[...], sigma * step)):
        own[pl.ds(i * tall, tall), :] = fold(wide, dims)
    copies[0].wait()
    sq = squares(packed[:size, :])
    top = [*pieces_of(sq), jnp.ones((3, size), jnp.float32), jnp.zeros((2, size), jnp.float32)]
    top += [step, jnp.zeros((lines - 8 - cands, size), jnp.float32)]
    top = jnp.concatenate([t for t in top if t.shape[0]], axis=0)
    packed[size:, :] = fold(top, dims).astype(jnp.bfloat16)


def widen_row(points):
    wide = points.astype(jnp.float32)
    sq = pieces_of(jnp.sum(wide * wide, axis=1, keepdims=True))
    lane = lax.broadcasted_iota(jnp.int32, wide.shape, 1)
    extra = jnp.where(lane < 3, 1.0, 0.0)
    for i, piece in enumerate(sq):
        extra = jnp.where(lane == 3 + i, piece, extra)
    return jnp.concatenate(
        [(wide * -2.0).astype(jnp.bfloat16), extra.astype(jnp.bfloat16)], axis=1
    )


def add_columns(cols, row_wide, rates, weights, dist, lo):
    dims = cols[0].shape[1]
    cands = rates.shape[0] // 8
    size = row_wide.shape[0] // lo
    wide = size // dims
    lines = (cols[0].shape[0] - size) // wide
    for h, col in enumerate(cols):
        at = pl.ds(h * size, size)
        top = unfold(col[size:, :], lines)
        top = jnp.concatenate(
            [top, jnp.zeros((dims - lines, size), top.dtype)], axis=0
        ).T
        steps = top.astype(jnp.float32)
        for c in range(cands):
            weights[c, at, :] = jnp.broadcast_to(steps[:, 8 + c : 9 + c], (size, dims))
        dist[at, :] = lax.dot_general(
            jnp.concatenate([col[:size, :], top], axis=1),
            row_wide[...],
            (((1,), (1,)), ((), ())),
            preferred_element_type=jnp.float32,
        )
    rate = [
        jnp.concatenate([rates[pl.ds(8 * c, 8), :]] * wide, axis=1) for c in range(cands)
    ]

    def body(step, total):
        total = list(total)
        for j in range(0, CHUNK, 8):
            at = pl.ds(pl.multiple_of(step * CHUNK + j, 8), 8)
            weight = [
                jnp.concatenate([weights[c, at, :]] * wide, axis=1) for c in range(cands)
            ]
            for k in range(lo):
                here = dist[at, pl.ds(k * size, size)]
                for c in range(cands):
                    total[k * cands + c] += jnp.exp(here * rate[c]) * weight[c]
        return tuple(total)

    total = lax.fori_loop(
        0,
        len(cols) * size // CHUNK,
        body,
        (jnp.zeros((8, size), jnp.float32),) * (lo * cands),
    )
    total = [jnp.sum(t, axis=0, keepdims=True) for t in total]
    return [
        fold(jnp.concatenate(total[k * cands : (k + 1) * cands], axis=0), dims)
        for k in range(lo)
    ]


def first_kernel(lo, col, *refs):
    rows, refs = refs[: lo - 1], refs[lo - 1 :]
    own, rates, out, row_wide, weights, dist = refs
    tall = own.shape[0] // 3
    size = row_wide.shape[0] // lo
    for k, block in enumerate((col, *rows)):
        row_wide[pl.ds(k * size, size), :] = widen_row(block[:size, :])
    parts = add_columns([col], row_wide, rates, weights, dist, lo)
    parts[0] += own[pl.ds(2 * tall, tall), :]
    for k in range(lo):
        out[pl.ds(k * tall, tall), :] = parts[k]
    out[pl.ds(lo * tall, 2 * tall), :] = own[pl.ds(0, 2 * tall), :]


def rest_kernel(lo, *refs):
    *cols, row_wide, rates, before, out, weights, dist = refs
    tall = before.shape[0] // (lo + 2)
    parts = add_columns(cols, row_wide, rates, weights, dist, lo)
    for k in range(lo):
        at = pl.ds(k * tall, tall)
        out[at, :] = before[at, :] + parts[k]
    at = pl.ds(lo * tall, 2 * tall)
    out[at, :] = before[at, :]


def merge_kernel(lo, *refs):
    *parts, out = refs
    tall = parts[0].shape[0] // (lo + 2)
    for k in range(lo):
        total = parts[0][pl.ds(k * tall, tall), :]
        for m in range(1, len(parts)):
            total = total + parts[m][pl.ds((k ^ (2 * m)) * tall, tall), :]
        out[pl.ds(k * tall, tall), :] = total
    for m, part in enumerate(parts):
        out[pl.ds((lo + 2 * m) * tall, 2 * tall), :] = part[pl.ds(lo * tall, 2 * tall), :]


def sums_kernel(lo, cands, mine, other, image_out, sums_out):
    tall, dims = image_out.shape
    sums = [jnp.zeros((tall, dims), jnp.float32)] * 4
    for k in range(lo):
        holder = other if k % 2 else mine
        base = lo + 2 * (k // 2)
        step = holder[pl.ds(base * tall, tall), :]
        rest = holder[pl.ds((base + 1) * tall, tall), :]
        image = mine[pl.ds(k * tall, tall), :] + other[pl.ds((k ^ 1) * tall, tall), :]
        if k == 0:
            image_out[...] = image
        terms = (rest * rest, step * image, rest * image, image * image)
        sums = [s + t for s, t in zip(sums, terms)]
    for i, s in enumerate(sums):
        sums_out[pl.ds(i * cands, cands), :] = sum(
            s[p : p + cands] for p in range(0, tall, cands)
        )


def update_kernel(*refs):
    *sums, image, solution, residual, direction, out_s, out_r, out_d = refs
    cands = solution.shape[0]
    total = sums[0][...]
    for part in sums[1:]:
        total = total + part[...]
    total = jnp.sum(total, axis=1, keepdims=True)
    norm, curve, cross, square = (
        total[i * cands : (i + 1) * cands] for i in range(4)
    )
    alpha = norm / curve
    norm_next = norm - 2.0 * alpha * cross + alpha * (alpha * square)
    beta = norm_next / norm
    step = direction[...]
    fresh = residual[...] - alpha * unfold(image[...], cands)
    out_s[...] = solution[...] + alpha * step
    out_r[...] = fresh
    out_d[...] = fresh + beta * step


def per_device(devices, points, lengthscale, noise, solution, residual, direction):
    col_masks, row_masks = split_masks(devices)
    hi, lo = len(col_masks), len(row_masks)
    size, dims = points.shape
    cands = direction.shape[0]
    tall = cands * size // dims
    extra = -(-(8 + cands) // 16) * 16 * size // dims

    def meet(x, mask, odd_mask=None):
        masks = (mask, mask if odd_mask is None else odd_mask)
        return lax.ppermute(x, "blk", [(d, d ^ masks[d % 2]) for d in range(devices)])

    vmem = pl.BlockSpec(memory_space=pltpu.VMEM)
    hbm = pl.BlockSpec(memory_space=pltpu.HBM)
    params = pltpu.CompilerParams(vmem_limit_bytes=50 * 1024 * 1024)

    packed, own, rates = pl.pallas_call(
        pack_kernel,
        out_shape=(
            jax.ShapeDtypeStruct((size + extra, dims), jnp.bfloat16),
            jax.ShapeDtypeStruct((3 * tall, dims), jnp.float32),
            jax.ShapeDtypeStruct((8 * cands, dims), jnp.float32),
        ),
        in_specs=[hbm] * 5,
        out_specs=(vmem,) * 3,
        scratch_shapes=[
            pltpu.VMEM((cands, size), jnp.float32),
            pltpu.VMEM((cands, size), jnp.float32),
            pltpu.SMEM((cands,), jnp.float32),
            pltpu.SMEM((cands,), jnp.float32),
            pltpu.SemaphoreType.DMA((5,)),
        ],
        compiler_params=params,
        name="pack",
    )(
        *(
            pltpu.with_memory_space_constraint(x, pltpu.HBM)
            for x in (points, direction, residual, lengthscale, noise)
        )
    )

    rows = [points]
    for mask in row_masks[1:]:
        rows.append(meet(rows[-1], 1) if mask % 2 else meet(points, mask))
    def spare(count):
        return [
            pltpu.VMEM((cands, count * size, dims), jnp.float32),
            pltpu.VMEM((count * size, lo * size), jnp.float32),
        ]

    result = jax.ShapeDtypeStruct(((lo + 2) * tall, dims), jnp.float32)
    partial, row_wide = pl.pallas_call(
        functools.partial(first_kernel, lo),
        out_shape=(result, jax.ShapeDtypeStruct((lo * size, 2 * dims), jnp.bfloat16)),
        in_specs=[vmem] * (lo + 2),
        out_specs=(vmem, vmem),
        scratch_shapes=spare(1),
        compiler_params=params,
        name="product_own",
    )(packed, *rows[1:], own, rates)
    partial = pl.pallas_call(
        functools.partial(rest_kernel, lo),
        out_shape=result,
        in_specs=[vmem] * (hi + 2),
        out_specs=vmem,
        scratch_shapes=spare(hi - 1),
        compiler_params=params,
        name="product_rest",
    )(*(meet(packed, mask) for mask in col_masks[1:]), row_wide, rates, partial)

    merged = pl.pallas_call(
        functools.partial(merge_kernel, lo),
        out_shape=jax.ShapeDtypeStruct((2 * lo * tall, dims), jnp.float32),
        in_specs=[vmem] * (lo // 2),
        out_specs=vmem,
        compiler_params=params,
        name="merge",
    )(partial, *(meet(partial, mask) for mask in row_masks[2::2]))

    image, sums = pl.pallas_call(
        functools.partial(sums_kernel, lo, cands),
        out_shape=(
            jax.ShapeDtypeStruct((tall, dims), jnp.float32),
            jax.ShapeDtypeStruct((4 * cands, dims), jnp.float32),
        ),
        in_specs=[vmem] * 2,
        out_specs=(vmem, vmem),
        compiler_params=params,
        name="sums",
    )(merged, meet(merged, 1))

    shared = [
        meet(sums, even, odd) for even, odd in zip(col_masks[1:-1:2], col_masks[2:-1:2])
    ]
    shared += [meet(x, 1) for x in shared]
    parts = [sums, meet(sums, col_masks[-1]), *shared]

    return pl.pallas_call(
        update_kernel,
        out_shape=(jax.ShapeDtypeStruct((cands, size), jnp.float32),) * 3,
        in_specs=[vmem] * (len(parts) + 4),
        out_specs=(vmem,) * 3,
        compiler_params=params,
        name="update",
    )(*parts, image, solution, residual, direction)


def solution(mesh):
    split = P(None, ("groups", "blk"))
    return jax.shard_map(
        functools.partial(per_device, mesh.shape["blk"]),
        mesh=mesh,
        in_specs=(P(("groups", "blk"), None), P("groups"), P("groups"), split, split, split),
        out_specs=(split, split, split),
        check_vma=False,
    )
```

```python
import functools

import jax
import jax.numpy as jnp
from jax import lax
from jax.experimental import pallas as pl
from jax.experimental.pallas import tpu as pltpu
from jax.sharding import PartitionSpec as P

def split_masks(devices):
    bits = devices.bit_length() - 1
    assert devices == 1 << bits and bits > 1
    far = bits // 2 - 1
    row = [m << (bits - far) for m in range(1 << far)]
    col = [m << 1 for m in range(1 << (bits - 1 - far))]
    return col, [m + core for m in row for core in (0, 1)]


def pieces_of(wide):
    high = wide.astype(jnp.bfloat16).astype(jnp.float32)
    middle = (wide - high).astype(jnp.bfloat16).astype(jnp.float32)
    return [high, middle, wide - high - middle]


def fold(wide, dims):
    return jnp.concatenate(
        [wide[:, p : p + dims] for p in range(0, wide.shape[1], dims)], axis=0
    )


def unfold(tall, n):
    return jnp.concatenate(
        [tall[p : p + n] for p in range(0, tall.shape[0], n)], axis=1
    )


def squares(points):
    wide = points.astype(jnp.float32)
    wide = wide * wide
    high = wide.astype(jnp.bfloat16)
    low = (wide - high.astype(jnp.float32)).astype(jnp.bfloat16)
    ones = jnp.ones((8, points.shape[1]), jnp.bfloat16)
    sums = [
        lax.dot_general(
            ones, half, (((1,), (1,)), ((), ())), preferred_element_type=jnp.float32
        )
        for half in (high, low)
    ]
    return (sums[0] + sums[1])[:1]


def pack_kernel(points, direction, residual, length, noise, packed, own, rates, *scratch):
    step_in, rest_in, length_in, noise_in, sems = scratch
    size, dims = points.shape
    cands = direction.shape[0]
    lines = (packed.shape[0] - size) * dims // size
    copies = [
        pltpu.make_async_copy(source, target, sems.at[i])
        for i, (source, target) in enumerate(
            (
                (points, packed.at[pl.ds(0, size), :]),
                (direction, step_in),
                (residual, rest_in),
                (length, length_in),
                (noise, noise_in),
            )
        )
    ]
    for copy in copies:
        copy.start()
    for copy in copies[1:]:
        copy.wait()
    step = step_in[...]
    which = lax.broadcasted_iota(jnp.int32, (cands, 1), 0)
    sigma = jnp.zeros((cands, 1), jnp.float32)
    for c in range(cands):
        sigma = jnp.where(which == c, noise_in[c], sigma)
        rate = -0.5 / (length_in[c] * length_in[c])
        rates[pl.ds(8 * c, 8), :] = jnp.full((8, dims), rate, jnp.float32)
    tall = own.shape[0] // 3
    for i, wide in enumerate((step, rest_in[...], sigma * step)):
        own[pl.ds(i * tall, tall), :] = fold(wide, dims)
    copies[0].wait()
    sq = squares(packed[:size, :])
    top = [*pieces_of(sq), jnp.ones((3, size), jnp.float32), jnp.zeros((2, size), jnp.float32)]
    top += [step, jnp.zeros((lines - 8 - cands, size), jnp.float32)]
    top = jnp.concatenate([t for t in top if t.shape[0]], axis=0)
    packed[size:, :] = fold(top, dims).astype(jnp.bfloat16)


def widen_row(points):
    wide = points.astype(jnp.float32)
    sq = pieces_of(jnp.sum(wide * wide, axis=1, keepdims=True))
    lane = lax.broadcasted_iota(jnp.int32, wide.shape, 1)
    extra = jnp.where(lane < 3, 1.0, 0.0)
    for i, piece in enumerate(sq):
        extra = jnp.where(lane == 3 + i, piece, extra)
    return jnp.concatenate(
        [(wide * -2.0).astype(jnp.bfloat16), extra.astype(jnp.bfloat16)], axis=1
    )


def add_column(col, row_wide, rates, weights, dist, before, out, lo):
    dims = col.shape[1]
    cands = rates.shape[0] // 8
    size = row_wide.shape[0] // lo
    wide = size // dims
    lines = (col.shape[0] - size) // wide
    top = unfold(col[size:, :], lines)
    top = jnp.concatenate([top, jnp.zeros((dims - lines, size), top.dtype)], axis=0).T
    both = jnp.concatenate([col[:size, :], top], axis=1)
    steps = top.astype(jnp.float32)

    def distances(k):
        dist[k] = lax.dot_general(
            both,
            row_wide[pl.ds(k * size, size), :],
            (((1,), (1,)), ((), ())),
            preferred_element_type=jnp.float32,
        )

    distances(0)
    for c in range(cands):
        weights[c] = jnp.broadcast_to(steps[:, 8 + c : 9 + c], (size, dims))
    rate = [
        jnp.concatenate([rates[pl.ds(8 * c, 8), :]] * wide, axis=1) for c in range(cands)
    ]
    for k in range(lo):
        if k + 1 < lo:
            distances(k + 1)
        places = [pl.ds((k * cands + c) * 8, 8) for c in range(cands)]
        total = [0.0 if before is None else before[at, :] for at in places]
        for j in range(0, size, 8):
            here = dist[k, pl.ds(j, 8), :]
            for c in range(cands):
                weight = jnp.concatenate([weights[c, pl.ds(j, 8), :]] * wide, axis=1)
                total[c] = total[c] + jnp.exp(here * rate[c]) * weight
        for c in range(cands):
            out[places[c], :] = total[c]


def first_kernel(lo, col, *refs):
    rows, refs = refs[: lo - 1], refs[lo - 1 :]
    rates, out, row_wide, weights, dist = refs
    size = row_wide.shape[0] // lo
    for k, block in enumerate((col, *rows)):
        row_wide[pl.ds(k * size, size), :] = widen_row(block[:size, :])
    add_column(col, row_wide, rates, weights, dist, None, out, lo)


def next_kernel(lo, col, row_wide, rates, before, out, weights, dist):
    add_column(col, row_wide, rates, weights, dist, before, out, lo)


def last_kernel(lo, col, row_wide, rates, before, own, out, weights, dist, spread):
    add_column(col, row_wide, rates, weights, dist, before, spread, lo)
    tall, dims = own.shape[0] // 3, own.shape[1]
    cands = rates.shape[0] // 8
    for k in range(lo):
        part = [
            jnp.sum(spread[pl.ds((k * cands + c) * 8, 8), :], axis=0, keepdims=True)
            for c in range(cands)
        ]
        part = fold(jnp.concatenate(part, axis=0), dims)
        if k == 0:
            part += own[pl.ds(2 * tall, tall), :]
        out[pl.ds(k * tall, tall), :] = part
    out[pl.ds(lo * tall, 2 * tall), :] = own[pl.ds(0, 2 * tall), :]


def sums_kernel(cands, *refs):
    *parts, image_out, sums_out = refs
    lo = len(parts)
    tall, dims = image_out.shape
    sums = [jnp.zeros((tall, dims), jnp.float32)] * 4
    for k in range(lo):
        step = parts[k][pl.ds(lo * tall, tall), :]
        rest = parts[k][pl.ds((lo + 1) * tall, tall), :]
        image = parts[0][pl.ds(k * tall, tall), :]
        for m in range(1, lo):
            image = image + parts[m][pl.ds((k ^ m) * tall, tall), :]
        if k == 0:
            image_out[...] = image
        terms = (rest * rest, step * image, rest * image, image * image)
        sums = [s + t for s, t in zip(sums, terms)]
    for i, s in enumerate(sums):
        sums_out[pl.ds(i * cands, cands), :] = sum(
            s[p : p + cands] for p in range(0, tall, cands)
        )


def update_kernel(*refs):
    *sums, image, solution, residual, direction, out_s, out_r, out_d = refs
    cands = solution.shape[0]
    total = sums[0][...]
    for part in sums[1:]:
        total = total + part[...]
    total = jnp.sum(total, axis=1, keepdims=True)
    norm, curve, cross, square = (
        total[i * cands : (i + 1) * cands] for i in range(4)
    )
    alpha = norm / curve
    norm_next = norm - 2.0 * alpha * cross + alpha * (alpha * square)
    beta = norm_next / norm
    step = direction[...]
    fresh = residual[...] - alpha * unfold(image[...], cands)
    out_s[...] = solution[...] + alpha * step
    out_r[...] = fresh
    out_d[...] = fresh + beta * step


def per_device(devices, points, lengthscale, noise, solution, residual, direction):
    col_masks, row_masks = split_masks(devices)
    hi, lo = len(col_masks), len(row_masks)
    size, dims = points.shape
    cands = direction.shape[0]
    tall = cands * size // dims
    extra = -(-(8 + cands) // 16) * 16 * size // dims

    def meet(x, mask, odd_mask=None):
        masks = (mask, mask if odd_mask is None else odd_mask)
        return lax.ppermute(x, "blk", [(d, d ^ masks[d % 2]) for d in range(devices)])

    vmem = pl.BlockSpec(memory_space=pltpu.VMEM)
    hbm = pl.BlockSpec(memory_space=pltpu.HBM)
    params = pltpu.CompilerParams(vmem_limit_bytes=50 * 1024 * 1024)

    packed, own, rates = pl.pallas_call(
        pack_kernel,
        out_shape=(
            jax.ShapeDtypeStruct((size + extra, dims), jnp.bfloat16),
            jax.ShapeDtypeStruct((3 * tall, dims), jnp.float32),
            jax.ShapeDtypeStruct((8 * cands, dims), jnp.float32),
        ),
        in_specs=[hbm] * 5,
        out_specs=(vmem,) * 3,
        scratch_shapes=[
            pltpu.VMEM((cands, size), jnp.float32),
            pltpu.VMEM((cands, size), jnp.float32),
            pltpu.SMEM((cands,), jnp.float32),
            pltpu.SMEM((cands,), jnp.float32),
            pltpu.SemaphoreType.DMA((5,)),
        ],
        compiler_params=params,
        name="pack",
    )(
        *(
            pltpu.with_memory_space_constraint(x, pltpu.HBM)
            for x in (points, direction, residual, lengthscale, noise)
        )
    )

    rows = [points]
    for mask in row_masks[1:]:
        rows.append(meet(rows[-1], 1) if mask % 2 else meet(points, mask))
    spare = [
        pltpu.VMEM((cands, size, dims), jnp.float32),
        pltpu.VMEM((lo, size, size), jnp.float32),
    ]
    spread = jax.ShapeDtypeStruct((lo * cands * 8, size), jnp.float32)
    total, row_wide = pl.pallas_call(
        functools.partial(first_kernel, lo),
        out_shape=(spread, jax.ShapeDtypeStruct((lo * size, 2 * dims), jnp.bfloat16)),
        in_specs=[vmem] * (lo + 1),
        out_specs=(vmem, vmem),
        scratch_shapes=spare,
        compiler_params=params,
        name="product_0",
    )(packed, *rows[1:], rates)
    for mask in reversed(col_masks[2:]):
        total = pl.pallas_call(
            functools.partial(next_kernel, lo),
            out_shape=spread,
            in_specs=[vmem] * 4,
            out_specs=vmem,
            scratch_shapes=spare,
            compiler_params=params,
            name="product_%d" % mask,
        )(meet(packed, mask), row_wide, rates, total)
    partial = pl.pallas_call(
        functools.partial(last_kernel, lo),
        out_shape=jax.ShapeDtypeStruct(((lo + 2) * tall, dims), jnp.float32),
        in_specs=[vmem] * 5,
        out_specs=vmem,
        scratch_shapes=[*spare, pltpu.VMEM(spread.shape, jnp.float32)],
        compiler_params=params,
        name="product_last",
    )(meet(packed, col_masks[1]), row_wide, rates, total, own)

    image, sums = pl.pallas_call(
        functools.partial(sums_kernel, cands),
        out_shape=(
            jax.ShapeDtypeStruct((tall, dims), jnp.float32),
            jax.ShapeDtypeStruct((4 * cands, dims), jnp.float32),
        ),
        in_specs=[vmem] * lo,
        out_specs=(vmem, vmem),
        compiler_params=params,
        name="sums",
    )(partial, *(meet(partial, mask) for mask in row_masks[1:]))

    shared = [
        meet(sums, even, odd) for even, odd in zip(col_masks[1:-1:2], col_masks[2:-1:2])
    ]
    shared += [meet(x, 1) for x in shared]
    parts = [sums, meet(sums, col_masks[-1]), *shared]

    return pl.pallas_call(
        update_kernel,
        out_shape=(jax.ShapeDtypeStruct((cands, size), jnp.float32),) * 3,
        in_specs=[vmem] * (len(parts) + 4),
        out_specs=(vmem,) * 3,
        compiler_params=params,
        name="update",
    )(*parts, image, solution, residual, direction)


def solution(mesh):
    split = P(None, ("groups", "blk"))
    return jax.shard_map(
        functools.partial(per_device, mesh.shape["blk"]),
        mesh=mesh,
        in_specs=(P(("groups", "blk"), None), P("groups"), P("groups"), split, split, split),
        out_specs=(split, split, split),
        check_vma=False,
    )
```

```python
import functools

import jax
import jax.numpy as jnp
from jax import lax
from jax.experimental import pallas as pl
from jax.experimental.pallas import tpu as pltpu
from jax.sharding import PartitionSpec as P

def split_masks(devices):
    bits = devices.bit_length() - 1
    assert devices == 1 << bits and bits > 1
    lo = 1 << (bits // 2)
    return list(range(0, devices, lo)), list(range(lo))


def pieces_of(wide):
    high = wide.astype(jnp.bfloat16).astype(jnp.float32)
    middle = (wide - high).astype(jnp.bfloat16).astype(jnp.float32)
    return [high, middle, wide - high - middle]


def fold(wide, dims):
    return jnp.concatenate(
        [wide[:, p : p + dims] for p in range(0, wide.shape[1], dims)], axis=0
    )


def unfold(tall, n):
    return jnp.concatenate(
        [tall[p : p + n] for p in range(0, tall.shape[0], n)], axis=1
    )


def squares(points):
    wide = points.astype(jnp.float32)
    wide = wide * wide
    high = wide.astype(jnp.bfloat16)
    low = (wide - high.astype(jnp.float32)).astype(jnp.bfloat16)
    ones = jnp.ones((8, points.shape[1]), jnp.bfloat16)
    sums = [
        lax.dot_general(
            ones, half, (((1,), (1,)), ((), ())), preferred_element_type=jnp.float32
        )
        for half in (high, low)
    ]
    return (sums[0] + sums[1])[:1]


def pack_kernel(points, direction, residual, length, noise, packed, own, rates, *scratch):
    step_in, rest_in, length_in, noise_in, sems = scratch
    size, dims = points.shape
    cands = direction.shape[0]
    lines = (packed.shape[0] - size) * dims // size
    copies = [
        pltpu.make_async_copy(source, target, sems.at[i])
        for i, (source, target) in enumerate(
            (
                (points, packed.at[pl.ds(0, size), :]),
                (direction, step_in),
                (residual, rest_in),
                (length, length_in),
                (noise, noise_in),
            )
        )
    ]
    for copy in copies:
        copy.start()
    for copy in copies[1:]:
        copy.wait()
    step = step_in[...]
    which = lax.broadcasted_iota(jnp.int32, (cands, 1), 0)
    sigma = jnp.zeros((cands, 1), jnp.float32)
    for c in range(cands):
        sigma = jnp.where(which == c, noise_in[c], sigma)
        rate = -0.5 / (length_in[c] * length_in[c])
        rates[pl.ds(8 * c, 8), :] = jnp.full((8, dims), rate, jnp.float32)
    tall = own.shape[0] // 3
    for i, wide in enumerate((step, rest_in[...], sigma * step)):
        own[pl.ds(i * tall, tall), :] = fold(wide, dims)
    copies[0].wait()
    sq = squares(packed[:size, :])
    top = [*pieces_of(sq), jnp.ones((3, size), jnp.float32), jnp.zeros((2, size), jnp.float32)]
    top += [step, jnp.zeros((lines - 8 - cands, size), jnp.float32)]
    top = jnp.concatenate([t for t in top if t.shape[0]], axis=0)
    packed[size:, :] = fold(top, dims).astype(jnp.bfloat16)


def widen_row(points):
    wide = points.astype(jnp.float32)
    sq = pieces_of(jnp.sum(wide * wide, axis=1, keepdims=True))
    lane = lax.broadcasted_iota(jnp.int32, wide.shape, 1)
    extra = jnp.where(lane < 3, 1.0, 0.0)
    for i, piece in enumerate(sq):
        extra = jnp.where(lane == 3 + i, piece, extra)
    return jnp.concatenate(
        [(wide * -2.0).astype(jnp.bfloat16), extra.astype(jnp.bfloat16)], axis=1
    )


def add_column(col, row_wide, rates, weights, dist, before, out, lo):
    dims = col.shape[1]
    cands = rates.shape[0] // 8
    size = row_wide.shape[0] // lo
    wide = size // dims
    lines = (col.shape[0] - size) // wide
    top = unfold(col[size:, :], lines)
    top = jnp.concatenate([top, jnp.zeros((dims - lines, size), top.dtype)], axis=0).T
    both = jnp.concatenate([col[:size, :], top], axis=1)
    steps = top.astype(jnp.float32)

    def distances(k):
        dist[k] = lax.dot_general(
            both,
            row_wide[pl.ds(k * size, size), :],
            (((1,), (1,)), ((), ())),
            preferred_element_type=jnp.float32,
        )

    distances(0)
    for c in range(cands):
        weights[c] = jnp.broadcast_to(steps[:, 8 + c : 9 + c], (size, dims))
    rate = [
        jnp.concatenate([rates[pl.ds(8 * c, 8), :]] * wide, axis=1) for c in range(cands)
    ]
    for k in range(lo):
        if k + 1 < lo:
            distances(k + 1)
        places = [pl.ds((k * cands + c) * 8, 8) for c in range(cands)]
        total = [0.0 if before is None else before[at, :] for at in places]
        for j in range(0, size, 8):
            here = dist[k, pl.ds(j, 8), :]
            for c in range(cands):
                weight = jnp.concatenate([weights[c, pl.ds(j, 8), :]] * wide, axis=1)
                total[c] = total[c] + jnp.exp(here * rate[c]) * weight
        for c in range(cands):
            out[places[c], :] = total[c]


def first_kernel(lo, col, *refs):
    rows, refs = refs[: lo - 1], refs[lo - 1 :]
    rates, out, row_wide, weights, dist = refs
    size = row_wide.shape[0] // lo
    for k, block in enumerate((col, *rows)):
        row_wide[pl.ds(k * size, size), :] = widen_row(block[:size, :])
    add_column(col, row_wide, rates, weights, dist, None, out, lo)


def next_kernel(lo, col, row_wide, rates, before, out, weights, dist):
    add_column(col, row_wide, rates, weights, dist, before, out, lo)


def last_kernel(lo, col, row_wide, rates, before, own, out, weights, dist, spread):
    add_column(col, row_wide, rates, weights, dist, before, spread, lo)
    tall, dims = own.shape[0] // 3, own.shape[1]
    cands = rates.shape[0] // 8
    for k in range(lo):
        part = [
            jnp.sum(spread[pl.ds((k * cands + c) * 8, 8), :], axis=0, keepdims=True)
            for c in range(cands)
        ]
        part = fold(jnp.concatenate(part, axis=0), dims)
        if k == 0:
            part += own[pl.ds(2 * tall, tall), :]
        out[pl.ds(k * tall, tall), :] = part
    out[pl.ds(lo * tall, 2 * tall), :] = own[pl.ds(0, 2 * tall), :]


def sums_kernel(cands, *refs):
    *parts, image_out, sums_out = refs
    lo = len(parts)
    tall, dims = image_out.shape
    sums = [jnp.zeros((tall, dims), jnp.float32)] * 4
    for k in range(lo):
        step = parts[k][pl.ds(lo * tall, tall), :]
        rest = parts[k][pl.ds((lo + 1) * tall, tall), :]
        image = parts[0][pl.ds(k * tall, tall), :]
        for m in range(1, lo):
            image = image + parts[m][pl.ds((k ^ m) * tall, tall), :]
        if k == 0:
            image_out[...] = image
        terms = (rest * rest, step * image, rest * image, image * image)
        sums = [s + t for s, t in zip(sums, terms)]
    for i, s in enumerate(sums):
        sums_out[pl.ds(i * cands, cands), :] = sum(
            s[p : p + cands] for p in range(0, tall, cands)
        )


def update_kernel(*refs):
    *sums, image, solution, residual, direction, out_s, out_r, out_d = refs
    cands = solution.shape[0]
    total = sums[0][...]
    for part in sums[1:]:
        total = total + part[...]
    total = jnp.sum(total, axis=1, keepdims=True)
    norm, curve, cross, square = (
        total[i * cands : (i + 1) * cands] for i in range(4)
    )
    alpha = norm / curve
    norm_next = norm - 2.0 * alpha * cross + alpha * (alpha * square)
    beta = norm_next / norm
    step = direction[...]
    fresh = residual[...] - alpha * unfold(image[...], cands)
    out_s[...] = solution[...] + alpha * step
    out_r[...] = fresh
    out_d[...] = fresh + beta * step


def per_device(devices, points, lengthscale, noise, solution, residual, direction):
    col_masks, row_masks = split_masks(devices)
    hi, lo = len(col_masks), len(row_masks)
    size, dims = points.shape
    cands = direction.shape[0]
    tall = cands * size // dims
    extra = -(-(8 + cands) // 16) * 16 * size // dims

    def meet(x, mask, odd_mask=None):
        masks = (mask, mask if odd_mask is None else odd_mask)
        return lax.ppermute(x, "blk", [(d, d ^ masks[d % 2]) for d in range(devices)])

    vmem = pl.BlockSpec(memory_space=pltpu.VMEM)
    hbm = pl.BlockSpec(memory_space=pltpu.HBM)
    params = pltpu.CompilerParams(vmem_limit_bytes=50 * 1024 * 1024)

    packed, own, rates = pl.pallas_call(
        pack_kernel,
        out_shape=(
            jax.ShapeDtypeStruct((size + extra, dims), jnp.bfloat16),
            jax.ShapeDtypeStruct((3 * tall, dims), jnp.float32),
            jax.ShapeDtypeStruct((8 * cands, dims), jnp.float32),
        ),
        in_specs=[hbm] * 5,
        out_specs=(vmem,) * 3,
        scratch_shapes=[
            pltpu.VMEM((cands, size), jnp.float32),
            pltpu.VMEM((cands, size), jnp.float32),
            pltpu.SMEM((cands,), jnp.float32),
            pltpu.SMEM((cands,), jnp.float32),
            pltpu.SemaphoreType.DMA((5,)),
        ],
        compiler_params=params,
        name="pack",
    )(
        *(
            pltpu.with_memory_space_constraint(x, pltpu.HBM)
            for x in (points, direction, residual, lengthscale, noise)
        )
    )

    rows = [points]
    for mask in row_masks[1:]:
        rows.append(meet(rows[-1], 1) if mask % 2 else meet(points, mask))
    spare = [
        pltpu.VMEM((cands, size, dims), jnp.float32),
        pltpu.VMEM((lo, size, size), jnp.float32),
    ]
    spread = jax.ShapeDtypeStruct((lo * cands * 8, size), jnp.float32)
    total, row_wide = pl.pallas_call(
        functools.partial(first_kernel, lo),
        out_shape=(spread, jax.ShapeDtypeStruct((lo * size, 2 * dims), jnp.bfloat16)),
        in_specs=[vmem] * (lo + 1),
        out_specs=(vmem, vmem),
        scratch_shapes=spare,
        compiler_params=params,
        name="product_0",
    )(packed, *rows[1:], rates)
    for mask in reversed(col_masks[2:]):
        total = pl.pallas_call(
            functools.partial(next_kernel, lo),
            out_shape=spread,
            in_specs=[vmem] * 4,
            out_specs=vmem,
            scratch_shapes=spare,
            compiler_params=params,
            name="product_%d" % mask,
        )(meet(packed, mask), row_wide, rates, total)
    partial = pl.pallas_call(
        functools.partial(last_kernel, lo),
        out_shape=jax.ShapeDtypeStruct(((lo + 2) * tall, dims), jnp.float32),
        in_specs=[vmem] * 5,
        out_specs=vmem,
        scratch_shapes=[*spare, pltpu.VMEM(spread.shape, jnp.float32)],
        compiler_params=params,
        name="product_last",
    )(meet(packed, col_masks[1]), row_wide, rates, total, own)

    image, sums = pl.pallas_call(
        functools.partial(sums_kernel, cands),
        out_shape=(
            jax.ShapeDtypeStruct((tall, dims), jnp.float32),
            jax.ShapeDtypeStruct((4 * cands, dims), jnp.float32),
        ),
        in_specs=[vmem] * lo,
        out_specs=(vmem, vmem),
        compiler_params=params,
        name="sums",
    )(partial, *(meet(partial, mask) for mask in row_masks[1:]))

    half = hi // 2
    shared = [
        meet(sums, even, odd)
        for even, odd in zip(col_masks[1:half], reversed(col_masks[half + 1 :]))
    ]
    shared += [meet(x, 1) for x in shared]
    parts = [sums, meet(sums, col_masks[half]), *shared]

    return pl.pallas_call(
        update_kernel,
        out_shape=(jax.ShapeDtypeStruct((cands, size), jnp.float32),) * 3,
        in_specs=[vmem] * (len(parts) + 4),
        out_specs=(vmem,) * 3,
        compiler_params=params,
        name="update",
    )(*parts, image, solution, residual, direction)


def solution(mesh):
    split = P(None, ("groups", "blk"))
    return jax.shard_map(
        functools.partial(per_device, mesh.shape["blk"]),
        mesh=mesh,
        in_specs=(P(("groups", "blk"), None), P("groups"), P("groups"), split, split, split),
        out_specs=(split, split, split),
        check_vma=False,
    )
```

```python
import functools

import jax
import jax.numpy as jnp
from jax import lax
from jax.experimental import pallas as pl
from jax.experimental.pallas import tpu as pltpu
from jax.sharding import PartitionSpec as P

def split_masks(devices):
    bits = devices.bit_length() - 1
    assert devices == 1 << bits and bits > 1
    lo = 1 << (bits // 2)
    return list(range(0, devices, lo)), list(range(lo))


def pieces_of(wide):
    high = wide.astype(jnp.bfloat16).astype(jnp.float32)
    middle = (wide - high).astype(jnp.bfloat16).astype(jnp.float32)
    return [high, middle, wide - high - middle]


def fold(wide, dims):
    return jnp.concatenate(
        [wide[:, p : p + dims] for p in range(0, wide.shape[1], dims)], axis=0
    )


def unfold(tall, n):
    return jnp.concatenate(
        [tall[p : p + n] for p in range(0, tall.shape[0], n)], axis=1
    )


def squares(points):
    wide = points.astype(jnp.float32)
    wide = wide * wide
    high = wide.astype(jnp.bfloat16)
    low = (wide - high.astype(jnp.float32)).astype(jnp.bfloat16)
    ones = jnp.ones((8, points.shape[1]), jnp.bfloat16)
    sums = [
        lax.dot_general(
            ones, half, (((1,), (1,)), ((), ())), preferred_element_type=jnp.float32
        )
        for half in (high, low)
    ]
    return (sums[0] + sums[1])[:1]


def pack_kernel(points, direction, residual, length, noise, packed, own, rates, *refs):
    *wider, step_in, rest_in, length_in, noise_in, sems = refs
    size, dims = points.shape
    cands = direction.shape[0]
    lines = (packed.shape[0] - size) * dims // size
    copies = [
        pltpu.make_async_copy(source, target, sems.at[i])
        for i, (source, target) in enumerate(
            (
                (points, packed.at[pl.ds(0, size), :]),
                (direction, step_in),
                (residual, rest_in),
                (length, length_in),
                (noise, noise_in),
            )
        )
    ]
    for copy in copies:
        copy.start()
    for copy in copies[1:]:
        copy.wait()
    step = step_in[...]
    which = lax.broadcasted_iota(jnp.int32, (cands, 1), 0)
    sigma = jnp.zeros((cands, 1), jnp.float32)
    for c in range(cands):
        sigma = jnp.where(which == c, noise_in[c], sigma)
        rate = -0.5 / (length_in[c] * length_in[c])
        rates[pl.ds(8 * c, 8), :] = jnp.full((8, dims), rate, jnp.float32)
    tall = own.shape[0] // 3
    for i, wide in enumerate((step, rest_in[...], sigma * step)):
        own[pl.ds(i * tall, tall), :] = fold(wide, dims)
    copies[0].wait()
    sq = squares(packed[:size, :])
    top = [*pieces_of(sq), step, jnp.zeros((lines - 3 - cands, size), jnp.float32)]
    top = jnp.concatenate([t for t in top if t.shape[0]], axis=0)
    packed[size:, :] = fold(top, dims).astype(jnp.bfloat16)
    filled = packed.shape[0]
    for copy in wider:
        copy[:filled, :] = packed[...]
        spare = copy.shape[0] - filled
        copy[filled:, :] = jnp.zeros((spare, dims), jnp.bfloat16)


def lines_of(cands):
    return -(-(3 + cands) // 8) * 8


def widen_row(points, lines):
    wide = points.astype(jnp.float32)
    sq = pieces_of(jnp.sum(wide * wide, axis=1, keepdims=True))
    lane = lax.broadcasted_iota(jnp.int32, wide.shape, 1)
    extra = jnp.where(lane < 3, 1.0, 0.0)
    for i, piece in enumerate(sq):
        extra = jnp.where(lane == lines + i, piece, extra)
    return jnp.concatenate(
        [(wide * -2.0).astype(jnp.bfloat16), extra.astype(jnp.bfloat16)], axis=1
    )


def add_column(col, row_wide, rates, weights, dist, before, out, lo):
    dims = col.shape[1]
    cands = rates.shape[0] // 8
    size = row_wide.shape[0] // lo
    wide = size // dims
    lines = lines_of(cands)
    top = unfold(col[size : size + lines * wide, :].astype(jnp.float32), lines)
    ones = lax.broadcasted_iota(jnp.int32, (8, size), 0) < 3
    rest = jnp.zeros((dims - lines - 8, size), jnp.float32)
    top = jnp.concatenate([top, ones.astype(jnp.float32), rest], axis=0)
    top = top.astype(jnp.bfloat16).T
    both = jnp.concatenate([col[:size, :], top], axis=1)
    steps = top.astype(jnp.float32)

    def distances(k):
        dist[k] = lax.dot_general(
            both,
            row_wide[pl.ds(k * size, size), :],
            (((1,), (1,)), ((), ())),
            preferred_element_type=jnp.float32,
        )

    distances(0)
    for c in range(cands):
        weights[c] = jnp.broadcast_to(steps[:, 3 + c : 4 + c], (size, dims))
    rate = [
        jnp.concatenate([rates[pl.ds(8 * c, 8), :]] * wide, axis=1) for c in range(cands)
    ]
    for k in range(lo):
        if k + 1 < lo:
            distances(k + 1)
        places = [pl.ds((k * cands + c) * 8, 8) for c in range(cands)]
        total = [0.0 if before is None else before[at, :] for at in places]
        for j in range(0, size, 8):
            here = dist[k, pl.ds(j, 8), :]
            for c in range(cands):
                weight = jnp.concatenate([weights[c, pl.ds(j, 8), :]] * wide, axis=1)
                total[c] = total[c] + jnp.exp(here * rate[c]) * weight
        for c in range(cands):
            out[places[c], :] = total[c]


def stretch_kernel(block, out):
    size = block.shape[0]
    out[:size, :] = block[...]
    out[size:, :] = jnp.zeros((out.shape[0] - size, out.shape[1]), out.dtype)


def first_kernel(lo, col, *refs):
    rows, refs = refs[: lo - 1], refs[lo - 1 :]
    rates, out, row_wide, weights, dist = refs
    size = row_wide.shape[0] // lo
    for k, block in enumerate((col, *rows)):
        row_wide[pl.ds(k * size, size), :] = widen_row(
            block[:size, :], lines_of(rates.shape[0] // 8)
        )
    add_column(col, row_wide, rates, weights, dist, None, out, lo)


def next_kernel(lo, col, row_wide, rates, before, out, weights, dist):
    add_column(col, row_wide, rates, weights, dist, before, out, lo)


def last_kernel(lo, col, row_wide, rates, before, own, out, weights, dist, spread):
    add_column(col, row_wide, rates, weights, dist, before, spread, lo)
    tall, dims = own.shape[0] // 3, own.shape[1]
    cands = rates.shape[0] // 8
    for k in range(lo):
        part = [
            jnp.sum(spread[pl.ds((k * cands + c) * 8, 8), :], axis=0, keepdims=True)
            for c in range(cands)
        ]
        part = fold(jnp.concatenate(part, axis=0), dims)
        if k == 0:
            part += own[pl.ds(2 * tall, tall), :]
        out[pl.ds(k * tall, tall), :] = part
    out[pl.ds(lo * tall, 2 * tall), :] = own[pl.ds(0, 2 * tall), :]


def sums_kernel(cands, *refs):
    *parts, image_out, sums_out = refs
    lo = len(parts)
    tall, dims = image_out.shape
    sums = [jnp.zeros((tall, dims), jnp.float32)] * 4
    for k in range(lo):
        step = parts[k][pl.ds(lo * tall, tall), :]
        rest = parts[k][pl.ds((lo + 1) * tall, tall), :]
        image = parts[0][pl.ds(k * tall, tall), :]
        for m in range(1, lo):
            image = image + parts[m][pl.ds((k ^ m) * tall, tall), :]
        if k == 0:
            image_out[...] = image
        terms = (rest * rest, step * image, rest * image, image * image)
        sums = [s + t for s, t in zip(sums, terms)]
    for i, s in enumerate(sums):
        sums_out[pl.ds(i * cands, cands), :] = sum(
            s[p : p + cands] for p in range(0, tall, cands)
        )


def update_kernel(*refs):
    *sums, image, solution, residual, direction, out_s, out_r, out_d = refs
    cands = solution.shape[0]
    total = sums[0][...]
    for part in sums[1:]:
        total = total + part[...]
    total = jnp.sum(total, axis=1, keepdims=True)
    norm, curve, cross, square = (
        total[i * cands : (i + 1) * cands] for i in range(4)
    )
    alpha = norm / curve
    norm_next = norm - 2.0 * alpha * cross + alpha * (alpha * square)
    beta = norm_next / norm
    step = direction[...]
    fresh = residual[...] - alpha * unfold(image[...], cands)
    out_s[...] = solution[...] + alpha * step
    out_r[...] = fresh
    out_d[...] = fresh + beta * step


def per_device(devices, points, lengthscale, noise, solution, residual, direction):
    col_masks, row_masks = split_masks(devices)
    hi, lo = len(col_masks), len(row_masks)
    size, dims = points.shape
    cands = direction.shape[0]
    tall = cands * size // dims
    filled = size + lines_of(cands) * size // dims

    def meet(x, mask, odd_mask=None):
        masks = (mask, mask if odd_mask is None else odd_mask)
        return lax.ppermute(x, "blk", [(d, d ^ masks[d % 2]) for d in range(devices)])

    vmem = pl.BlockSpec(memory_space=pltpu.VMEM)
    hbm = pl.BlockSpec(memory_space=pltpu.HBM)
    params = pltpu.CompilerParams(vmem_limit_bytes=50 * 1024 * 1024)

    packed, own, rates, middle, core, far = pl.pallas_call(
        pack_kernel,
        out_shape=(
            jax.ShapeDtypeStruct((filled, dims), jnp.bfloat16),
            jax.ShapeDtypeStruct((3 * tall, dims), jnp.float32),
            jax.ShapeDtypeStruct((8 * cands, dims), jnp.float32),
            jax.ShapeDtypeStruct((filled + 16, dims), jnp.bfloat16),
            jax.ShapeDtypeStruct((filled + 32, dims), jnp.bfloat16),
            jax.ShapeDtypeStruct((filled + 48, dims), jnp.bfloat16),
        ),
        in_specs=[hbm] * 5,
        out_specs=(vmem,) * 6,
        scratch_shapes=[
            pltpu.VMEM((cands, size), jnp.float32),
            pltpu.VMEM((cands, size), jnp.float32),
            pltpu.SMEM((cands,), jnp.float32),
            pltpu.SMEM((cands,), jnp.float32),
            pltpu.SemaphoreType.DMA((5,)),
        ],
        compiler_params=params,
        name="pack",
    )(
        *(
            pltpu.with_memory_space_constraint(x, pltpu.HBM)
            for x in (points, direction, residual, lengthscale, noise)
        )
    )

    rows = [packed, meet(core, 1)]
    for mask in row_masks[2::2]:
        block = meet(points, mask)
        stretched = pl.pallas_call(
            stretch_kernel,
            out_shape=jax.ShapeDtypeStruct(core.shape, core.dtype),
            in_specs=[vmem],
            out_specs=vmem,
            compiler_params=params,
            name="stretch",
        )(block)
        rows += [block, meet(stretched, 1)]

    def column(k):
        wider = far if k > hi // 2 else middle if k == hi // 2 else packed
        return meet(wider, col_masks[k])

    spare = [
        pltpu.VMEM((cands, size, dims), jnp.float32),
        pltpu.VMEM((lo, size, size), jnp.float32),
    ]
    spread = jax.ShapeDtypeStruct((lo * cands * 8, size), jnp.float32)
    total, row_wide = pl.pallas_call(
        functools.partial(first_kernel, lo),
        out_shape=(spread, jax.ShapeDtypeStruct((lo * size, 2 * dims), jnp.bfloat16)),
        in_specs=[vmem] * (lo + 1),
        out_specs=(vmem, vmem),
        scratch_shapes=spare,
        compiler_params=params,
        name="product_0",
    )(packed, *rows[1:], rates)
    order = [*range(hi - 1, hi // 2, -1), *range(1, hi // 2 + 1)]
    for k in order[:-1]:
        total = pl.pallas_call(
            functools.partial(next_kernel, lo),
            out_shape=spread,
            in_specs=[vmem] * 4,
            out_specs=vmem,
            scratch_shapes=spare,
            compiler_params=params,
            name="product_%d" % k,
        )(column(k), row_wide, rates, total)
    partial = pl.pallas_call(
        functools.partial(last_kernel, lo),
        out_shape=jax.ShapeDtypeStruct(((lo + 2) * tall, dims), jnp.float32),
        in_specs=[vmem] * 5,
        out_specs=vmem,
        scratch_shapes=[*spare, pltpu.VMEM(spread.shape, jnp.float32)],
        compiler_params=params,
        name="product_last",
    )(column(order[-1]), row_wide, rates, total, own)

    image, sums = pl.pallas_call(
        functools.partial(sums_kernel, cands),
        out_shape=(
            jax.ShapeDtypeStruct((tall, dims), jnp.float32),
            jax.ShapeDtypeStruct((4 * cands, dims), jnp.float32),
        ),
        in_specs=[vmem] * lo,
        out_specs=(vmem, vmem),
        compiler_params=params,
        name="sums",
    )(partial, *(meet(partial, mask) for mask in row_masks[1:]))

    half = hi // 2
    shared = [
        meet(sums, even, odd)
        for even, odd in zip(col_masks[1:half], reversed(col_masks[half + 1 :]))
    ]
    shared += [meet(x, 1) for x in shared]
    parts = [sums, meet(sums, col_masks[half]), *shared]

    return pl.pallas_call(
        update_kernel,
        out_shape=(jax.ShapeDtypeStruct((cands, size), jnp.float32),) * 3,
        in_specs=[vmem] * (len(parts) + 4),
        out_specs=(vmem,) * 3,
        compiler_params=params,
        name="update",
    )(*parts, image, solution, residual, direction)


def solution(mesh):
    split = P(None, ("groups", "blk"))
    return jax.shard_map(
        functools.partial(per_device, mesh.shape["blk"]),
        mesh=mesh,
        in_specs=(P(("groups", "blk"), None), P("groups"), P("groups"), split, split, split),
        out_specs=(split, split, split),
        check_vma=False,
    )
```

```python
import functools

import jax
import jax.numpy as jnp
from jax import lax
from jax.experimental import pallas as pl
from jax.experimental.pallas import tpu as pltpu
from jax.sharding import PartitionSpec as P

def split_masks(devices):
    bits = devices.bit_length() - 1
    assert devices == 1 << bits and bits > 1
    far = bits // 2 - 1
    row = [m << (bits - far) for m in range(1 << far)]
    col = [m << 1 for m in range(1 << (bits - 1 - far))]
    return col, [m + core for m in row for core in (0, 1)]


def pieces_of(wide):
    high = wide.astype(jnp.bfloat16).astype(jnp.float32)
    middle = (wide - high).astype(jnp.bfloat16).astype(jnp.float32)
    return [high, middle, wide - high - middle]


def fold(wide, dims):
    return jnp.concatenate(
        [wide[:, p : p + dims] for p in range(0, wide.shape[1], dims)], axis=0
    )


def unfold(tall, n):
    return jnp.concatenate(
        [tall[p : p + n] for p in range(0, tall.shape[0], n)], axis=1
    )


def squares(points):
    wide = points.astype(jnp.float32)
    wide = wide * wide
    high = wide.astype(jnp.bfloat16)
    low = (wide - high.astype(jnp.float32)).astype(jnp.bfloat16)
    ones = jnp.ones((8, points.shape[1]), jnp.bfloat16)
    sums = [
        lax.dot_general(
            ones, half, (((1,), (1,)), ((), ())), preferred_element_type=jnp.float32
        )
        for half in (high, low)
    ]
    return (sums[0] + sums[1])[:1]


def pack_kernel(points, direction, residual, length, noise, packed, own, rates, *refs):
    *wider, step_in, rest_in, length_in, noise_in, sems = refs
    size, dims = points.shape
    cands = direction.shape[0]
    lines = (packed.shape[0] - size) * dims // size
    copies = [
        pltpu.make_async_copy(source, target, sems.at[i])
        for i, (source, target) in enumerate(
            (
                (points, packed.at[pl.ds(0, size), :]),
                (direction, step_in),
                (residual, rest_in),
                (length, length_in),
                (noise, noise_in),
            )
        )
    ]
    for copy in copies:
        copy.start()
    for copy in copies[1:]:
        copy.wait()
    step = step_in[...]
    which = lax.broadcasted_iota(jnp.int32, (cands, 1), 0)
    sigma = jnp.zeros((cands, 1), jnp.float32)
    for c in range(cands):
        sigma = jnp.where(which == c, noise_in[c], sigma)
        rate = -0.5 / (length_in[c] * length_in[c])
        rates[pl.ds(8 * c, 8), :] = jnp.full((8, dims), rate, jnp.float32)
    tall = own.shape[0] // 3
    for i, wide in enumerate((step, rest_in[...], sigma * step)):
        own[pl.ds(i * tall, tall), :] = fold(wide, dims)
    copies[0].wait()
    sq = squares(packed[:size, :])
    top = [*pieces_of(sq), step, jnp.zeros((lines - 3 - cands, size), jnp.float32)]
    top = jnp.concatenate([t for t in top if t.shape[0]], axis=0)
    packed[size:, :] = fold(top, dims).astype(jnp.bfloat16)
    filled = packed.shape[0]
    for copy in wider:
        copy[:filled, :] = packed[...]
        spare = copy.shape[0] - filled
        copy[filled:, :] = jnp.zeros((spare, dims), jnp.bfloat16)


def lines_of(cands):
    return -(-(3 + cands) // 8) * 8


def widen_row(points, lines):
    wide = points.astype(jnp.float32)
    sq = pieces_of(jnp.sum(wide * wide, axis=1, keepdims=True))
    lane = lax.broadcasted_iota(jnp.int32, wide.shape, 1)
    extra = jnp.where(lane < 3, 1.0, 0.0)
    for i, piece in enumerate(sq):
        extra = jnp.where(lane == lines + i, piece, extra)
    return jnp.concatenate(
        [(wide * -2.0).astype(jnp.bfloat16), extra.astype(jnp.bfloat16)], axis=1
    )


def add_column(col, row_wide, rates, weights, dist, before, out, lo):
    dims = col.shape[1]
    cands = rates.shape[0] // 8
    size = row_wide.shape[0] // lo
    wide = size // dims
    lines = lines_of(cands)
    top = unfold(col[size : size + lines * wide, :].astype(jnp.float32), lines)
    ones = lax.broadcasted_iota(jnp.int32, (8, size), 0) < 3
    rest = jnp.zeros((dims - lines - 8, size), jnp.float32)
    top = jnp.concatenate([top, ones.astype(jnp.float32), rest], axis=0)
    top = top.astype(jnp.bfloat16).T
    both = jnp.concatenate([col[:size, :], top], axis=1)
    steps = top.astype(jnp.float32)

    def distances(k):
        dist[k] = lax.dot_general(
            both,
            row_wide[pl.ds(k * size, size), :],
            (((1,), (1,)), ((), ())),
            preferred_element_type=jnp.float32,
        )

    distances(0)
    for c in range(cands):
        weights[c] = jnp.broadcast_to(steps[:, 3 + c : 4 + c], (size, dims))
    rate = [
        jnp.concatenate([rates[pl.ds(8 * c, 8), :]] * wide, axis=1) for c in range(cands)
    ]
    for k in range(lo):
        if k + 1 < lo:
            distances(k + 1)
        places = [pl.ds((k * cands + c) * 8, 8) for c in range(cands)]
        total = [0.0 if before is None else before[at, :] for at in places]
        for j in range(0, size, 8):
            here = dist[k, pl.ds(j, 8), :]
            for c in range(cands):
                weight = jnp.concatenate([weights[c, pl.ds(j, 8), :]] * wide, axis=1)
                total[c] = total[c] + jnp.exp(here * rate[c]) * weight
        for c in range(cands):
            out[places[c], :] = total[c]


def stretch_kernel(block, out):
    size = block.shape[0]
    out[:size, :] = block[...]
    out[size:, :] = jnp.zeros((out.shape[0] - size, out.shape[1]), out.dtype)


def first_kernel(lo, col, *refs):
    rows, refs = refs[: lo - 1], refs[lo - 1 :]
    rates, out, row_wide, weights, dist = refs
    size = row_wide.shape[0] // lo
    for k, block in enumerate((col, *rows)):
        row_wide[pl.ds(k * size, size), :] = widen_row(
            block[:size, :], lines_of(rates.shape[0] // 8)
        )
    add_column(col, row_wide, rates, weights, dist, None, out, lo)


def next_kernel(lo, col, row_wide, rates, before, out, weights, dist):
    add_column(col, row_wide, rates, weights, dist, before, out, lo)


def last_kernel(lo, col, row_wide, rates, before, own, out, weights, dist, spread):
    add_column(col, row_wide, rates, weights, dist, before, spread, lo)
    tall, dims = own.shape[0] // 3, own.shape[1]
    cands = rates.shape[0] // 8
    for k in range(lo):
        part = [
            jnp.sum(spread[pl.ds((k * cands + c) * 8, 8), :], axis=0, keepdims=True)
            for c in range(cands)
        ]
        part = fold(jnp.concatenate(part, axis=0), dims)
        if k == 0:
            part += own[pl.ds(2 * tall, tall), :]
        out[pl.ds(k * tall, tall), :] = part
    out[pl.ds(lo * tall, 2 * tall), :] = own[pl.ds(0, 2 * tall), :]


def sums_kernel(cands, *refs):
    *parts, image_out, sums_out = refs
    lo = len(parts)
    tall, dims = image_out.shape
    sums = [jnp.zeros((tall, dims), jnp.float32)] * 4
    for k in range(lo):
        step = parts[k][pl.ds(lo * tall, tall), :]
        rest = parts[k][pl.ds((lo + 1) * tall, tall), :]
        image = parts[0][pl.ds(k * tall, tall), :]
        for m in range(1, lo):
            image = image + parts[m][pl.ds((k ^ m) * tall, tall), :]
        if k == 0:
            image_out[...] = image
        terms = (rest * rest, step * image, rest * image, image * image)
        sums = [s + t for s, t in zip(sums, terms)]
    for i, s in enumerate(sums):
        sums_out[pl.ds(i * cands, cands), :] = sum(
            s[p : p + cands] for p in range(0, tall, cands)
        )


def update_kernel(*refs):
    *sums, image, solution, residual, direction, out_s, out_r, out_d = refs
    cands = solution.shape[0]
    total = sums[0][...]
    for part in sums[1:]:
        total = total + part[...]
    total = jnp.sum(total, axis=1, keepdims=True)
    norm, curve, cross, square = (
        total[i * cands : (i + 1) * cands] for i in range(4)
    )
    alpha = norm / curve
    norm_next = norm - 2.0 * alpha * cross + alpha * (alpha * square)
    beta = norm_next / norm
    step = direction[...]
    fresh = residual[...] - alpha * unfold(image[...], cands)
    out_s[...] = solution[...] + alpha * step
    out_r[...] = fresh
    out_d[...] = fresh + beta * step


def per_device(devices, points, lengthscale, noise, solution, residual, direction):
    col_masks, row_masks = split_masks(devices)
    hi, lo = len(col_masks), len(row_masks)
    size, dims = points.shape
    cands = direction.shape[0]
    tall = cands * size // dims
    filled = size + lines_of(cands) * size // dims

    def meet(x, mask, odd_mask=None):
        masks = (mask, mask if odd_mask is None else odd_mask)
        return lax.ppermute(x, "blk", [(d, d ^ masks[d % 2]) for d in range(devices)])

    vmem = pl.BlockSpec(memory_space=pltpu.VMEM)
    hbm = pl.BlockSpec(memory_space=pltpu.HBM)
    params = pltpu.CompilerParams(vmem_limit_bytes=50 * 1024 * 1024)

    packed, own, rates, core, middle, far = pl.pallas_call(
        pack_kernel,
        out_shape=(
            jax.ShapeDtypeStruct((filled, dims), jnp.bfloat16),
            jax.ShapeDtypeStruct((3 * tall, dims), jnp.float32),
            jax.ShapeDtypeStruct((8 * cands, dims), jnp.float32),
            jax.ShapeDtypeStruct((filled + 16, dims), jnp.bfloat16),
            jax.ShapeDtypeStruct((filled + 32, dims), jnp.bfloat16),
            jax.ShapeDtypeStruct((filled + 48, dims), jnp.bfloat16),
        ),
        in_specs=[hbm] * 5,
        out_specs=(vmem,) * 6,
        scratch_shapes=[
            pltpu.VMEM((cands, size), jnp.float32),
            pltpu.VMEM((cands, size), jnp.float32),
            pltpu.SMEM((cands,), jnp.float32),
            pltpu.SMEM((cands,), jnp.float32),
            pltpu.SemaphoreType.DMA((5,)),
        ],
        compiler_params=params,
        name="pack",
    )(
        *(
            pltpu.with_memory_space_constraint(x, pltpu.HBM)
            for x in (points, direction, residual, lengthscale, noise)
        )
    )

    rows = [packed, meet(core, 1)]
    for mask in row_masks[2::2]:
        block = meet(points, mask)
        stretched = pl.pallas_call(
            stretch_kernel,
            out_shape=jax.ShapeDtypeStruct(core.shape, core.dtype),
            in_specs=[vmem],
            out_specs=vmem,
            compiler_params=params,
            name="stretch",
        )(block)
        rows += [block, meet(stretched, 1)]

    def column(k):
        wider = far if k > hi // 2 else middle if k == hi // 2 else packed
        return meet(wider, col_masks[k])

    spare = [
        pltpu.VMEM((cands, size, dims), jnp.float32),
        pltpu.VMEM((lo, size, size), jnp.float32),
    ]
    spread = jax.ShapeDtypeStruct((lo * cands * 8, size), jnp.float32)
    total, row_wide = pl.pallas_call(
        functools.partial(first_kernel, lo),
        out_shape=(spread, jax.ShapeDtypeStruct((lo * size, 2 * dims), jnp.bfloat16)),
        in_specs=[vmem] * (lo + 1),
        out_specs=(vmem, vmem),
        scratch_shapes=spare,
        compiler_params=params,
        name="product_0",
    )(packed, *rows[1:], rates)
    order = list(range(hi - 1, 0, -1))
    for k in order[:-1]:
        total = pl.pallas_call(
            functools.partial(next_kernel, lo),
            out_shape=spread,
            in_specs=[vmem] * 4,
            out_specs=vmem,
            scratch_shapes=spare,
            compiler_params=params,
            name="product_%d" % k,
        )(column(k), row_wide, rates, total)
    partial = pl.pallas_call(
        functools.partial(last_kernel, lo),
        out_shape=jax.ShapeDtypeStruct(((lo + 2) * tall, dims), jnp.float32),
        in_specs=[vmem] * 5,
        out_specs=vmem,
        scratch_shapes=[*spare, pltpu.VMEM(spread.shape, jnp.float32)],
        compiler_params=params,
        name="product_last",
    )(column(order[-1]), row_wide, rates, total, own)

    image, sums = pl.pallas_call(
        functools.partial(sums_kernel, cands),
        out_shape=(
            jax.ShapeDtypeStruct((tall, dims), jnp.float32),
            jax.ShapeDtypeStruct((4 * cands, dims), jnp.float32),
        ),
        in_specs=[vmem] * lo,
        out_specs=(vmem, vmem),
        compiler_params=params,
        name="sums",
    )(partial, *(meet(partial, mask) for mask in row_masks[1:]))

    half = hi // 2
    shared = [
        meet(sums, even, odd)
        for even, odd in zip(col_masks[1:half], reversed(col_masks[half + 1 :]))
    ]
    shared += [meet(x, 1) for x in shared]
    parts = [sums, meet(sums, col_masks[half]), *shared]

    return pl.pallas_call(
        update_kernel,
        out_shape=(jax.ShapeDtypeStruct((cands, size), jnp.float32),) * 3,
        in_specs=[vmem] * (len(parts) + 4),
        out_specs=(vmem,) * 3,
        compiler_params=params,
        name="update",
    )(*parts, image, solution, residual, direction)


def solution(mesh):
    split = P(None, ("groups", "blk"))
    return jax.shard_map(
        functools.partial(per_device, mesh.shape["blk"]),
        mesh=mesh,
        in_specs=(P(("groups", "blk"), None), P("groups"), P("groups"), split, split, split),
        out_specs=(split, split, split),
        check_vma=False,
    )
```

```python
import functools

import jax
import jax.numpy as jnp
from jax import lax
from jax.experimental import pallas as pl
from jax.experimental.pallas import tpu as pltpu
from jax.sharding import PartitionSpec as P

LOG2E = 1.4426950408889634


def split_masks(devices):
    bits = devices.bit_length() - 1
    assert devices == 1 << bits and bits > 1
    far = bits // 2 - 1
    row = [m << (bits - far) for m in range(1 << far)]
    col = [m << 1 for m in range(1 << (bits - 1 - far))]
    return col, [m + core for m in row for core in (0, 1)]


def pieces_of(wide):
    high = wide.astype(jnp.bfloat16).astype(jnp.float32)
    middle = (wide - high).astype(jnp.bfloat16).astype(jnp.float32)
    return [high, middle, wide - high - middle]


def fold(wide, dims):
    return jnp.concatenate(
        [wide[:, p : p + dims] for p in range(0, wide.shape[1], dims)], axis=0
    )


def unfold(tall, n):
    return jnp.concatenate(
        [tall[p : p + n] for p in range(0, tall.shape[0], n)], axis=1
    )


def squares(points):
    wide = points.astype(jnp.float32)
    wide = wide * wide
    high = wide.astype(jnp.bfloat16)
    low = (wide - high.astype(jnp.float32)).astype(jnp.bfloat16)
    ones = jnp.ones((8, points.shape[1]), jnp.bfloat16)
    sums = [
        lax.dot_general(
            ones, half, (((1,), (1,)), ((), ())), preferred_element_type=jnp.float32
        )
        for half in (high, low)
    ]
    return (sums[0] + sums[1])[:1]


def pack_kernel(points, direction, residual, length, noise, packed, own, rates, *refs):
    *wider, step_in, rest_in, length_in, noise_in, sems = refs
    size, dims = points.shape
    cands = direction.shape[0]
    lines = (packed.shape[0] - size) * dims // size
    copies = [
        pltpu.make_async_copy(source, target, sems.at[i])
        for i, (source, target) in enumerate(
            (
                (points, packed.at[pl.ds(0, size), :]),
                (direction, step_in),
                (residual, rest_in),
                (length, length_in),
                (noise, noise_in),
            )
        )
    ]
    for copy in copies:
        copy.start()
    for copy in copies[1:]:
        copy.wait()
    step = step_in[...]
    which = lax.broadcasted_iota(jnp.int32, (cands, 1), 0)
    sigma = jnp.zeros((cands, 1), jnp.float32)
    for c in range(cands):
        sigma = jnp.where(which == c, noise_in[c], sigma)
        rate = (-0.5 * LOG2E) / (length_in[c] * length_in[c])
        rates[pl.ds(8 * c, 8), :] = jnp.full((8, dims), rate, jnp.float32)
    tall = own.shape[0] // 3
    for i, wide in enumerate((step, rest_in[...], sigma * step)):
        own[pl.ds(i * tall, tall), :] = fold(wide, dims)
    copies[0].wait()
    sq = squares(packed[:size, :])
    top = [*pieces_of(sq), step, jnp.zeros((lines - 3 - cands, size), jnp.float32)]
    top = jnp.concatenate([t for t in top if t.shape[0]], axis=0)
    packed[size:, :] = fold(top, dims).astype(jnp.bfloat16)
    filled = packed.shape[0]
    for copy in wider:
        copy[:filled, :] = packed[...]
        spare = copy.shape[0] - filled
        copy[filled:, :] = jnp.zeros((spare, dims), jnp.bfloat16)


def lines_of(cands):
    return -(-(3 + cands) // 8) * 8


def widen_row(points, lines):
    wide = points.astype(jnp.float32)
    sq = pieces_of(jnp.sum(wide * wide, axis=1, keepdims=True))
    lane = lax.broadcasted_iota(jnp.int32, wide.shape, 1)
    extra = jnp.where(lane < 3, 1.0, 0.0)
    for i, piece in enumerate(sq):
        extra = jnp.where(lane == lines + i, piece, extra)
    return jnp.concatenate(
        [(wide * -2.0).astype(jnp.bfloat16), extra.astype(jnp.bfloat16)], axis=1
    )


def add_column(col, row_wide, rates, weights, dist, before, out, lo):
    dims = col.shape[1]
    cands = rates.shape[0] // 8
    size = row_wide.shape[0] // lo
    wide = size // dims
    lines = lines_of(cands)
    top = unfold(col[size : size + lines * wide, :].astype(jnp.float32), lines)
    ones = lax.broadcasted_iota(jnp.int32, (8, size), 0) < 3
    rest = jnp.zeros((dims - lines - 8, size), jnp.float32)
    top = jnp.concatenate([top, ones.astype(jnp.float32), rest], axis=0)
    top = top.astype(jnp.bfloat16).T
    both = jnp.concatenate([col[:size, :], top], axis=1)
    steps = top.astype(jnp.float32)

    def distances(k):
        dist[k] = lax.dot_general(
            both,
            row_wide[pl.ds(k * size, size), :],
            (((1,), (1,)), ((), ())),
            preferred_element_type=jnp.float32,
        )

    distances(0)
    for c in range(cands):
        weights[c] = jnp.broadcast_to(steps[:, 3 + c : 4 + c], (size, dims))
    rate = [
        jnp.concatenate([rates[pl.ds(8 * c, 8), :]] * wide, axis=1) for c in range(cands)
    ]
    for k in range(lo):
        if k + 1 < lo:
            distances(k + 1)
        places = [pl.ds((k * cands + c) * 8, 8) for c in range(cands)]
        total = [0.0 if before is None else before[at, :] for at in places]
        for j in range(0, size, 8):
            here = dist[k, pl.ds(j, 8), :]
            for c in range(cands):
                weight = jnp.concatenate([weights[c, pl.ds(j, 8), :]] * wide, axis=1)
                total[c] = total[c] + jnp.exp2(here * rate[c]) * weight
        for c in range(cands):
            out[places[c], :] = total[c]


def stretch_kernel(block, out):
    size = block.shape[0]
    out[:size, :] = block[...]
    out[size:, :] = jnp.zeros((out.shape[0] - size, out.shape[1]), out.dtype)


def first_kernel(lo, col, *refs):
    rows, refs = refs[: lo - 1], refs[lo - 1 :]
    rates, out, row_wide, weights, dist = refs
    size = row_wide.shape[0] // lo
    for k, block in enumerate((col, *rows)):
        row_wide[pl.ds(k * size, size), :] = widen_row(
            block[:size, :], lines_of(rates.shape[0] // 8)
        )
    add_column(col, row_wide, rates, weights, dist, None, out, lo)


def next_kernel(lo, col, row_wide, rates, before, out, weights, dist):
    add_column(col, row_wide, rates, weights, dist, before, out, lo)


def last_kernel(lo, col, row_wide, rates, before, own, out, weights, dist, spread):
    add_column(col, row_wide, rates, weights, dist, before, spread, lo)
    tall, dims = own.shape[0] // 3, own.shape[1]
    cands = rates.shape[0] // 8
    for k in range(lo):
        part = [
            jnp.sum(spread[pl.ds((k * cands + c) * 8, 8), :], axis=0, keepdims=True)
            for c in range(cands)
        ]
        part = fold(jnp.concatenate(part, axis=0), dims)
        if k == 0:
            part += own[pl.ds(2 * tall, tall), :]
        out[pl.ds(k * tall, tall), :] = part
    out[pl.ds(lo * tall, 2 * tall), :] = own[pl.ds(0, 2 * tall), :]


def sums_kernel(cands, *refs):
    *parts, image_out, sums_out = refs
    parts = [*reversed(parts[-2:]), *parts[:-2]]
    lo = len(parts)
    tall, dims = image_out.shape
    sums = [jnp.zeros((tall, dims), jnp.float32)] * 4
    for k in range(lo):
        step = parts[k][pl.ds(lo * tall, tall), :]
        rest = parts[k][pl.ds((lo + 1) * tall, tall), :]
        image = parts[0][pl.ds(k * tall, tall), :]
        for m in range(1, lo):
            image = image + parts[m][pl.ds((k ^ m) * tall, tall), :]
        if k == 0:
            image_out[...] = image
        terms = (rest * rest, step * image, rest * image, image * image)
        sums = [s + t for s, t in zip(sums, terms)]
    for i, s in enumerate(sums):
        sums_out[pl.ds(i * cands, cands), :] = sum(
            s[p : p + cands] for p in range(0, tall, cands)
        )


def update_kernel(*refs):
    *sums, image, solution, residual, direction, out_s, out_r, out_d = refs
    cands = solution.shape[0]
    total = sums[0][...]
    for part in sums[1:]:
        total = total + part[...]
    total = jnp.sum(total, axis=1, keepdims=True)
    norm, curve, cross, square = (
        total[i * cands : (i + 1) * cands] for i in range(4)
    )
    alpha = norm / curve
    norm_next = norm - 2.0 * alpha * cross + alpha * (alpha * square)
    beta = norm_next / norm
    step = direction[...]
    fresh = residual[...] - alpha * unfold(image[...], cands)
    out_s[...] = solution[...] + alpha * step
    out_r[...] = fresh
    out_d[...] = fresh + beta * step


def per_device(devices, points, lengthscale, noise, solution, residual, direction):
    col_masks, row_masks = split_masks(devices)
    hi, lo = len(col_masks), len(row_masks)
    size, dims = points.shape
    cands = direction.shape[0]
    tall = cands * size // dims
    filled = size + lines_of(cands) * size // dims

    def meet(x, mask, odd_mask=None):
        masks = (mask, mask if odd_mask is None else odd_mask)
        return lax.ppermute(x, "blk", [(d, d ^ masks[d % 2]) for d in range(devices)])

    vmem = pl.BlockSpec(memory_space=pltpu.VMEM)
    hbm = pl.BlockSpec(memory_space=pltpu.HBM)
    params = pltpu.CompilerParams(vmem_limit_bytes=50 * 1024 * 1024)

    packed, own, rates, core, middle, far = pl.pallas_call(
        pack_kernel,
        out_shape=(
            jax.ShapeDtypeStruct((filled, dims), jnp.bfloat16),
            jax.ShapeDtypeStruct((3 * tall, dims), jnp.float32),
            jax.ShapeDtypeStruct((8 * cands, dims), jnp.float32),
            jax.ShapeDtypeStruct((filled + 16, dims), jnp.bfloat16),
            jax.ShapeDtypeStruct((filled + 32, dims), jnp.bfloat16),
            jax.ShapeDtypeStruct((filled + 48, dims), jnp.bfloat16),
        ),
        in_specs=[hbm] * 5,
        out_specs=(vmem,) * 6,
        scratch_shapes=[
            pltpu.VMEM((cands, size), jnp.float32),
            pltpu.VMEM((cands, size), jnp.float32),
            pltpu.SMEM((cands,), jnp.float32),
            pltpu.SMEM((cands,), jnp.float32),
            pltpu.SemaphoreType.DMA((5,)),
        ],
        compiler_params=params,
        name="pack",
    )(
        *(
            pltpu.with_memory_space_constraint(x, pltpu.HBM)
            for x in (points, direction, residual, lengthscale, noise)
        )
    )

    rows = [packed, meet(core, 1)]
    for mask in row_masks[2::2]:
        block = meet(points, mask)
        stretched = pl.pallas_call(
            stretch_kernel,
            out_shape=jax.ShapeDtypeStruct(core.shape, core.dtype),
            in_specs=[vmem],
            out_specs=vmem,
            compiler_params=params,
            name="stretch",
        )(block)
        rows += [block, meet(stretched, 1)]

    def column(k):
        wider = far if k > hi // 2 else middle if k == hi // 2 else packed
        return meet(wider, col_masks[k])

    spare = [
        pltpu.VMEM((cands, size, dims), jnp.float32),
        pltpu.VMEM((lo, size, size), jnp.float32),
    ]
    spread = jax.ShapeDtypeStruct((lo * cands * 8, size), jnp.float32)
    total, row_wide = pl.pallas_call(
        functools.partial(first_kernel, lo),
        out_shape=(spread, jax.ShapeDtypeStruct((lo * size, 2 * dims), jnp.bfloat16)),
        in_specs=[vmem] * (lo + 1),
        out_specs=(vmem, vmem),
        scratch_shapes=spare,
        compiler_params=params,
        name="product_0",
    )(packed, *rows[1:], rates)
    order = [hi // 2, *range(hi - 1, hi // 2, -1), *range(hi // 2 - 1, 0, -1)]
    for k in order[:-1]:
        total = pl.pallas_call(
            functools.partial(next_kernel, lo),
            out_shape=spread,
            in_specs=[vmem] * 4,
            out_specs=vmem,
            scratch_shapes=spare,
            compiler_params=params,
            name="product_%d" % k,
        )(column(k), row_wide, rates, total)
    partial = pl.pallas_call(
        functools.partial(last_kernel, lo),
        out_shape=jax.ShapeDtypeStruct(((lo + 2) * tall, dims), jnp.float32),
        in_specs=[vmem] * 5,
        out_specs=vmem,
        scratch_shapes=[*spare, pltpu.VMEM(spread.shape, jnp.float32)],
        compiler_params=params,
        name="product_last",
    )(column(order[-1]), row_wide, rates, total, own)

    image, sums = pl.pallas_call(
        functools.partial(sums_kernel, cands),
        out_shape=(
            jax.ShapeDtypeStruct((tall, dims), jnp.float32),
            jax.ShapeDtypeStruct((4 * cands, dims), jnp.float32),
        ),
        in_specs=[vmem] * lo,
        out_specs=(vmem, vmem),
        compiler_params=params,
        name="sums",
    )(*(meet(partial, mask) for mask in (*row_masks[2:], 1)), partial)

    half = hi // 2
    shared = [
        meet(sums, even, odd)
        for even, odd in zip(col_masks[1:half], reversed(col_masks[half + 1 :]))
    ]
    shared += [meet(x, 1) for x in shared]
    parts = [sums, meet(sums, col_masks[half]), *shared]

    return pl.pallas_call(
        update_kernel,
        out_shape=(jax.ShapeDtypeStruct((cands, size), jnp.float32),) * 3,
        in_specs=[vmem] * (len(parts) + 4),
        out_specs=(vmem,) * 3,
        compiler_params=params,
        name="update",
    )(*parts, image, solution, residual, direction)


def solution(mesh):
    split = P(None, ("groups", "blk"))
    return jax.shard_map(
        functools.partial(per_device, mesh.shape["blk"]),
        mesh=mesh,
        in_specs=(P(("groups", "blk"), None), P("groups"), P("groups"), split, split, split),
        out_specs=(split, split, split),
        check_vma=False,
    )
```

```python
import functools

import jax
import jax.numpy as jnp
from jax import lax
from jax.experimental import pallas as pl
from jax.experimental.pallas import tpu as pltpu
from jax.sharding import PartitionSpec as P

LOG2E = 1.4426950408889634


def split_masks(devices):
    bits = devices.bit_length() - 1
    assert devices == 1 << bits and bits > 1
    far = bits // 2 - 1
    row = [m << (bits - far) for m in range(1 << far)]
    col = [m << 1 for m in range(1 << (bits - 1 - far))]
    return col, [m + core for m in row for core in (0, 1)]


def pieces_of(wide):
    high = wide.astype(jnp.bfloat16).astype(jnp.float32)
    middle = (wide - high).astype(jnp.bfloat16).astype(jnp.float32)
    return [high, middle, wide - high - middle]


def fold(wide, dims):
    return jnp.concatenate(
        [wide[:, p : p + dims] for p in range(0, wide.shape[1], dims)], axis=0
    )


def unfold(tall, n):
    return jnp.concatenate(
        [tall[p : p + n] for p in range(0, tall.shape[0], n)], axis=1
    )


def squares(points):
    wide = points.astype(jnp.float32)
    wide = wide * wide
    high = wide.astype(jnp.bfloat16)
    low = (wide - high.astype(jnp.float32)).astype(jnp.bfloat16)
    ones = jnp.ones((8, points.shape[1]), jnp.bfloat16)
    sums = [
        lax.dot_general(
            ones, half, (((1,), (1,)), ((), ())), preferred_element_type=jnp.float32
        )
        for half in (high, low)
    ]
    return (sums[0] + sums[1])[:1]


def pack_kernel(points, direction, residual, length, noise, packed, own, rates, *refs):
    *wider, step_in, rest_in, length_in, noise_in, sems = refs
    size, dims = points.shape
    cands = direction.shape[0]
    lines = (packed.shape[0] - size) * dims // size
    copies = [
        pltpu.make_async_copy(source, target, sems.at[i])
        for i, (source, target) in enumerate(
            (
                (points, packed.at[pl.ds(0, size), :]),
                (direction, step_in),
                (residual, rest_in),
                (length, length_in),
                (noise, noise_in),
            )
        )
    ]
    for copy in copies:
        copy.start()
    for copy in copies[1:]:
        copy.wait()
    step = step_in[...]
    which = lax.broadcasted_iota(jnp.int32, (cands, 1), 0)
    sigma = jnp.zeros((cands, 1), jnp.float32)
    for c in range(cands):
        sigma = jnp.where(which == c, noise_in[c], sigma)
        rate = (-0.5 * LOG2E) / (length_in[c] * length_in[c])
        rates[pl.ds(8 * c, 8), :] = jnp.full((8, dims), rate, jnp.float32)
    tall = own.shape[0] // 3
    for i, wide in enumerate((step, rest_in[...], sigma * step)):
        own[pl.ds(i * tall, tall), :] = fold(wide, dims)
    copies[0].wait()
    sq = squares(packed[:size, :])
    top = [*pieces_of(sq), step, jnp.zeros((lines - 3 - cands, size), jnp.float32)]
    top = jnp.concatenate([t for t in top if t.shape[0]], axis=0)
    packed[size:, :] = fold(top, dims).astype(jnp.bfloat16)
    filled = packed.shape[0]
    for copy in wider:
        copy[:filled, :] = packed[...]
        spare = copy.shape[0] - filled
        copy[filled:, :] = jnp.zeros((spare, dims), jnp.bfloat16)


def lines_of(cands):
    return -(-(3 + cands) // 8) * 8


def widen_row(points, lines):
    wide = points.astype(jnp.float32)
    sq = pieces_of(jnp.sum(wide * wide, axis=1, keepdims=True))
    lane = lax.broadcasted_iota(jnp.int32, wide.shape, 1)
    extra = jnp.where(lane < 3, 1.0, 0.0)
    for i, piece in enumerate(sq):
        extra = jnp.where(lane == lines + i, piece, extra)
    return jnp.concatenate(
        [(wide * -2.0).astype(jnp.bfloat16), extra.astype(jnp.bfloat16)], axis=1
    )


def add_column(col, row_wide, rates, weights, dist, before, out, lo):
    dims = col.shape[1]
    cands = rates.shape[0] // 8
    size = row_wide.shape[0] // lo
    wide = size // dims
    lines = lines_of(cands)
    top = unfold(col[size : size + lines * wide, :].astype(jnp.float32), lines)
    ones = lax.broadcasted_iota(jnp.int32, (8, size), 0) < 3
    rest = jnp.zeros((dims - lines - 8, size), jnp.float32)
    top = jnp.concatenate([top, ones.astype(jnp.float32), rest], axis=0)
    top = top.astype(jnp.bfloat16).T
    both = jnp.concatenate([col[:size, :], top], axis=1)
    steps = top.astype(jnp.float32)

    def distances(k):
        dist[k] = lax.dot_general(
            both,
            row_wide[pl.ds(k * size, size), :],
            (((1,), (1,)), ((), ())),
            preferred_element_type=jnp.float32,
        )

    distances(0)
    for c in range(cands):
        weights[c] = jnp.broadcast_to(steps[:, 3 + c : 4 + c], (size, dims))
    rate = [
        jnp.concatenate([rates[pl.ds(8 * c, 8), :]] * wide, axis=1) for c in range(cands)
    ]
    for k in range(lo):
        if k + 1 < lo:
            distances(k + 1)
        places = [pl.ds((k * cands + c) * 8, 8) for c in range(cands)]
        total = [0.0 if before is None else before[at, :] for at in places]
        for j in range(0, size, 8):
            here = dist[k, pl.ds(j, 8), :]
            for c in range(cands):
                weight = jnp.concatenate([weights[c, pl.ds(j, 8), :]] * wide, axis=1)
                total[c] = total[c] + jnp.exp2(here * rate[c]) * weight
        for c in range(cands):
            out[places[c], :] = total[c]


def stretch_kernel(block, out):
    size = block.shape[0]
    out[:size, :] = block[...]
    out[size:, :] = jnp.zeros((out.shape[0] - size, out.shape[1]), out.dtype)


def first_kernel(lo, col, *refs):
    rows, refs = refs[: lo - 1], refs[lo - 1 :]
    rates, out, row_wide, weights, dist = refs
    size = row_wide.shape[0] // lo
    for k, block in enumerate((col, *rows)):
        row_wide[pl.ds(k * size, size), :] = widen_row(
            block[:size, :], lines_of(rates.shape[0] // 8)
        )
    add_column(col, row_wide, rates, weights, dist, None, out, lo)


def next_kernel(lo, col, row_wide, rates, before, out, weights, dist):
    add_column(col, row_wide, rates, weights, dist, before, out, lo)


def last_kernel(lo, col, row_wide, rates, before, own, out, weights, dist, spread):
    add_column(col, row_wide, rates, weights, dist, before, spread, lo)
    tall, dims = own.shape[0] // 3, own.shape[1]
    cands = rates.shape[0] // 8
    for k in range(lo):
        part = [
            jnp.sum(spread[pl.ds((k * cands + c) * 8, 8), :], axis=0, keepdims=True)
            for c in range(cands)
        ]
        part = fold(jnp.concatenate(part, axis=0), dims)
        if k == 0:
            part += own[pl.ds(2 * tall, tall), :]
        out[pl.ds(k * tall, tall), :] = part
    out[pl.ds(lo * tall, 2 * tall), :] = own[pl.ds(0, 2 * tall), :]


def sums_kernel(cands, *refs):
    *parts, image_out, sums_out = refs
    parts = parts[::-1]
    lo = len(parts)
    tall, dims = image_out.shape
    sums = [jnp.zeros((tall, dims), jnp.float32)] * 4
    for k in range(lo):
        step = parts[k][pl.ds(lo * tall, tall), :]
        rest = parts[k][pl.ds((lo + 1) * tall, tall), :]
        image = parts[0][pl.ds(k * tall, tall), :]
        for m in range(1, lo):
            image = image + parts[m][pl.ds((k ^ m) * tall, tall), :]
        if k == 0:
            image_out[...] = image
        terms = (rest * rest, step * image, rest * image, image * image)
        sums = [s + t for s, t in zip(sums, terms)]
    for i, s in enumerate(sums):
        sums_out[pl.ds(i * cands, cands), :] = sum(
            s[p : p + cands] for p in range(0, tall, cands)
        )


def update_kernel(*refs):
    *sums, image, solution, residual, direction, out_s, out_r, out_d = refs
    cands = solution.shape[0]
    total = sums[0][...]
    for part in sums[1:]:
        total = total + part[...]
    total = jnp.sum(total, axis=1, keepdims=True)
    norm, curve, cross, square = (
        total[i * cands : (i + 1) * cands] for i in range(4)
    )
    alpha = norm / curve
    norm_next = norm - 2.0 * alpha * cross + alpha * (alpha * square)
    beta = norm_next / norm
    step = direction[...]
    fresh = residual[...] - alpha * unfold(image[...], cands)
    out_s[...] = solution[...] + alpha * step
    out_r[...] = fresh
    out_d[...] = fresh + beta * step


def per_device(devices, points, lengthscale, noise, solution, residual, direction):
    col_masks, row_masks = split_masks(devices)
    hi, lo = len(col_masks), len(row_masks)
    size, dims = points.shape
    cands = direction.shape[0]
    tall = cands * size // dims
    filled = size + lines_of(cands) * size // dims

    def meet(x, mask, odd_mask=None):
        masks = (mask, mask if odd_mask is None else odd_mask)
        return lax.ppermute(x, "blk", [(d, d ^ masks[d % 2]) for d in range(devices)])

    vmem = pl.BlockSpec(memory_space=pltpu.VMEM)
    hbm = pl.BlockSpec(memory_space=pltpu.HBM)
    params = pltpu.CompilerParams(vmem_limit_bytes=50 * 1024 * 1024)

    packed, own, rates, wider, widest = pl.pallas_call(
        pack_kernel,
        out_shape=(
            jax.ShapeDtypeStruct((filled, dims), jnp.bfloat16),
            jax.ShapeDtypeStruct((3 * tall, dims), jnp.float32),
            jax.ShapeDtypeStruct((8 * cands, dims), jnp.float32),
            jax.ShapeDtypeStruct((filled + 16, dims), jnp.bfloat16),
            jax.ShapeDtypeStruct((filled + 32, dims), jnp.bfloat16),
        ),
        in_specs=[hbm] * 5,
        out_specs=(vmem,) * 5,
        scratch_shapes=[
            pltpu.VMEM((cands, size), jnp.float32),
            pltpu.VMEM((cands, size), jnp.float32),
            pltpu.SMEM((cands,), jnp.float32),
            pltpu.SMEM((cands,), jnp.float32),
            pltpu.SemaphoreType.DMA((5,)),
        ],
        compiler_params=params,
        name="pack",
    )(
        *(
            pltpu.with_memory_space_constraint(x, pltpu.HBM)
            for x in (points, direction, residual, lengthscale, noise)
        )
    )

    rows = [packed, meet(wider, 1)]
    for mask in row_masks[2::2]:
        block = meet(points, mask)
        stretched = pl.pallas_call(
            stretch_kernel,
            out_shape=jax.ShapeDtypeStruct(wider.shape, wider.dtype),
            in_specs=[vmem],
            out_specs=vmem,
            compiler_params=params,
            name="stretch",
        )(block)
        rows += [block, meet(stretched, 1)]

    def column(k):
        return meet(packed if k < hi // 2 else widest, col_masks[k])

    spare = [
        pltpu.VMEM((cands, size, dims), jnp.float32),
        pltpu.VMEM((lo, size, size), jnp.float32),
    ]
    spread = jax.ShapeDtypeStruct((lo * cands * 8, size), jnp.float32)
    total, row_wide = pl.pallas_call(
        functools.partial(first_kernel, lo),
        out_shape=(spread, jax.ShapeDtypeStruct((lo * size, 2 * dims), jnp.bfloat16)),
        in_specs=[vmem] * (lo + 1),
        out_specs=(vmem, vmem),
        scratch_shapes=spare,
        compiler_params=params,
        name="product_0",
    )(packed, *rows[1:], rates)
    order = [hi // 2, *range(hi - 1, hi // 2, -1), *range(hi // 2 - 1, 0, -1)]
    for k in order[:-1]:
        total = pl.pallas_call(
            functools.partial(next_kernel, lo),
            out_shape=spread,
            in_specs=[vmem] * 4,
            out_specs=vmem,
            scratch_shapes=spare,
            compiler_params=params,
            name="product_%d" % k,
        )(column(k), row_wide, rates, total)
    partial = pl.pallas_call(
        functools.partial(last_kernel, lo),
        out_shape=jax.ShapeDtypeStruct(((lo + 2) * tall, dims), jnp.float32),
        in_specs=[vmem] * 5,
        out_specs=vmem,
        scratch_shapes=[*spare, pltpu.VMEM(spread.shape, jnp.float32)],
        compiler_params=params,
        name="product_last",
    )(column(order[-1]), row_wide, rates, total, own)

    image, sums = pl.pallas_call(
        functools.partial(sums_kernel, cands),
        out_shape=(
            jax.ShapeDtypeStruct((tall, dims), jnp.float32),
            jax.ShapeDtypeStruct((4 * cands, dims), jnp.float32),
        ),
        in_specs=[vmem] * lo,
        out_specs=(vmem, vmem),
        compiler_params=params,
        name="sums",
    )(*(meet(partial, mask) for mask in reversed(row_masks[1:])), partial)

    half = hi // 2
    shared = [
        meet(sums, even, odd)
        for even, odd in zip(col_masks[1:half], reversed(col_masks[half + 1 :]))
    ]
    shared += [meet(x, 1) for x in shared]
    parts = [sums, meet(sums, col_masks[half]), *shared]

    return pl.pallas_call(
        update_kernel,
        out_shape=(jax.ShapeDtypeStruct((cands, size), jnp.float32),) * 3,
        in_specs=[vmem] * (len(parts) + 4),
        out_specs=(vmem,) * 3,
        compiler_params=params,
        name="update",
    )(*parts, image, solution, residual, direction)


def solution(mesh):
    split = P(None, ("groups", "blk"))
    return jax.shard_map(
        functools.partial(per_device, mesh.shape["blk"]),
        mesh=mesh,
        in_specs=(P(("groups", "blk"), None), P("groups"), P("groups"), split, split, split),
        out_specs=(split, split, split),
        check_vma=False,
    )
```

```python
import functools

import jax
import jax.numpy as jnp
from jax import lax
from jax.experimental import pallas as pl
from jax.experimental.pallas import tpu as pltpu
from jax.sharding import PartitionSpec as P

LOG2E = 1.4426950408889634


def split_masks(devices):
    bits = devices.bit_length() - 1
    assert devices == 1 << bits and bits > 1
    far = bits // 2 - 1
    row = [m << (bits - far) for m in range(1 << far)]
    col = [m << 1 for m in range(1 << (bits - 1 - far))]
    return col, [m + core for m in row for core in (0, 1)]


def pieces_of(wide):
    high = wide.astype(jnp.bfloat16).astype(jnp.float32)
    middle = (wide - high).astype(jnp.bfloat16).astype(jnp.float32)
    return [high, middle, wide - high - middle]


def fold(wide, dims):
    return jnp.concatenate(
        [wide[:, p : p + dims] for p in range(0, wide.shape[1], dims)], axis=0
    )


def unfold(tall, n):
    return jnp.concatenate(
        [tall[p : p + n] for p in range(0, tall.shape[0], n)], axis=1
    )


def squares(points):
    wide = points.astype(jnp.float32)
    wide = wide * wide
    high = wide.astype(jnp.bfloat16)
    low = (wide - high.astype(jnp.float32)).astype(jnp.bfloat16)
    ones = jnp.ones((8, points.shape[1]), jnp.bfloat16)
    sums = [
        lax.dot_general(
            ones, half, (((1,), (1,)), ((), ())), preferred_element_type=jnp.float32
        )
        for half in (high, low)
    ]
    return (sums[0] + sums[1])[:1]


def pack_kernel(points, direction, residual, length, noise, packed, own, rates, *scratch):
    step_in, rest_in, length_in, noise_in, sems = scratch
    size, dims = points.shape
    cands = direction.shape[0]
    lines = (packed.shape[0] - size) * dims // size
    copies = [
        pltpu.make_async_copy(source, target, sems.at[i])
        for i, (source, target) in enumerate(
            (
                (points, packed.at[pl.ds(0, size), :]),
                (direction, step_in),
                (residual, rest_in),
                (length, length_in),
                (noise, noise_in),
            )
        )
    ]
    for copy in copies:
        copy.start()
    for copy in copies[1:]:
        copy.wait()
    step = step_in[...]
    which = lax.broadcasted_iota(jnp.int32, (cands, 1), 0)
    sigma = jnp.zeros((cands, 1), jnp.float32)
    for c in range(cands):
        sigma = jnp.where(which == c, noise_in[c], sigma)
        rate = (-0.5 * LOG2E) / (length_in[c] * length_in[c])
        rates[pl.ds(8 * c, 8), :] = jnp.full((8, dims), rate, jnp.float32)
    tall = own.shape[0] // 3
    for i, wide in enumerate((step, rest_in[...], sigma * step)):
        own[pl.ds(i * tall, tall), :] = fold(wide, dims)
    copies[0].wait()
    sq = squares(packed[:size, :])
    top = [*pieces_of(sq), step, jnp.zeros((lines - 3 - cands, size), jnp.float32)]
    top = jnp.concatenate([t for t in top if t.shape[0]], axis=0)
    packed[size:, :] = fold(top, dims).astype(jnp.bfloat16)


def lines_of(cands):
    return -(-(3 + cands) // 8) * 8


def widen_row(points, lines):
    wide = points.astype(jnp.float32)
    sq = pieces_of(jnp.sum(wide * wide, axis=1, keepdims=True))
    lane = lax.broadcasted_iota(jnp.int32, wide.shape, 1)
    extra = jnp.where(lane < 3, 1.0, 0.0)
    for i, piece in enumerate(sq):
        extra = jnp.where(lane == lines + i, piece, extra)
    return jnp.concatenate(
        [(wide * -2.0).astype(jnp.bfloat16), extra.astype(jnp.bfloat16)], axis=1
    )


def add_column(col, row_wide, rates, weights, dist, before, out, lo):
    dims = col.shape[1]
    cands = rates.shape[0] // 8
    size = row_wide.shape[0] // lo
    wide = size // dims
    lines = lines_of(cands)
    top = unfold(col[size : size + lines * wide, :].astype(jnp.float32), lines)
    ones = lax.broadcasted_iota(jnp.int32, (8, size), 0) < 3
    rest = jnp.zeros((dims - lines - 8, size), jnp.float32)
    top = jnp.concatenate([top, ones.astype(jnp.float32), rest], axis=0)
    top = top.astype(jnp.bfloat16).T
    both = jnp.concatenate([col[:size, :], top], axis=1)
    steps = top.astype(jnp.float32)

    def distances(k):
        dist[k] = lax.dot_general(
            both,
            row_wide[pl.ds(k * size, size), :],
            (((1,), (1,)), ((), ())),
            preferred_element_type=jnp.float32,
        )

    distances(0)
    for c in range(cands):
        weights[c] = jnp.broadcast_to(steps[:, 3 + c : 4 + c], (size, dims))
    rate = [
        jnp.concatenate([rates[pl.ds(8 * c, 8), :]] * wide, axis=1) for c in range(cands)
    ]
    for k in range(lo):
        if k + 1 < lo:
            distances(k + 1)
        places = [pl.ds((k * cands + c) * 8, 8) for c in range(cands)]
        total = [0.0 if before is None else before[at, :] for at in places]
        for j in range(0, size, 8):
            here = dist[k, pl.ds(j, 8), :]
            for c in range(cands):
                weight = jnp.concatenate([weights[c, pl.ds(j, 8), :]] * wide, axis=1)
                total[c] = total[c] + jnp.exp2(here * rate[c]) * weight
        for c in range(cands):
            out[places[c], :] = total[c]


def first_kernel(lo, col, *refs):
    rows, refs = refs[: lo - 1], refs[lo - 1 :]
    rates, out, row_wide, weights, dist = refs
    size = row_wide.shape[0] // lo
    for k, block in enumerate((col, *rows)):
        row_wide[pl.ds(k * size, size), :] = widen_row(
            block[:size, :], lines_of(rates.shape[0] // 8)
        )
    add_column(col, row_wide, rates, weights, dist, None, out, lo)


def next_kernel(lo, col, row_wide, rates, before, out, weights, dist):
    add_column(col, row_wide, rates, weights, dist, before, out, lo)


def last_kernel(lo, col, row_wide, rates, before, own, out, weights, dist, spread):
    add_column(col, row_wide, rates, weights, dist, before, spread, lo)
    tall, dims = own.shape[0] // 3, own.shape[1]
    cands = rates.shape[0] // 8
    for k in range(lo):
        part = [
            jnp.sum(spread[pl.ds((k * cands + c) * 8, 8), :], axis=0, keepdims=True)
            for c in range(cands)
        ]
        part = fold(jnp.concatenate(part, axis=0), dims)
        if k == 0:
            part += own[pl.ds(2 * tall, tall), :]
        out[pl.ds(k * tall, tall), :] = part
    out[pl.ds(lo * tall, 2 * tall), :] = own[pl.ds(0, 2 * tall), :]


def sums_kernel(cands, *refs):
    *parts, image_out, sums_out = refs
    parts = parts[::-1]
    lo = len(parts)
    tall, dims = image_out.shape
    sums = [jnp.zeros((tall, dims), jnp.float32)] * 4
    for k in range(lo):
        step = parts[k][pl.ds(lo * tall, tall), :]
        rest = parts[k][pl.ds((lo + 1) * tall, tall), :]
        image = parts[0][pl.ds(k * tall, tall), :]
        for m in range(1, lo):
            image = image + parts[m][pl.ds((k ^ m) * tall, tall), :]
        if k == 0:
            image_out[...] = image
        terms = (rest * rest, step * image, rest * image, image * image)
        sums = [s + t for s, t in zip(sums, terms)]
    for i, s in enumerate(sums):
        sums_out[pl.ds(i * cands, cands), :] = sum(
            s[p : p + cands] for p in range(0, tall, cands)
        )


def update_kernel(*refs):
    *sums, image, solution, residual, direction, out_s, out_r, out_d = refs
    cands = solution.shape[0]
    total = sums[0][...]
    for part in sums[1:]:
        total = total + part[...]
    total = jnp.sum(total, axis=1, keepdims=True)
    norm, curve, cross, square = (
        total[i * cands : (i + 1) * cands] for i in range(4)
    )
    alpha = norm / curve
    norm_next = norm - 2.0 * alpha * cross + alpha * (alpha * square)
    beta = norm_next / norm
    step = direction[...]
    fresh = residual[...] - alpha * unfold(image[...], cands)
    out_s[...] = solution[...] + alpha * step
    out_r[...] = fresh
    out_d[...] = fresh + beta * step


def per_device(devices, points, lengthscale, noise, solution, residual, direction):
    col_masks, row_masks = split_masks(devices)
    hi, lo = len(col_masks), len(row_masks)
    size, dims = points.shape
    cands = direction.shape[0]
    tall = cands * size // dims
    filled = size + lines_of(cands) * size // dims

    def meet(x, mask, odd_mask=None):
        masks = (mask, mask if odd_mask is None else odd_mask)
        return lax.ppermute(x, "blk", [(d, d ^ masks[d % 2]) for d in range(devices)])

    vmem = pl.BlockSpec(memory_space=pltpu.VMEM)
    hbm = pl.BlockSpec(memory_space=pltpu.HBM)
    params = pltpu.CompilerParams(vmem_limit_bytes=50 * 1024 * 1024)

    packed, own, rates = pl.pallas_call(
        pack_kernel,
        out_shape=(
            jax.ShapeDtypeStruct((filled, dims), jnp.bfloat16),
            jax.ShapeDtypeStruct((3 * tall, dims), jnp.float32),
            jax.ShapeDtypeStruct((8 * cands, dims), jnp.float32),
        ),
        in_specs=[hbm] * 5,
        out_specs=(vmem,) * 3,
        scratch_shapes=[
            pltpu.VMEM((cands, size), jnp.float32),
            pltpu.VMEM((cands, size), jnp.float32),
            pltpu.SMEM((cands,), jnp.float32),
            pltpu.SMEM((cands,), jnp.float32),
            pltpu.SemaphoreType.DMA((5,)),
        ],
        compiler_params=params,
        name="pack",
    )(
        *(
            pltpu.with_memory_space_constraint(x, pltpu.HBM)
            for x in (points, direction, residual, lengthscale, noise)
        )
    )

    rows = [points]
    for mask in row_masks[1:]:
        rows.append(meet(rows[-1], 1) if mask % 2 else meet(points, mask))

    spare = [
        pltpu.VMEM((cands, size, dims), jnp.float32),
        pltpu.VMEM((lo, size, size), jnp.float32),
    ]
    spread = jax.ShapeDtypeStruct((lo * cands * 8, size), jnp.float32)
    total, row_wide = pl.pallas_call(
        functools.partial(first_kernel, lo),
        out_shape=(spread, jax.ShapeDtypeStruct((lo * size, 2 * dims), jnp.bfloat16)),
        in_specs=[vmem] * (lo + 1),
        out_specs=(vmem, vmem),
        scratch_shapes=spare,
        compiler_params=params,
        name="product_0",
    )(packed, *rows[1:], rates)
    order = [hi // 2, *range(hi - 1, hi // 2, -1), *range(hi // 2 - 1, 0, -1)]
    for k in order[:-1]:
        total = pl.pallas_call(
            functools.partial(next_kernel, lo),
            out_shape=spread,
            in_specs=[vmem] * 4,
            out_specs=vmem,
            scratch_shapes=spare,
            compiler_params=params,
            name="product_%d" % k,
        )(meet(packed, col_masks[k]), row_wide, rates, total)
    partial = pl.pallas_call(
        functools.partial(last_kernel, lo),
        out_shape=jax.ShapeDtypeStruct(((lo + 2) * tall, dims), jnp.float32),
        in_specs=[vmem] * 5,
        out_specs=vmem,
        scratch_shapes=[*spare, pltpu.VMEM(spread.shape, jnp.float32)],
        compiler_params=params,
        name="product_last",
    )(meet(packed, col_masks[order[-1]]), row_wide, rates, total, own)

    image, sums = pl.pallas_call(
        functools.partial(sums_kernel, cands),
        out_shape=(
            jax.ShapeDtypeStruct((tall, dims), jnp.float32),
            jax.ShapeDtypeStruct((4 * cands, dims), jnp.float32),
        ),
        in_specs=[vmem] * lo,
        out_specs=(vmem, vmem),
        compiler_params=params,
        name="sums",
    )(*(meet(partial, mask) for mask in reversed(row_masks[1:])), partial)

    half = hi // 2
    shared = [
        meet(sums, even, odd)
        for even, odd in zip(col_masks[1:half], reversed(col_masks[half + 1 :]))
    ]
    shared += [meet(x, 1) for x in shared]
    parts = [sums, meet(sums, col_masks[half]), *shared]

    return pl.pallas_call(
        update_kernel,
        out_shape=(jax.ShapeDtypeStruct((cands, size), jnp.float32),) * 3,
        in_specs=[vmem] * (len(parts) + 4),
        out_specs=(vmem,) * 3,
        compiler_params=params,
        name="update",
    )(*parts, image, solution, residual, direction)


def solution(mesh):
    split = P(None, ("groups", "blk"))
    return jax.shard_map(
        functools.partial(per_device, mesh.shape["blk"]),
        mesh=mesh,
        in_specs=(P(("groups", "blk"), None), P("groups"), P("groups"), split, split, split),
        out_specs=(split, split, split),
        check_vma=False,
    )
```

```python
import functools

import jax
import jax.numpy as jnp
from jax import lax
from jax.experimental import pallas as pl
from jax.experimental.pallas import tpu as pltpu
from jax.sharding import PartitionSpec as P

LOG2E = 1.4426950408889634


def split_masks(devices):
    bits = devices.bit_length() - 1
    assert devices == 1 << bits and bits > 1
    far = bits // 2 - 1
    row = [m << (bits - far) for m in range(1 << far)]
    col = [m << 1 for m in range(1 << (bits - 1 - far))]
    return col, [m + core for m in row for core in (0, 1)]


def pieces_of(wide):
    high = wide.astype(jnp.bfloat16).astype(jnp.float32)
    middle = (wide - high).astype(jnp.bfloat16).astype(jnp.float32)
    return [high, middle, wide - high - middle]


def fold(wide, dims):
    return jnp.concatenate(
        [wide[:, p : p + dims] for p in range(0, wide.shape[1], dims)], axis=0
    )


def unfold(tall, n):
    return jnp.concatenate(
        [tall[p : p + n] for p in range(0, tall.shape[0], n)], axis=1
    )


def squares(points):
    wide = points.astype(jnp.float32)
    wide = wide * wide
    high = wide.astype(jnp.bfloat16)
    low = (wide - high.astype(jnp.float32)).astype(jnp.bfloat16)
    ones = jnp.ones((8, points.shape[1]), jnp.bfloat16)
    sums = [
        lax.dot_general(
            ones, half, (((1,), (1,)), ((), ())), preferred_element_type=jnp.float32
        )
        for half in (high, low)
    ]
    return (sums[0] + sums[1])[:1]


def pack_kernel(points, direction, residual, length, noise, packed, own, rates, *scratch):
    step_in, rest_in, length_in, noise_in, sems = scratch
    size, dims = points.shape
    cands = direction.shape[0]
    lines = (packed.shape[0] - size) * dims // size
    copies = [
        pltpu.make_async_copy(source, target, sems.at[i])
        for i, (source, target) in enumerate(
            (
                (points, packed.at[pl.ds(0, size), :]),
                (direction, step_in),
                (residual, rest_in),
                (length, length_in),
                (noise, noise_in),
            )
        )
    ]
    for copy in copies:
        copy.start()
    for copy in copies[1:]:
        copy.wait()
    step = step_in[...]
    which = lax.broadcasted_iota(jnp.int32, (cands, 1), 0)
    sigma = jnp.zeros((cands, 1), jnp.float32)
    for c in range(cands):
        sigma = jnp.where(which == c, noise_in[c], sigma)
        rate = (-0.5 * LOG2E) / (length_in[c] * length_in[c])
        rates[pl.ds(8 * c, 8), :] = jnp.full((8, dims), rate, jnp.float32)
    tall = own.shape[0] // 3
    for i, wide in enumerate((step, rest_in[...], sigma * step)):
        own[pl.ds(i * tall, tall), :] = fold(wide, dims)
    copies[0].wait()
    sq = squares(packed[:size, :])
    top = [*pieces_of(sq), step, jnp.zeros((lines - 3 - cands, size), jnp.float32)]
    top = jnp.concatenate([t for t in top if t.shape[0]], axis=0)
    packed[size:, :] = fold(top, dims).astype(jnp.bfloat16)


def lines_of(cands):
    return -(-(3 + cands) // 8) * 8


def widen_row(points, lines):
    wide = points.astype(jnp.float32)
    sq = pieces_of(jnp.sum(wide * wide, axis=1, keepdims=True))
    lane = lax.broadcasted_iota(jnp.int32, wide.shape, 1)
    extra = jnp.where(lane < 3, 1.0, 0.0)
    for i, piece in enumerate(sq):
        extra = jnp.where(lane == lines + i, piece, extra)
    return jnp.concatenate(
        [(wide * -2.0).astype(jnp.bfloat16), extra.astype(jnp.bfloat16)], axis=1
    )


def add_column(col, row_wide, rates, weights, dist, before, out, lo, ks=None):
    dims = col.shape[1]
    cands = rates.shape[0] // 8
    size = dist.shape[1]
    wide = size // dims
    ks = list(range(lo)) if ks is None else ks
    lines = lines_of(cands)
    top = unfold(col[size : size + lines * wide, :].astype(jnp.float32), lines)
    ones = lax.broadcasted_iota(jnp.int32, (8, size), 0) < 3
    rest = jnp.zeros((dims - lines - 8, size), jnp.float32)
    top = jnp.concatenate([top, ones.astype(jnp.float32), rest], axis=0)
    top = top.astype(jnp.bfloat16).T
    both = jnp.concatenate([col[:size, :], top], axis=1)
    steps = top.astype(jnp.float32)

    def distances(k):
        dist[k] = lax.dot_general(
            both,
            row_wide[pl.ds(k * size, size), :],
            (((1,), (1,)), ((), ())),
            preferred_element_type=jnp.float32,
        )

    distances(ks[0])
    for c in range(cands):
        weights[c] = jnp.broadcast_to(steps[:, 3 + c : 4 + c], (size, dims))
    rate = [
        jnp.concatenate([rates[pl.ds(8 * c, 8), :]] * wide, axis=1) for c in range(cands)
    ]
    for i, k in enumerate(ks):
        if i + 1 < len(ks):
            distances(ks[i + 1])
        places = [pl.ds((k * cands + c) * 8, 8) for c in range(cands)]
        total = [0.0 if before is None else before[at, :] for at in places]
        for j in range(0, size, 8):
            here = dist[k, pl.ds(j, 8), :]
            for c in range(cands):
                weight = jnp.concatenate([weights[c, pl.ds(j, 8), :]] * wide, axis=1)
                total[c] = total[c] + jnp.exp2(here * rate[c]) * weight
        for c in range(cands):
            out[places[c], :] = total[c]


def first_kernel(lo, col, *refs):
    *rows, rates, out, row_wide, weights, dist = refs
    size = dist.shape[1]
    for i, block in enumerate(rows):
        row_wide[pl.ds(2 * i * size, size), :] = widen_row(
            block[...], lines_of(rates.shape[0] // 8)
        )
    ks = range(0, lo, 2)
    add_column(col, row_wide, rates, weights, dist, None, out, lo, list(ks))


def second_kernel(lo, col, *refs):
    *rows, rates, half, half_wide, out, row_wide, weights, dist = refs
    size = dist.shape[1]
    tall = out.shape[0] // lo
    for i, block in enumerate(rows):
        row_wide[pl.ds((2 * i + 1) * size, size), :] = widen_row(
            block[...], lines_of(rates.shape[0] // 8)
        )
        at = pl.ds(2 * i * size, size)
        row_wide[at, :] = half_wide[at, :]
        at = pl.ds(2 * i * tall, tall)
        out[at, :] = half[at, :]
    ks = range(1, lo, 2)
    add_column(col, row_wide, rates, weights, dist, None, out, lo, list(ks))


def next_kernel(lo, col, row_wide, rates, before, out, weights, dist):
    add_column(col, row_wide, rates, weights, dist, before, out, lo)


def last_kernel(lo, col, row_wide, rates, before, own, out, weights, dist, spread):
    add_column(col, row_wide, rates, weights, dist, before, spread, lo)
    tall, dims = own.shape[0] // 3, own.shape[1]
    cands = rates.shape[0] // 8
    for k in range(lo):
        part = [
            jnp.sum(spread[pl.ds((k * cands + c) * 8, 8), :], axis=0, keepdims=True)
            for c in range(cands)
        ]
        part = fold(jnp.concatenate(part, axis=0), dims)
        if k == 0:
            part += own[pl.ds(2 * tall, tall), :]
        out[pl.ds(k * tall, tall), :] = part
    out[pl.ds(lo * tall, 2 * tall), :] = own[pl.ds(0, 2 * tall), :]


def sums_kernel(cands, *refs):
    *parts, image_out, sums_out = refs
    parts = parts[::-1]
    lo = len(parts)
    tall, dims = image_out.shape
    sums = [jnp.zeros((tall, dims), jnp.float32)] * 4
    for k in range(lo):
        step = parts[k][pl.ds(lo * tall, tall), :]
        rest = parts[k][pl.ds((lo + 1) * tall, tall), :]
        image = parts[0][pl.ds(k * tall, tall), :]
        for m in range(1, lo):
            image = image + parts[m][pl.ds((k ^ m) * tall, tall), :]
        if k == 0:
            image_out[...] = image
        terms = (rest * rest, step * image, rest * image, image * image)
        sums = [s + t for s, t in zip(sums, terms)]
    for i, s in enumerate(sums):
        sums_out[pl.ds(i * cands, cands), :] = sum(
            s[p : p + cands] for p in range(0, tall, cands)
        )


def update_kernel(*refs):
    *sums, image, solution, residual, direction, out_s, out_r, out_d = refs
    cands = solution.shape[0]
    total = sums[0][...]
    for part in sums[1:]:
        total = total + part[...]
    total = jnp.sum(total, axis=1, keepdims=True)
    norm, curve, cross, square = (
        total[i * cands : (i + 1) * cands] for i in range(4)
    )
    alpha = norm / curve
    norm_next = norm - 2.0 * alpha * cross + alpha * (alpha * square)
    beta = norm_next / norm
    step = direction[...]
    fresh = residual[...] - alpha * unfold(image[...], cands)
    out_s[...] = solution[...] + alpha * step
    out_r[...] = fresh
    out_d[...] = fresh + beta * step


def per_device(devices, points, lengthscale, noise, solution, residual, direction):
    col_masks, row_masks = split_masks(devices)
    hi, lo = len(col_masks), len(row_masks)
    size, dims = points.shape
    cands = direction.shape[0]
    tall = cands * size // dims
    filled = size + lines_of(cands) * size // dims

    def meet(x, mask, odd_mask=None):
        masks = (mask, mask if odd_mask is None else odd_mask)
        return lax.ppermute(x, "blk", [(d, d ^ masks[d % 2]) for d in range(devices)])

    vmem = pl.BlockSpec(memory_space=pltpu.VMEM)
    hbm = pl.BlockSpec(memory_space=pltpu.HBM)
    params = pltpu.CompilerParams(vmem_limit_bytes=50 * 1024 * 1024)

    packed, own, rates = pl.pallas_call(
        pack_kernel,
        out_shape=(
            jax.ShapeDtypeStruct((filled, dims), jnp.bfloat16),
            jax.ShapeDtypeStruct((3 * tall, dims), jnp.float32),
            jax.ShapeDtypeStruct((8 * cands, dims), jnp.float32),
        ),
        in_specs=[hbm] * 5,
        out_specs=(vmem,) * 3,
        scratch_shapes=[
            pltpu.VMEM((cands, size), jnp.float32),
            pltpu.VMEM((cands, size), jnp.float32),
            pltpu.SMEM((cands,), jnp.float32),
            pltpu.SMEM((cands,), jnp.float32),
            pltpu.SemaphoreType.DMA((5,)),
        ],
        compiler_params=params,
        name="pack",
    )(
        *(
            pltpu.with_memory_space_constraint(x, pltpu.HBM)
            for x in (points, direction, residual, lengthscale, noise)
        )
    )

    rows = [points]
    for mask in row_masks[1:]:
        rows.append(meet(rows[-1], 1) if mask % 2 else meet(points, mask))

    spare = [
        pltpu.VMEM((cands, size, dims), jnp.float32),
        pltpu.VMEM((lo, size, size), jnp.float32),
    ]
    spread = jax.ShapeDtypeStruct((lo * cands * 8, size), jnp.float32)
    wide_shape = jax.ShapeDtypeStruct((lo * size, 2 * dims), jnp.bfloat16)
    half, half_wide = pl.pallas_call(
        functools.partial(first_kernel, lo),
        out_shape=(spread, wide_shape),
        in_specs=[vmem] * (lo // 2 + 2),
        out_specs=(vmem, vmem),
        scratch_shapes=spare,
        compiler_params=params,
        name="product_own",
    )(packed, *rows[::2], rates)
    total, row_wide = pl.pallas_call(
        functools.partial(second_kernel, lo),
        out_shape=(spread, wide_shape),
        in_specs=[vmem] * (lo // 2 + 4),
        out_specs=(vmem, vmem),
        scratch_shapes=spare,
        compiler_params=params,
        name="product_core",
    )(packed, *rows[1::2], rates, half, half_wide)
    order = [hi // 2, *range(hi - 1, hi // 2, -1), *range(hi // 2 - 1, 0, -1)]
    for k in order[:-1]:
        total = pl.pallas_call(
            functools.partial(next_kernel, lo),
            out_shape=spread,
            in_specs=[vmem] * 4,
            out_specs=vmem,
            scratch_shapes=spare,
            compiler_params=params,
            name="product_%d" % k,
        )(meet(packed, col_masks[k]), row_wide, rates, total)
    partial = pl.pallas_call(
        functools.partial(last_kernel, lo),
        out_shape=jax.ShapeDtypeStruct(((lo + 2) * tall, dims), jnp.float32),
        in_specs=[vmem] * 5,
        out_specs=vmem,
        scratch_shapes=[*spare, pltpu.VMEM(spread.shape, jnp.float32)],
        compiler_params=params,
        name="product_last",
    )(meet(packed, col_masks[order[-1]]), row_wide, rates, total, own)

    image, sums = pl.pallas_call(
        functools.partial(sums_kernel, cands),
        out_shape=(
            jax.ShapeDtypeStruct((tall, dims), jnp.float32),
            jax.ShapeDtypeStruct((4 * cands, dims), jnp.float32),
        ),
        in_specs=[vmem] * lo,
        out_specs=(vmem, vmem),
        compiler_params=params,
        name="sums",
    )(*(meet(partial, mask) for mask in reversed(row_masks[1:])), partial)

    half = hi // 2
    shared = [
        meet(sums, even, odd)
        for even, odd in zip(col_masks[1:half], reversed(col_masks[half + 1 :]))
    ]
    shared += [meet(x, 1) for x in shared]
    parts = [sums, meet(sums, col_masks[half]), *shared]

    return pl.pallas_call(
        update_kernel,
        out_shape=(jax.ShapeDtypeStruct((cands, size), jnp.float32),) * 3,
        in_specs=[vmem] * (len(parts) + 4),
        out_specs=(vmem,) * 3,
        compiler_params=params,
        name="update",
    )(*parts, image, solution, residual, direction)


def solution(mesh):
    split = P(None, ("groups", "blk"))
    return jax.shard_map(
        functools.partial(per_device, mesh.shape["blk"]),
        mesh=mesh,
        in_specs=(P(("groups", "blk"), None), P("groups"), P("groups"), split, split, split),
        out_specs=(split, split, split),
        check_vma=False,
    )
```
